32 devices in a mesh: grp: 2 (over y), pulse: 16 (over z, x, core), rng: 1.
Axes of the slice: x: 2, y: 2, z: 4, core: 2. Of those that a mesh axis runs over, the one named last changes fastest.
Arguments:
- raw_echoes: bfloat16 [256, 64, 2, 128], P(('grp', 'pulse'), 'rng'), parts along dimension 0, may hold values from -6 to 6
- matched: float32 [2, 128], replicated, may hold values from -0.375 to 0.375
- delays: int32 [256, 16], P(('grp', 'pulse')), parts along dimension 0, may hold values from -24 to 24
- pulse_phase: float32 [256, 16], P(('grp', 'pulse')), parts along dimension 0, may hold values from -3.140625 to 3.140625
- beam_map: int32 [4, 2, 2, 16], replicated, may hold values from 0 to 15, as said below
- range_shift: int32 [4, 2, 2, 16], replicated, may hold values from -24 to 24
- phase_base: float32 [4, 2, 2, 16], replicated, may hold values from -3.140625 to 3.140625
- phase_rate: float32 [4, 2, 2, 16], replicated, may hold values from -4 to 4
- tap_offsets: int32 [4, 4], replicated, may hold values from -4 to 4, as said below
Outputs:
- final_image: float32 [2, 512, 8192], P(None, ('grp', 'pulse'), 'rng'), parts along dimension 1
The draws below stay inside these ranges and needn't reach their ends.
There are 2 independent parts, one for each index of `grp`. The reference program is written for one: setup_inputs(seed, part) draws one part's arguments, and reference() takes and returns one part's arrays. A program takes and returns all parts, laid end to end along the dimension named above; an argument that names none is the same for every part. Nothing has to cross between parts.
Inputs may be any that keep to these rules, and one draw needn't show every extreme that they name: `beam_map`: entry [l, h, s, k] is h * 8 + k // 2 plus -1, 0 or 1, clamped to the range. `tap_offsets`: the 4 entries of one level are distinct.
All inputs are finite; a program needn't handle non-finite values.
Results may differ from the reference program's by a relative error of at most 0.0055.
Values may be sent and summed in bfloat16 or wider, within the bound.
No kernel may reach another device: no remote copies, remote signals or barrier semaphores. Data moves between devices by JAX's collectives and lax.ppermute only.
A program may use at most 64 MiB of HBM per device.

```python
import math
import jax
import jax.numpy as jnp
from jax import lax

R = 8192
BLOCK = 256
BEAMS = 16
LEVELS = 4
TAPS = 4
SHIFT = 24
SPREAD = 4
PUL_DEV = 8
HOP = 128
PULSES = 128
N_PULSE = 16


def draw_beam_map(key, part):
    jitter = jax.random.randint(key, (LEVELS, 2, 2, BEAMS), -1, 2)
    half_index = jnp.arange(2, dtype=jnp.int32)[None, :, None, None]
    position = jnp.arange(BEAMS, dtype=jnp.int32)[None, None, None, :]
    return jnp.clip(half_index * (BEAMS // 2) + position // 2 + jitter, 0, BEAMS - 1).astype(jnp.int32)


def draw_tap_offsets(key, part):
    rows_list = []
    for level_index in range(LEVELS):
        shuffled = jax.random.permutation(jax.random.fold_in(key, level_index + 17), 2 * SPREAD + 1)
        rows_list.append(shuffled[:TAPS])
    return (jnp.stack(rows_list) - SPREAD).astype(jnp.int32)


def touch_ends(values, key, smallest, top_value):
    index_at = [jax.random.randint(jax.random.fold_in(key, axis), (), 0, length) for axis, length in enumerate(values.shape)]
    main_axis = values.shape.index(max(values.shape))
    beside = index_at[:main_axis] + [(index_at[main_axis] + 1) % values.shape[main_axis]] + index_at[main_axis + 1:]
    return values.at[tuple(index_at)].set(smallest).at[tuple(beside)].set(top_value)


def block_scale(own_key, dims, cuts, least, largest):
    def one(dim, blocks):
        draws = jax.random.uniform(jax.random.fold_in(jax.random.fold_in(own_key, 6), dim), (blocks,), jnp.float32, least / len(cuts), largest / len(cuts))
        return jnp.repeat(jnp.exp(draws), dims[dim] // blocks).reshape((-1,) + (1,) * (len(dims) - dim - 1))

    gain = one(*cuts[0])
    for cut in cuts[1:]:
        gain = gain * one(*cut)
    return gain


def centred(own_key, dims, scale, most, split=(), kind=jnp.bfloat16):
    drawn = jax.random.normal(own_key, dims, jnp.float32) * scale
    if len(split) > 0:
        drawn = block_scale(own_key, dims, split, -0.22, 0.18) * drawn
    return jnp.clip(drawn, min=-most, max=most).astype(kind)


def setup_inputs(seed: int = 0, part: int = 0) -> dict:
    key_list = jax.random.split(jax.random.key(seed), 10)
    part_splits = jax.random.split(jax.random.fold_in(key_list[9], part), 10)
    return {
        "raw_echoes": centred(part_splits[0], (PULSES, R // HOP, 2, HOP), 1.0, 6.0, ((0, 16),)),
        "matched": centred(key_list[1], (2, HOP), (2 * HOP) ** -0.5, 0.375, (), jnp.float32),
        "delays": touch_ends(jax.random.randint(part_splits[2], (PULSES, BEAMS), -SHIFT, SHIFT + 1), jax.random.fold_in(part_splits[2], 1), -SHIFT, SHIFT).astype(jnp.int32),
        "pulse_phase": jnp.clip(jax.random.uniform(part_splits[3], (PULSES, BEAMS), jnp.float32, -3.140625, 3.140625), -3.140625, 3.140625),
        "beam_map": draw_beam_map(jax.random.fold_in(key_list[9], 71), part),
        "range_shift": touch_ends(jax.random.randint(key_list[5], (LEVELS, 2, 2, BEAMS), -SHIFT, SHIFT + 1), jax.random.fold_in(key_list[5], 1), -SHIFT, SHIFT).astype(jnp.int32),
        "phase_base": jnp.clip(jax.random.uniform(key_list[6], (LEVELS, 2, 2, BEAMS), jnp.float32, -3.140625, 3.140625), -3.140625, 3.140625),
        "phase_rate": jnp.clip(jax.random.uniform(key_list[7], (LEVELS, 2, 2, BEAMS), jnp.float32, -4.0, 4.0), -4.0, 4.0),
        "tap_offsets": draw_tap_offsets(jax.random.fold_in(key_list[9], 71), part),
    }


SQRT_HALF = 0.7071067811865476

def tables(length):
    counter = jnp.arange(length, dtype=jnp.int32)
    product = counter[:, None] * counter[None, :] % length
    angles = product.astype(jnp.float32) * (2.0 * math.pi / length)
    cosine = jnp.cos(angles)
    sine_part = jnp.sin(angles)
    forward = jnp.concatenate([jnp.concatenate([cosine, -sine_part], axis=1), jnp.concatenate([sine_part, cosine], axis=1)], axis=0)
    inverse = jnp.concatenate([jnp.concatenate([cosine, sine_part], axis=1), jnp.concatenate([-sine_part, cosine], axis=1)], axis=0)
    return (forward, inverse)

def compress(echoes, tail, matched, forward_exact, forward, inverse_kept):
    pulses, blocks, parts, hop_bins = echoes.shape
    length = 2 * hop_bins
    previous = jnp.concatenate([tail[:, None], echoes[:, :-1]], axis=1)
    windows = jnp.concatenate([previous, echoes], axis=3).reshape(pulses * blocks, parts * length)
    taps_padded = jnp.concatenate([matched, jnp.zeros((2, length - hop_bins), jnp.float32)], axis=1).reshape(1, 2 * length)
    response = jnp.dot(taps_padded, forward_exact, precision=lax.Precision.HIGHEST)[0]
    resp_real = response[:length]
    resp_imag = response[length:]
    spectrum = jnp.dot(windows, forward, preferred_element_type=jnp.float32)
    spec_real = spectrum[:, :length]
    spec_imag = spectrum[:, length:]
    filt_real = spec_real * resp_real - spec_imag * resp_imag
    filt_imag = spec_real * resp_imag + spec_imag * resp_real
    shaped = jnp.concatenate([filt_real, filt_imag], axis=1).astype(jnp.bfloat16)
    restored = jnp.dot(shaped, inverse_kept, preferred_element_type=jnp.float32) * (1.0 / length)
    return restored.astype(jnp.bfloat16).reshape(pulses, blocks, parts, hop_bins)

def kept_columns(inverse, length):
    half = length // 2
    return jnp.concatenate([inverse[:, half:length], inverse[:, length + half:]], axis=1)

def inside_mask(first_cell, out_cells):
    global_cells = first_cell + jnp.arange(out_cells, dtype=jnp.int32)
    return ((global_cells >= 0) & (global_cells < R)).astype(jnp.float32)

def row_slices(rows, starts, width):

    def per_pulse(row, start_row):
        return jax.vmap(lambda start: lax.dynamic_slice_in_dim(row, start, width, 1))(start_row)
    return jax.vmap(per_pulse)(rows, starts)

def project(padded, delay_rows, phase_rows, offset_base, out_cells, first_cell):
    pulses = padded.shape[0]
    beam_count = delay_rows.shape[1]
    group_size = math.gcd(pulses, 4)
    block_count = pulses // group_size

    def accumulate(summed, block_index):
        first_row = block_index * group_size
        pulses_block = lax.dynamic_slice_in_dim(padded, first_row, group_size, 0)
        delay_block = lax.dynamic_slice_in_dim(delay_rows, first_row, group_size, 0)
        phase_block = lax.dynamic_slice_in_dim(phase_rows, first_row, group_size, 0)
        starts = (delay_block + offset_base).astype(jnp.int32)
        gathered = row_slices(pulses_block, starts, out_cells).astype(jnp.float32)
        cosine = jnp.cos(phase_block)[:, :, None]
        sine_part = jnp.sin(phase_block)[:, :, None]
        real_part = gathered[:, :, 0] * cosine - gathered[:, :, 1] * sine_part
        imag_part = gathered[:, :, 0] * sine_part + gathered[:, :, 1] * cosine
        return (summed + jnp.stack([lax.optimization_barrier(jnp.sum(real_part, axis=0)), lax.optimization_barrier(jnp.sum(imag_part, axis=0))]), None)
    summed, unused = lax.scan(accumulate, jnp.zeros((2, beam_count, out_cells), jnp.float32), jnp.arange(block_count, dtype=jnp.int32))
    return summed * inside_mask(first_cell, out_cells) * (1.0 / math.sqrt(pulses))

def tap_weights(tap_values):
    weights = SPREAD + 1.0 - jnp.abs(tap_values).astype(jnp.float32)
    return weights / jnp.sum(weights)

def merge_side(source, beam_rows, offsets, phase_zero, phase_slope, weights, tap_values, offset_base, out_cells, first_cell):
    picked = jnp.take(source, beam_rows, axis=1)
    span = out_cells + 2 * SPREAD
    starts = (offsets + offset_base - SPREAD).astype(jnp.int32)
    windows = jax.vmap(lambda beam_data, start: lax.dynamic_slice_in_dim(beam_data, start, span, 1), in_axes=(1, 0), out_axes=1)(picked, starts)
    summed = jnp.zeros((2, beam_rows.shape[0], out_cells), jnp.float32)
    for tap_index in range(tap_values.shape[0]):
        tap_start = (tap_values[tap_index] + SPREAD).astype(jnp.int32)
        summed = summed + weights[tap_index] * lax.dynamic_slice_in_dim(windows, tap_start, out_cells, 2)
    positions = jnp.arange(out_cells, dtype=jnp.int32)
    global_cells = (first_cell + positions).astype(jnp.float32)
    angle_grid = phase_zero[:, None] + 2.0 * math.pi / R * phase_slope[:, None] * global_cells[None, :]
    cosine = jnp.cos(angle_grid)
    sine_part = jnp.sin(angle_grid)
    return jnp.stack([summed[0] * cosine - summed[1] * sine_part, summed[0] * sine_part + summed[1] * cosine])

def reference(raw_echoes, matched, delays, pulse_phase, beam_map, range_shift, phase_base, phase_rate, tap_offsets):
    forward_exact, inverse_exact = tables(BLOCK)
    forward = forward_exact.astype(jnp.bfloat16)
    inverse_kept = kept_columns(inverse_exact.astype(jnp.bfloat16), BLOCK)

    def initial(device):
        first_row = device * PUL_DEV
        echoes = lax.dynamic_slice_in_dim(raw_echoes, first_row, PUL_DEV, 0)
        delay_rows = lax.dynamic_slice_in_dim(delays, first_row, PUL_DEV, 0)
        phase_rows = lax.dynamic_slice_in_dim(pulse_phase, first_row, PUL_DEV, 0)
        tail = jnp.zeros((PUL_DEV, 2, HOP), jnp.bfloat16)
        compressed = compress(echoes, tail, matched, forward_exact, forward, inverse_kept)
        compressed = jnp.transpose(compressed, (0, 2, 1, 3)).reshape(PUL_DEV, 2, R)
        padded = jnp.pad(compressed, ((0, 0), (0, 0), (SHIFT, SHIFT)))
        return project(padded, delay_rows, phase_rows, SHIFT, R, 0)
    images = lax.map(initial, jnp.arange(N_PULSE, dtype=jnp.int32))
    rim_cells = SHIFT + SPREAD
    for level_index in range(LEVELS):
        stride = 2 ** level_index
        grouped = images.reshape(N_PULSE // (2 * stride), 2, stride, 2, BEAMS, R)
        widths = ((0, 0), (0, 0), (0, 0), (rim_cells, rim_cells))
        lower_half = jnp.pad(grouped[:, 0].reshape(-1, 2, BEAMS, R), widths)
        upper_half = jnp.pad(grouped[:, 1].reshape(-1, 2, BEAMS, R), widths)
        tap_values = tap_offsets[level_index]
        weights = tap_weights(tap_values)
        halves = []
        for side_bit in range(2):

            def merge_pair(pair_data):
                lower_source, upper_source = pair_data
                first_side = merge_side(lower_source, beam_map[level_index, side_bit, 0], range_shift[level_index, side_bit, 0], phase_base[level_index, side_bit, 0], phase_rate[level_index, side_bit, 0], weights, tap_values, rim_cells, R, 0)
                second_side = merge_side(upper_source, beam_map[level_index, side_bit, 1], range_shift[level_index, side_bit, 1], phase_base[level_index, side_bit, 1], phase_rate[level_index, side_bit, 1], weights, tap_values, rim_cells, R, 0)
                return (first_side + second_side) * SQRT_HALF
            merged = lax.map(merge_pair, (lower_half, upper_half))
            halves.append(merged.reshape(N_PULSE // (2 * stride), stride, 2, BEAMS, R))
        images = jnp.stack(halves, axis=1).reshape(N_PULSE, 2, BEAMS, R)
    return jnp.transpose(images, (1, 0, 2, 3)).reshape(2, N_PULSE * BEAMS, R)
```

```python
import functools
import math

import jax
import jax.numpy as jnp
import numpy as np
from jax import lax
from jax.experimental import pallas as pl
from jax.experimental.pallas import tpu as pltpu
from jax.sharding import PartitionSpec as P

SPREAD = 4
SHIFT = 24
HALO = 32
LANES = 128
HALF = 64
SQRT_HALF = 0.7071067811865476
VMEM_LIMIT = 24 * 2**20

COS_COEFFS = (
    1.0,
    -19.73920440673828,
    64.93911743164062,
    -85.45014190673828,
    60.16762924194336,
    -25.967599868774414,
    6.528658390045166,
)
SIN_COEFFS = (
    6.2831854820251465,
    -41.34170150756836,
    81.60513305664062,
    -76.70301818847656,
    42.02592849731445,
    -14.899847030639648,
    3.2381374835968018,
)

SMEM_SPEC = pl.BlockSpec(memory_space=pltpu.SMEM)
VMEM_SPEC = pl.BlockSpec(memory_space=pltpu.VMEM)


def cos_sin_turns(turns):
    f = turns - jnp.round(turns)
    u = f * f
    c = jnp.full_like(u, COS_COEFFS[-1])
    for a in COS_COEFFS[-2::-1]:
        c = c * u + a
    s = jnp.full_like(u, SIN_COEFFS[-1])
    for a in SIN_COEFFS[-2::-1]:
        s = s * u + a
    return c, s * f


def lane_iota(rows):
    return lax.broadcasted_iota(jnp.int32, (rows, LANES), 1)


def store_extended(ext_ref, where, low, high, body):
    lane = lane_iota(HALO)
    ext_ref[(*where, pl.ds(HALO, HALF))] = body
    after = jnp.where(lane < HALF, pltpu.roll(high, HALF, 1), pltpu.roll(high, HALF - 1, 1))
    ext_ref[(*where, pl.ds(HALO + HALF, HALO))] = jnp.where(lane == LANES - 1, 0.0, after)
    before = jnp.where(lane < HALF, pltpu.roll(low, HALF + 1, 1), pltpu.roll(low, HALF, 1))
    ext_ref[(*where, pl.ds(0, HALO))] = jnp.where(lane == 0, 0.0, before)


def front_kernel(
    index_ref, raw_ref, matched_ref, delays_ref, phase_ref, image_ref, send_ref,
    raw32, taps, windows, ext, trig, trig_smem, sem,
):
    pulses, beams = phase_ref.shape
    rows = raw_ref.shape[0] // 2
    blocks = rows // pulses
    side_bit = index_ref[0] % 2
    scale = 1.0 / math.sqrt(pulses)
    c, s = cos_sin_turns(phase_ref[...] * (0.5 / math.pi))
    trig[0] = c * scale
    trig[1] = s * scale
    copy = pltpu.make_async_copy(trig, trig_smem, sem)
    copy.start()
    raw32[0:16] = jnp.zeros((16, LANES), jnp.float32)
    raw32[16 : 16 + 2 * rows] = raw_ref[...].astype(jnp.float32)
    first = lax.broadcasted_iota(jnp.int32, (rows, LANES), 0) % blocks == 0
    for part in range(2):
        previous = raw32[pl.ds(14 + part, rows, stride=2), :]
        windows[:, part * LANES : (part + 1) * LANES] = jnp.where(first, 0.0, previous).astype(jnp.bfloat16)
        current = raw32[pl.ds(16 + part, rows, stride=2), :]
        windows[:, (2 + part) * LANES : (3 + part) * LANES] = current.astype(jnp.bfloat16)
    row = lax.broadcasted_iota(jnp.int32, (LANES, LANES), 0)
    column = lax.broadcasted_iota(jnp.int32, (LANES, LANES), 1)
    for part in range(2):
        line = jnp.broadcast_to(matched_ref[part : part + 1, :], (LANES, LANES))
        circulant = pltpu.roll(line, 0, 1, stride=1, stride_axis=0).T
        now = jnp.where(column <= row, circulant, 0.0).astype(jnp.bfloat16)
        before = jnp.where(column > row, circulant, 0.0).astype(jnp.bfloat16)
        if part == 0:
            taps[0:LANES, 0:LANES] = before
            taps[LANES:, LANES : 2 * LANES] = before
            taps[0:LANES, 2 * LANES : 3 * LANES] = now
            taps[LANES:, 3 * LANES :] = now
        else:
            taps[0:LANES, LANES : 2 * LANES] = -before
            taps[LANES:, 0:LANES] = before
            taps[0:LANES, 3 * LANES :] = -now
            taps[LANES:, 2 * LANES : 3 * LANES] = now
    lane = lane_iota(HALF)
    for pair in range(rows // LANES):
        made = lax.dot_general(
            taps[...],
            windows[pair * LANES : (pair + 1) * LANES, :],
            (((1,), (1,)), ((), ())),
            preferred_element_type=jnp.float32,
        )
        for part in range(2):
            a = made[part * LANES : part * LANES + HALF]
            b = made[part * LANES + HALF : (part + 1) * LANES]
            even = jnp.where(lane < HALF, a, pltpu.roll(b, HALF, 1))
            odd = jnp.where(lane < HALF, pltpu.roll(a, HALF, 1), b)
            for which, body in ((0, even), (1, odd)):
                store_extended(ext, (2 * pair + which, part), body[HALF - HALO :], body[:HALO], body)
    copy.wait()
    send_first = (1 - side_bit) * 7

    def beam(k, carry):
        for piece in range(HALF // 32):
            real = jnp.zeros((32, LANES), jnp.float32)
            imag = jnp.zeros((32, LANES), jnp.float32)
            for p in range(pulses):
                start = delays_ref[p, k] + (HALO + piece * 32)
                x = ext[p, 0, pl.ds(start, 32), :]
                y = ext[p, 1, pl.ds(start, 32), :]
                cosine = trig_smem[0, p, k]
                sine = trig_smem[1, p, k]
                real = real + (x * cosine - y * sine)
                imag = imag + (x * sine + y * cosine)
            image_ref[k, 0, pl.ds(piece * 32, 32)] = real
            image_ref[k, 1, pl.ds(piece * 32, 32)] = imag
            slot = k - send_first

            @pl.when((slot >= 0) & (slot < send_ref.shape[0]))
            def _():
                send_ref[slot, 0, pl.ds(piece * 32, 32)] = real.astype(jnp.bfloat16)
                send_ref[slot, 1, pl.ds(piece * 32, 32)] = imag.astype(jnp.bfloat16)

        return carry

    lax.fori_loop(0, beams, beam, 0)


def tap_factors(taps_ref, level):
    count = taps_ref.shape[1]
    offsets = [taps_ref[level, t] for t in range(count)]
    weights = [(SPREAD + 1.0) - jnp.abs(o).astype(jnp.float32) for o in offsets]
    return offsets, weights


def filtered(ext, slot, part, start, offsets, weights):
    total = None
    for offset, weight in zip(offsets, weights):
        term = ext[slot, part, pl.ds(start + offset, HALF), :] * weight
        total = term if total is None else total + term
    return total


def cells():
    t = lax.broadcasted_iota(jnp.int32, (HALF, LANES), 0)
    lane = lane_iota(HALF)
    return (t + (lane % HALF) * LANES + (lane // HALF) * HALF).astype(jnp.float32)


def own_kernel(
    level, bins, index_ref, beam_ref, shift_ref, base_ref, rate_ref, taps_ref, image_ref, partial_ref, turn_ref, ext,
):
    side_bit = (index_ref[0] >> level) % 2
    beams = image_ref.shape[0]
    low_beam = side_bit * 7

    def extend(slot, carry):
        for part in range(2):
            body = image_ref[low_beam + slot, part]
            store_extended(ext, (slot, part), body[HALF - HALO :], body[:HALO], body)
        return carry

    lax.fori_loop(0, ext.shape[0], extend, 0)
    offsets, weights = tap_factors(taps_ref, level)
    position = cells() * (1.0 / bins)

    def beam(k, carry):
        own = (level, side_bit, side_bit, k)
        other = (level, side_bit, 1 - side_bit, k)
        slot = beam_ref[own] - low_beam
        start = shift_ref[own] + HALO
        real = filtered(ext, slot, 0, start, offsets, weights)
        imag = filtered(ext, slot, 1, start, offsets, weights)
        c, s = cos_sin_turns(position * rate_ref[own] + base_ref[own] * (0.5 / math.pi))
        partial_ref[k, 0] = real * c - imag * s
        partial_ref[k, 1] = real * s + imag * c
        c, s = cos_sin_turns(position * rate_ref[other] + base_ref[other] * (0.5 / math.pi))
        turn_ref[k, 0] = c
        turn_ref[k, 1] = s
        return carry

    lax.fori_loop(0, beams, beam, 0)


def merged(level, side_bit, k, scale, beam_ref, shift_ref, offsets, weights, ext, partial_ref, turn_ref):
    other = (level, side_bit, 1 - side_bit, k)
    slot = beam_ref[other] - side_bit * 7
    start = shift_ref[other] + HALO
    real = filtered(ext, slot, 0, start, offsets, weights)
    imag = filtered(ext, slot, 1, start, offsets, weights)
    c = turn_ref[k, 0]
    s = turn_ref[k, 1]
    return (
        (real * c - imag * s + partial_ref[k, 0]) * scale,
        (real * s + imag * c + partial_ref[k, 1]) * scale,
    )


def extend_received(received_ref, ext):
    def extend(slot, carry):
        for part in range(2):
            body = received_ref[slot, part].astype(jnp.float32)
            store_extended(ext, (slot, part), body[HALF - HALO :], body[:HALO], body)
        return carry

    lax.fori_loop(0, ext.shape[0], extend, 0)


def total_scale(weights):
    total = weights[0]
    for w in weights[1:]:
        total = total + w
    return SQRT_HALF / total


def middle_kernel(
    level, index_ref, beam_ref, shift_ref, taps_ref, received_ref, partial_ref, turn_ref, image_ref, send_ref, ext,
):
    side_bit = (index_ref[0] >> level) % 2
    next_bit = (index_ref[0] >> (level + 1)) % 2
    send_first = (1 - next_bit) * 7
    extend_received(received_ref, ext)
    offsets, weights = tap_factors(taps_ref, level)
    scale = total_scale(weights)

    def beam(k, carry):
        real, imag = merged(
            level, side_bit, k, scale, beam_ref, shift_ref, offsets, weights, ext, partial_ref, turn_ref
        )
        image_ref[k, 0] = real
        image_ref[k, 1] = imag
        slot = k - send_first

        @pl.when((slot >= 0) & (slot < send_ref.shape[0]))
        def _():
            send_ref[slot, 0] = real.astype(jnp.bfloat16)
            send_ref[slot, 1] = imag.astype(jnp.bfloat16)

        return carry

    lax.fori_loop(0, image_ref.shape[0], beam, 0)


def last_kernel(
    level, index_ref, beam_ref, shift_ref, taps_ref, received_ref, partial_ref, turn_ref, out_ref, ext,
):
    side_bit = (index_ref[0] >> level) % 2
    extend_received(received_ref, ext)
    offsets, weights = tap_factors(taps_ref, level)
    scale = total_scale(weights)
    lane = lane_iota(HALF)

    def pair(m, carry):
        even = merged(
            level, side_bit, 2 * m, scale, beam_ref, shift_ref, offsets, weights, ext, partial_ref, turn_ref
        )
        odd = merged(
            level, side_bit, 2 * m + 1, scale, beam_ref, shift_ref, offsets, weights, ext, partial_ref, turn_ref
        )
        high, low = m // 4, 2 * (m % 4)
        for part in range(2):
            turned = jnp.concatenate([even[part], odd[part]], axis=0).T
            a = turned[:HALF]
            b = turned[HALF:]
            out_ref[part, high, pl.ds(low, HALF, stride=8), :] = jnp.where(lane < HALF, a, pltpu.roll(b, HALF, 1))
            out_ref[part, high, pl.ds(low + 1, HALF, stride=8), :] = jnp.where(lane < HALF, pltpu.roll(a, HALF, 1), b)
        return carry

    lax.fori_loop(0, partial_ref.shape[0] // 2, pair, 0)


def params():
    return pltpu.CompilerParams(vmem_limit_bytes=VMEM_LIMIT)


def route(axis, bit):
    count = lax.axis_size(axis)
    return [(i, i ^ (1 << bit)) for i in range(count) if i ^ (1 << bit) < count]


def local(raw_echoes, matched, delays, pulse_phase, beam_map, range_shift, phase_base, phase_rate, tap_offsets):
    pulses, blocks, parts, hop = raw_echoes.shape
    beams = delays.shape[1]
    levels = tap_offsets.shape[0]
    bins = blocks * hop
    slots = beams // 2 + 1
    index = lax.axis_index("pulse").astype(jnp.int32).reshape(1)
    f32, bf16 = jnp.float32, jnp.bfloat16
    image_shape = jax.ShapeDtypeStruct((beams, 2, HALF, LANES), f32)
    send_shape = jax.ShapeDtypeStruct((slots, 2, HALF, LANES), bf16)
    ext_scratch = pltpu.VMEM((slots, 2, HALF + 2 * HALO, LANES), f32)
    rows = pulses * blocks
    image, send = pl.pallas_call(
        front_kernel,
        out_shape=(image_shape, send_shape),
        in_specs=[SMEM_SPEC, VMEM_SPEC, VMEM_SPEC, SMEM_SPEC, VMEM_SPEC],
        out_specs=(VMEM_SPEC, VMEM_SPEC),
        scratch_shapes=[
            pltpu.VMEM((16 + 2 * rows, LANES), f32),
            pltpu.VMEM((2 * LANES, 4 * LANES), bf16),
            pltpu.VMEM((rows, 4 * LANES), bf16),
            pltpu.VMEM((pulses, 2, HALF + 2 * HALO, LANES), f32),
            pltpu.VMEM((2, pulses, beams), f32),
            pltpu.SMEM((2, pulses, beams), f32),
            pltpu.SemaphoreType.DMA,
        ],
        compiler_params=params(),
        name="front",
    )(index, raw_echoes.reshape(pulses * blocks * parts, hop), matched, delays, pulse_phase)
    for level in range(levels):
        received = lax.ppermute(send, "pulse", route("pulse", level))
        partial, turn = pl.pallas_call(
            functools.partial(own_kernel, level, bins),
            out_shape=(image_shape, image_shape),
            in_specs=[SMEM_SPEC] * 6 + [VMEM_SPEC],
            out_specs=(VMEM_SPEC, VMEM_SPEC),
            scratch_shapes=[ext_scratch],
            compiler_params=params(),
            cost_estimate=pl.CostEstimate(flops=4 * 10**6, bytes_accessed=3 * 2**20, transcendentals=0),
            name=f"own{level}",
        )(index, beam_map, range_shift, phase_base, phase_rate, tap_offsets, image)
        operands = (index, beam_map, range_shift, tap_offsets, received, partial, turn)
        in_specs = [SMEM_SPEC] * 4 + [VMEM_SPEC] * 3
        if level < levels - 1:
            image, send = pl.pallas_call(
                functools.partial(middle_kernel, level),
                out_shape=(image_shape, send_shape),
                in_specs=in_specs,
                out_specs=(VMEM_SPEC, VMEM_SPEC),
                scratch_shapes=[ext_scratch],
                compiler_params=params(),
                name=f"middle{level}",
            )(*operands)
        else:
            out = pl.pallas_call(
                functools.partial(last_kernel, level),
                out_shape=jax.ShapeDtypeStruct((2, beams // 8, HALF * 8, LANES), f32),
                in_specs=in_specs,
                out_specs=VMEM_SPEC,
                scratch_shapes=[ext_scratch],
                compiler_params=params(),
                name="last",
            )(*operands)
    out = out.reshape(2, beams // 8, HALF, 8, LANES)
    return jnp.transpose(out, (0, 1, 3, 2, 4)).reshape(2, beams, bins)


def shifted(array, axis, by):
    count = lax.axis_size(axis)
    pairs = [(i, i + by) for i in range(count) if 0 <= i + by < count]
    return lax.ppermute(array, axis, pairs)


def padded_2(block, sides, width):
    for axis, dim in sides:
        count = lax.axis_size(axis)
        forward = [(i, i + 1) for i in range(count - 1)]
        backward = [(target, source) for source, target in forward]
        low = lax.ppermute(
            lax.slice_in_dim(block, block.shape[dim] - width, None, axis=dim), axis, forward
        )
        high = lax.ppermute(lax.slice_in_dim(block, 0, width, axis=dim), axis, backward)
        block = jnp.concatenate([low, block, high], axis=dim)
    return block


def from_partner(block, axis, bit):
    count = lax.axis_size(axis)
    route = []
    for low in range(count):
        high = low | 1 << bit
        if high != low and high < count:
            route += [(low, high), (high, low)]
    return lax.ppermute(block, axis, route)


def tables(length):
    counter = jnp.arange(length, dtype=jnp.int32)
    product = counter[:, None] * counter[None, :] % length
    angles = product.astype(jnp.float32) * (2.0 * math.pi / length)
    cosine = jnp.cos(angles)
    sine_part = jnp.sin(angles)
    forward = jnp.concatenate(
        [
            jnp.concatenate([cosine, -sine_part], axis=1),
            jnp.concatenate([sine_part, cosine], axis=1),
        ],
        axis=0,
    )
    inverse = jnp.concatenate(
        [
            jnp.concatenate([cosine, sine_part], axis=1),
            jnp.concatenate([-sine_part, cosine], axis=1),
        ],
        axis=0,
    )
    return (forward, inverse)


def compress(echoes, tail, matched, forward_exact, forward, inverse_kept):
    pulses, blocks, parts, hop_bins = echoes.shape
    length = 2 * hop_bins
    previous = jnp.concatenate([tail[:, None], echoes[:, :-1]], axis=1)
    windows = jnp.concatenate([previous, echoes], axis=3).reshape(pulses * blocks, parts * length)
    taps_padded = jnp.concatenate(
        [matched, jnp.zeros((2, length - hop_bins), jnp.float32)], axis=1
    ).reshape(1, 2 * length)
    response = jnp.dot(taps_padded, forward_exact, precision=lax.Precision.HIGHEST)[0]
    resp_real = response[:length]
    resp_imag = response[length:]
    spectrum = jnp.dot(windows, forward, preferred_element_type=jnp.float32)
    spec_real = spectrum[:, :length]
    spec_imag = spectrum[:, length:]
    filt_real = spec_real * resp_real - spec_imag * resp_imag
    filt_imag = spec_real * resp_imag + spec_imag * resp_real
    shaped = jnp.concatenate([filt_real, filt_imag], axis=1).astype(jnp.bfloat16)
    restored = jnp.dot(shaped, inverse_kept, preferred_element_type=jnp.float32) * (1.0 / length)
    return restored.astype(jnp.bfloat16).reshape(pulses, blocks, parts, hop_bins)


def kept_columns(inverse, length):
    half = length // 2
    return jnp.concatenate([inverse[:, half:length], inverse[:, length + half :]], axis=1)


def inside_mask(first_cell, out_cells, bins):
    global_cells = first_cell + jnp.arange(out_cells, dtype=jnp.int32)
    return ((global_cells >= 0) & (global_cells < bins)).astype(jnp.float32)


def row_slices(rows, starts, width):

    def per_pulse(row, start_row):
        return jax.vmap(lambda start: lax.dynamic_slice_in_dim(row, start, width, 1))(start_row)

    return jax.vmap(per_pulse)(rows, starts)


def project(padded, delay_rows, phase_rows, offset_base, out_cells, first_cell, bins):
    pulses = padded.shape[0]
    beam_count = delay_rows.shape[1]
    group_size = math.gcd(pulses, 4)
    block_count = pulses // group_size

    def accumulate(summed, block_index):
        first_row = block_index * group_size
        pulses_block = lax.dynamic_slice_in_dim(padded, first_row, group_size, 0)
        delay_block = lax.dynamic_slice_in_dim(delay_rows, first_row, group_size, 0)
        phase_block = lax.dynamic_slice_in_dim(phase_rows, first_row, group_size, 0)
        starts = delay_block + offset_base
        gathered = row_slices(pulses_block, starts, out_cells).astype(jnp.float32)
        cosine = jnp.cos(phase_block)[:, :, None]
        sine_part = jnp.sin(phase_block)[:, :, None]
        real_part = gathered[:, :, 0] * cosine - gathered[:, :, 1] * sine_part
        imag_part = gathered[:, :, 0] * sine_part + gathered[:, :, 1] * cosine
        return (summed + jnp.stack([jnp.sum(real_part, axis=0), jnp.sum(imag_part, axis=0)]), None)

    summed, unused = lax.scan(
        accumulate,
        jnp.zeros((2, beam_count, out_cells), jnp.float32),
        jnp.arange(block_count, dtype=jnp.int32),
    )
    return summed * inside_mask(first_cell, out_cells, bins) * (1.0 / math.sqrt(pulses))


def tap_weights(tap_values):
    weights = SPREAD + 1.0 - jnp.abs(tap_values).astype(jnp.float32)
    return weights / jnp.sum(weights)


def merge_side(
    source,
    beam_rows,
    offsets,
    phase_zero,
    phase_slope,
    weights,
    tap_values,
    offset_base,
    out_cells,
    first_cell,
    bins,
):
    span = out_cells + 2 * SPREAD
    starts = offsets + offset_base - SPREAD
    windows = jax.vmap(
        lambda beam, start: lax.dynamic_slice(source, (0, beam, start), (2, 1, span))[:, 0],
        out_axes=1,
    )(beam_rows, starts)
    summed = jnp.zeros((2, beam_rows.shape[0], out_cells), jnp.float32)
    for tap_index in range(tap_values.shape[0]):
        tap_start = tap_values[tap_index] + SPREAD
        summed = summed + weights[tap_index] * lax.dynamic_slice_in_dim(
            windows, tap_start, out_cells, 2
        )
    positions = jnp.arange(out_cells, dtype=jnp.int32)
    global_cells = (first_cell + positions).astype(jnp.float32)
    angle_grid = (
        phase_zero[:, None] + 2.0 * math.pi / bins * phase_slope[:, None] * global_cells[None, :]
    )
    cosine = jnp.cos(angle_grid)
    sine_part = jnp.sin(angle_grid)
    return jnp.stack(
        [summed[0] * cosine - summed[1] * sine_part, summed[0] * sine_part + summed[1] * cosine]
    )


def pick_sides(table, level_index, side_bit):
    half_rows = lax.dynamic_index_in_dim(table[level_index], side_bit, 0, keepdims=False)
    own_rows = lax.dynamic_index_in_dim(half_rows, side_bit, 0, keepdims=False)
    other_rows = lax.dynamic_index_in_dim(half_rows, 1 - side_bit, 0, keepdims=False)
    return (own_rows, other_rows)


def local_split(
    raw_echoes,
    matched,
    delays,
    pulse_phase,
    beam_map,
    range_shift,
    phase_base,
    phase_rate,
    tap_offsets,
):
    pulses = raw_echoes.shape[0]
    hop_bins = raw_echoes.shape[3]
    local_cells = raw_echoes.shape[1] * hop_bins
    bins = local_cells * lax.axis_size("rng")
    length = 2 * hop_bins
    levels = tap_offsets.shape[0]
    forward_exact, inverse_exact = tables(length)
    forward = forward_exact.astype(jnp.bfloat16)
    inverse_kept = kept_columns(inverse_exact.astype(jnp.bfloat16), length)
    tail = shifted(raw_echoes[:, -1], "rng", 1)
    compressed = compress(raw_echoes, tail, matched, forward_exact, forward, inverse_kept)
    compressed = jnp.transpose(compressed, (0, 2, 1, 3)).reshape(pulses, 2, local_cells)
    first_cell = lax.axis_index("rng") * local_cells
    rim_cells = SHIFT + SPREAD
    margin_cells = levels * rim_cells
    padded = padded_2(compressed, (("rng", 2),), SHIFT + margin_cells)
    polar_image = project(
        padded,
        delays,
        pulse_phase,
        SHIFT,
        local_cells + 2 * margin_cells,
        first_cell - margin_cells,
        bins,
    )
    pulse_index = lax.axis_index("pulse")
    for level_index in range(levels):
        side_bit = pulse_index // 2**level_index % 2
        own_beams, other_beams = pick_sides(beam_map, level_index, side_bit)
        own_offsets, other_offsets = pick_sides(range_shift, level_index, side_bit)
        own_zero, other_zero = pick_sides(phase_base, level_index, side_bit)
        own_slope, other_slope = pick_sides(phase_rate, level_index, side_bit)
        tap_values = tap_offsets[level_index]
        weights = tap_weights(tap_values)
        received = from_partner(polar_image, "pulse", level_index)
        own_source = polar_image
        out_margin = max(margin_cells - rim_cells * (level_index + 1), 0)
        out_cells = local_cells + 2 * out_margin
        start_cell = first_cell - out_margin
        own_side = merge_side(
            own_source,
            own_beams,
            own_offsets,
            own_zero,
            own_slope,
            weights,
            tap_values,
            rim_cells,
            out_cells,
            start_cell,
            bins,
        )
        other_side = merge_side(
            received,
            other_beams,
            other_offsets,
            other_zero,
            other_slope,
            weights,
            tap_values,
            rim_cells,
            out_cells,
            start_cell,
            bins,
        )
        polar_image = (own_side + other_side) * SQRT_HALF * inside_mask(start_cell, out_cells, bins)
    return polar_image


def solution(mesh):
    in_specs = (
        P(("grp", "pulse"), "rng", None, None),
        P(),
        P(("grp", "pulse"), None),
        P(("grp", "pulse"), None),
        P(),
        P(),
        P(),
        P(),
        P(),
    )
    out_specs = P(None, ("grp", "pulse"), "rng")
    whole_range = mesh.shape["rng"] == 1
    return jax.shard_map(local if whole_range else local_split, mesh=mesh, in_specs=in_specs, out_specs=out_specs, check_vma=False)
```

```python
import functools
import math

import jax
import jax.numpy as jnp
import numpy as np
from jax import lax
from jax.experimental import pallas as pl
from jax.experimental.pallas import tpu as pltpu
from jax.sharding import PartitionSpec as P

SPREAD = 4
SHIFT = 24
HALO = 32
LANES = 128
HALF = 64
SQRT_HALF = 0.7071067811865476
VMEM_LIMIT = 24 * 2**20

COS_COEFFS = (
    1.0,
    -19.73920440673828,
    64.93911743164062,
    -85.45014190673828,
    60.16762924194336,
    -25.967599868774414,
    6.528658390045166,
)
SIN_COEFFS = (
    6.2831854820251465,
    -41.34170150756836,
    81.60513305664062,
    -76.70301818847656,
    42.02592849731445,
    -14.899847030639648,
    3.2381374835968018,
)

SMEM_SPEC = pl.BlockSpec(memory_space=pltpu.SMEM)
VMEM_SPEC = pl.BlockSpec(memory_space=pltpu.VMEM)
HBM_SPEC = pl.BlockSpec(memory_space=pltpu.HBM)


def cos_sin_turns(turns):
    f = turns - jnp.round(turns)
    u = f * f
    c = jnp.full_like(u, COS_COEFFS[-1])
    for a in COS_COEFFS[-2::-1]:
        c = c * u + a
    s = jnp.full_like(u, SIN_COEFFS[-1])
    for a in SIN_COEFFS[-2::-1]:
        s = s * u + a
    return c, s * f


def times(x, y):
    return x[0] * y[0] - x[1] * y[1], x[0] * y[1] + x[1] * y[0]


def lane_iota(rows):
    return lax.broadcasted_iota(jnp.int32, (rows, LANES), 1)


def store_extended(ext_ref, where, body):
    lane = lane_iota(HALO)
    high, low = body[:HALO], body[HALF - HALO :]
    ext_ref[(*where, pl.ds(HALO, HALF))] = body
    after = jnp.where(lane < HALF, pltpu.roll(high, HALF, 1), pltpu.roll(high, HALF - 1, 1))
    ext_ref[(*where, pl.ds(HALO + HALF, HALO))] = jnp.where(lane == LANES - 1, 0.0, after)
    before = jnp.where(lane < HALF, pltpu.roll(low, HALF + 1, 1), pltpu.roll(low, HALF, 1))
    ext_ref[(*where, pl.ds(0, HALO))] = jnp.where(lane == 0, 0.0, before)


def front_kernel(
    index_ref, raw_hbm, matched_hbm, delays_hbm, phase_hbm, *rest
):
    tables, rest = rest[:5], rest[5:]
    send_ref, rest_ref, rest = rest[0], rest[1], rest[2:]
    copied, rest = rest[:5], rest[5:]
    raw, matched, phase, delays, raw32, taps, windows, ext, trig, trig_smem, sems = rest
    pulses, beams = phase.shape
    rows = raw.shape[0] // 2
    blocks = rows // pulses
    pairs = rows // LANES
    size = raw.shape[0] // pairs
    side_bit = index_ref[0] % 2

    small = [
        pltpu.make_async_copy(matched_hbm, matched, sems.at[0]),
        pltpu.make_async_copy(phase_hbm, phase, sems.at[1]),
        pltpu.make_async_copy(delays_hbm, delays, sems.at[2]),
    ]
    small += [
        pltpu.make_async_copy(source, target, sems.at[4 + i]) for i, (source, target) in enumerate(zip(tables, copied))
    ]
    large = [
        pltpu.make_async_copy(
            raw_hbm.at[pl.ds(pair * size, size)], raw.at[pl.ds(pair * size, size)], sems.at[4 + len(tables) + pair]
        )
        for pair in range(pairs)
    ]
    small[1].start()
    small[0].start()
    for copy in large:
        copy.start()
    for copy in small[2:]:
        copy.start()
    small[1].wait()
    scale = 1.0 / math.sqrt(pulses)
    c, s = cos_sin_turns(phase[...] * (0.5 / math.pi))
    trig[0] = c * scale
    trig[1] = s * scale
    factors = pltpu.make_async_copy(trig, trig_smem, sems.at[3])
    factors.start()
    small[0].wait()
    row = lax.broadcasted_iota(jnp.int32, (LANES, LANES), 0)
    column = lax.broadcasted_iota(jnp.int32, (LANES, LANES), 1)
    for part in range(2):
        line = jnp.broadcast_to(matched[part : part + 1, :], (LANES, LANES))
        circulant = pltpu.roll(line, 0, 1, stride=1, stride_axis=0).T
        now = jnp.where(column <= row, circulant, 0.0).astype(jnp.bfloat16)
        before = jnp.where(column > row, circulant, 0.0).astype(jnp.bfloat16)
        if part == 0:
            taps[0:LANES, 0:LANES] = before
            taps[LANES:, LANES : 2 * LANES] = before
            taps[0:LANES, 2 * LANES : 3 * LANES] = now
            taps[LANES:, 3 * LANES :] = now
        else:
            taps[0:LANES, LANES : 2 * LANES] = -before
            taps[LANES:, 0:LANES] = before
            taps[0:LANES, 3 * LANES :] = -now
            taps[LANES:, 2 * LANES : 3 * LANES] = now
    raw32[0:16] = jnp.zeros((16, LANES), jnp.float32)
    first = lax.broadcasted_iota(jnp.int32, (LANES, LANES), 0) % blocks == 0
    lane = lane_iota(HALF)
    for pair in range(pairs):
        large[pair].wait()
        raw32[16 + pair * size : 16 + (pair + 1) * size] = raw[pair * size : (pair + 1) * size, :].astype(jnp.float32)
        mine = slice(pair * LANES, (pair + 1) * LANES)
        for part in range(2):
            previous = raw32[pl.ds(14 + pair * size + part, LANES, stride=2), :]
            windows[mine, part * LANES : (part + 1) * LANES] = jnp.where(first, 0.0, previous).astype(jnp.bfloat16)
            current = raw32[pl.ds(16 + pair * size + part, LANES, stride=2), :]
            windows[mine, (2 + part) * LANES : (3 + part) * LANES] = current.astype(jnp.bfloat16)
    for pair in range(pairs):
        made = lax.dot_general(
            taps[...],
            windows[pair * LANES : (pair + 1) * LANES, :],
            (((1,), (1,)), ((), ())),
            preferred_element_type=jnp.float32,
        )
        for part in range(2):
            a = made[part * LANES : part * LANES + HALF]
            b = made[part * LANES + HALF : (part + 1) * LANES]
            store_extended(ext, (2 * pair, part), jnp.where(lane < HALF, a, pltpu.roll(b, HALF, 1)))
            store_extended(ext, (2 * pair + 1, part), jnp.where(lane < HALF, pltpu.roll(a, HALF, 1), b))
    factors.wait()
    small[2].wait()
    urgent = (1 - side_bit) * 7
    count = send_ref.shape[0]
    piece = 32

    def beam(m, carry, sent):
        k = (urgent + m) % beams
        for first_row in range(0, HALF, piece):
            real = imag = None
            for p in range(pulses):
                start = delays[p, k] + (HALO + first_row)
                x = ext[p, 0, pl.ds(start, piece), :]
                y = ext[p, 1, pl.ds(start, piece), :]
                cosine = trig_smem[0, p, k]
                sine = trig_smem[1, p, k]
                re = x * cosine - y * sine
                im = x * sine + y * cosine
                real = re if real is None else real + re
                imag = im if imag is None else imag + im
            rows_here = pl.ds(first_row, piece)
            if sent:
                send_ref[m, 0, rows_here] = real.astype(jnp.bfloat16)
                send_ref[m, 1, rows_here] = imag.astype(jnp.bfloat16)
            else:
                rest_ref[m - count, 0, rows_here] = real
                rest_ref[m - count, 1, rows_here] = imag
        return carry

    lax.fori_loop(0, count, functools.partial(beam, sent=True), 0, unroll=3)
    lax.fori_loop(count, beams, functools.partial(beam, sent=False), 0, unroll=7)
    for copy in small[3:]:
        copy.wait()


def tap_factors(taps_ref, level):
    count = taps_ref.shape[1]
    offsets = [taps_ref[level, t] for t in range(count)]
    weights = [(SPREAD + 1.0) - jnp.abs(o).astype(jnp.float32) for o in offsets]
    total = weights[0]
    for w in weights[1:]:
        total = total + w
    scale = SQRT_HALF / total
    return offsets, [w * scale for w in weights]


def filtered(ext, slot, start, rows, offsets, weights):
    sums = []
    for part in range(2):
        total = None
        for offset, weight in zip(offsets, weights):
            term = ext[slot, part, pl.ds(start + offset, rows), :] * weight
            total = term if total is None else total + term
        sums.append(total)
    return tuple(sums)


def merged(level, side_bit, k, first_row, rows, tables, factors, ext, partial_ref, turn_ref):
    beam_ref, shift_ref = tables
    other = (level, side_bit, 1 - side_bit, k)
    slot = beam_ref[other] - side_bit * 7
    start = shift_ref[other] + (HALO + first_row)
    here = pl.ds(first_row, rows)
    real, imag = times(filtered(ext, slot, start, rows, *factors), (turn_ref[k, 0, here], turn_ref[k, 1, here]))
    return real + partial_ref[k, 0, here], imag + partial_ref[k, 1, here]


def turns(base, rate, bins):
    t = lax.broadcasted_iota(jnp.int32, (8, LANES), 0)
    lane = lane_iota(8)
    position = (t + (lane % HALF) * LANES + (lane // HALF) * HALF).astype(jnp.float32) * (1.0 / bins)
    groups = [cos_sin_turns(position * rate + base * (0.5 / math.pi))]
    step = cos_sin_turns(jnp.full((8, LANES), rate * (8.0 / bins)))
    while len(groups) < HALF // 8:
        groups += [times(g, step) for g in groups]
        step = times(step, step)
    return tuple(jnp.concatenate([g[i] for g in groups], axis=0) for i in range(2))


def own_kernel(
    level, bins, index_ref, beam_ref, shift_ref, base_ref, rate_ref, taps_ref, send_ref, *rest
):
    if level == 0:
        (rest_ref, partial_ref, turn_ref, ext) = rest
    else:
        (received_ext, last_partial, last_turn, partial_ref, turn_ref, ext) = rest
    side_bit = (index_ref[0] >> level) % 2
    beams = partial_ref.shape[0]
    count = send_ref.shape[0]
    shared = 2 * count - beams
    low_beam = side_bit * 7
    urgent = (1 - side_bit) * 7

    for i in range(shared):
        for part in range(2):
            body = send_ref[7 * side_bit + i, part].astype(jnp.float32)
            store_extended(ext, (7 * (1 - side_bit) + i, part), body)
    if level > 0:
        last_bit = (index_ref[0] >> (level - 1)) % 2
        last_factors = tap_factors(taps_ref, level - 1)

    def remaining(m, carry):
        k = (urgent + m) % beams
        if level == 0:
            pair = rest_ref[m - count, 0], rest_ref[m - count, 1]
        else:
            pair = merged(
                level - 1, last_bit, k, 0, HALF, (beam_ref, shift_ref), last_factors, received_ext, last_partial, last_turn
            )
        for part in range(2):
            store_extended(ext, (k - low_beam, part), pair[part])
        return carry

    lax.fori_loop(count, beams, remaining, 0, unroll=7)
    factors = tap_factors(taps_ref, level)

    def beam(k, carry):
        own = (level, side_bit, side_bit, k)
        other = (level, side_bit, 1 - side_bit, k)
        slot = beam_ref[own] - low_beam
        start = shift_ref[own] + HALO
        turn = turns(base_ref[own], rate_ref[own], bins)
        for first_row in range(0, HALF, 32):
            here = slice(first_row, first_row + 32)
            real, imag = times(
                filtered(ext, slot, start + first_row, 32, *factors), (turn[0][here], turn[1][here])
            )
            partial_ref[k, 0, here] = real
            partial_ref[k, 1, here] = imag
        turn_ref[k, 0], turn_ref[k, 1] = turns(base_ref[other], rate_ref[other], bins)
        return carry

    lax.fori_loop(0, beams, beam, 0, unroll=2)


def extend_received(received_ref, ext):
    def extend(slot, carry):
        for part in range(2):
            store_extended(ext, (slot, part), received_ref[slot, part].astype(jnp.float32))
        return carry

    lax.fori_loop(0, ext.shape[0], extend, 0, unroll=3)


def middle_kernel(
    level, index_ref, beam_ref, shift_ref, taps_ref, received_ref, partial_ref, turn_ref, send_ref, ext,
):
    side_bit = (index_ref[0] >> level) % 2
    urgent = (1 - (index_ref[0] >> (level + 1)) % 2) * 7
    extend_received(received_ref, ext)
    factors = tap_factors(taps_ref, level)

    def beam(m, carry):
        for first_row in range(0, HALF, 32):
            pair = merged(
                level, side_bit, urgent + m, first_row, 32, (beam_ref, shift_ref), factors, ext, partial_ref, turn_ref
            )
            for part in range(2):
                send_ref[m, part, pl.ds(first_row, 32)] = pair[part].astype(jnp.bfloat16)
        return carry

    lax.fori_loop(0, send_ref.shape[0], beam, 0, unroll=9)


def last_kernel(
    level, index_ref, beam_ref, shift_ref, taps_ref, received_ref, partial_ref, turn_ref, out_ref, ext,
):
    side_bit = (index_ref[0] >> level) % 2
    extend_received(received_ref, ext)
    factors = tap_factors(taps_ref, level)
    lane = lane_iota(HALF)
    tables = (beam_ref, shift_ref)

    def pair(m, carry):
        even = merged(level, side_bit, 2 * m, 0, HALF, tables, factors, ext, partial_ref, turn_ref)
        odd = merged(level, side_bit, 2 * m + 1, 0, HALF, tables, factors, ext, partial_ref, turn_ref)
        high, low = m // 4, 2 * (m % 4)
        for part in range(2):
            turned = jnp.concatenate([even[part], odd[part]], axis=0).T
            a = turned[:HALF]
            b = turned[HALF:]
            out_ref[part, high, pl.ds(low, HALF, stride=8), :] = jnp.where(lane < HALF, a, pltpu.roll(b, HALF, 1))
            out_ref[part, high, pl.ds(low + 1, HALF, stride=8), :] = jnp.where(lane < HALF, pltpu.roll(a, HALF, 1), b)
        return carry

    lax.fori_loop(0, partial_ref.shape[0] // 2, pair, 0, unroll=2)


def params():
    return pltpu.CompilerParams(vmem_limit_bytes=VMEM_LIMIT)


def route(axis, bit):
    count = lax.axis_size(axis)
    return [(i, i ^ (1 << bit)) for i in range(count) if i ^ (1 << bit) < count]


def local(raw_echoes, matched, delays, pulse_phase, beam_map, range_shift, phase_base, phase_rate, tap_offsets):
    pulses, blocks, parts, hop = raw_echoes.shape
    beams = delays.shape[1]
    levels = tap_offsets.shape[0]
    bins = blocks * hop
    slots = beams // 2 + 1
    index = lax.axis_index("pulse").astype(jnp.int32).reshape(1)
    f32, bf16 = jnp.float32, jnp.bfloat16
    image_shape = jax.ShapeDtypeStruct((beams, 2, HALF, LANES), f32)
    rest_shape = jax.ShapeDtypeStruct((beams - slots, 2, HALF, LANES), f32)
    send_shape = jax.ShapeDtypeStruct((slots, 2, HALF, LANES), bf16)
    ext_dims = (slots, 2, HALF + 2 * HALO, LANES)
    rows = pulses * blocks
    inputs = (beam_map, range_shift, phase_base, phase_rate, tap_offsets)
    sources = (raw_echoes.reshape(rows * parts, hop), matched, delays, pulse_phase, *inputs)
    send, rest, *tables = pl.pallas_call(
        front_kernel,
        out_shape=(send_shape, rest_shape, *(pltpu.SMEM(x.shape, x.dtype) for x in inputs)),
        in_specs=[SMEM_SPEC] + [HBM_SPEC] * (4 + len(inputs)),
        out_specs=(VMEM_SPEC, VMEM_SPEC, *(SMEM_SPEC for x in inputs)),
        scratch_shapes=[
            pltpu.VMEM((parts * rows, LANES), bf16),
            pltpu.VMEM(matched.shape, f32),
            pltpu.VMEM(pulse_phase.shape, f32),
            pltpu.SMEM(delays.shape, jnp.int32),
            pltpu.VMEM((16 + parts * rows, LANES), f32),
            pltpu.VMEM((2 * LANES, 4 * LANES), bf16),
            pltpu.VMEM((rows, 4 * LANES), bf16),
            pltpu.VMEM((pulses, 2, HALF + 2 * HALO, LANES), f32),
            pltpu.VMEM((2, pulses, beams), f32),
            pltpu.SMEM((2, pulses, beams), f32),
            pltpu.SemaphoreType.DMA((4 + len(inputs) + rows // LANES,)),
        ],
        compiler_params=params(),
        name="front",
    )(index, *(pltpu.with_memory_space_constraint(x, pltpu.HBM) for x in sources))
    beam_table, shift_table, base_table, rate_table, tap_table = tables
    received_ext = partial = turn = None
    for level in range(levels):
        received = lax.ppermute(send, "pulse", route("pulse", level))
        before = (rest,) if level == 0 else (received_ext, partial, turn)
        partial, turn = pl.pallas_call(
            functools.partial(own_kernel, level, bins),
            out_shape=(image_shape, image_shape),
            in_specs=[SMEM_SPEC] * 6 + [VMEM_SPEC] * (1 + len(before)),
            out_specs=(VMEM_SPEC, VMEM_SPEC),
            scratch_shapes=[pltpu.VMEM(ext_dims, f32)],
            compiler_params=params(),
            cost_estimate=pl.CostEstimate(flops=4 * 10**6, bytes_accessed=3 * 2**20, transcendentals=0),
            name=f"own{level}",
        )(index, *tables, send, *before)
        operands = (index, beam_table, shift_table, tap_table, received, partial, turn)
        in_specs = [SMEM_SPEC] * 4 + [VMEM_SPEC] * 3
        if level < levels - 1:
            send, received_ext = pl.pallas_call(
                functools.partial(middle_kernel, level),
                out_shape=(send_shape, jax.ShapeDtypeStruct(ext_dims, f32)),
                in_specs=in_specs,
                out_specs=(VMEM_SPEC, VMEM_SPEC),
                compiler_params=params(),
                name=f"middle{level}",
            )(*operands)
        else:
            out = pl.pallas_call(
                functools.partial(last_kernel, level),
                out_shape=jax.ShapeDtypeStruct((2, beams // 8, HALF * 8, LANES), f32),
                in_specs=in_specs,
                out_specs=VMEM_SPEC,
                scratch_shapes=[pltpu.VMEM(ext_dims, f32)],
                compiler_params=params(),
                name="last",
            )(*operands)
    out = out.reshape(2, beams // 8, HALF, 8, LANES)
    return jnp.transpose(out, (0, 1, 3, 2, 4)).reshape(2, beams, bins)


def shifted(array, axis, by):
    count = lax.axis_size(axis)
    pairs = [(i, i + by) for i in range(count) if 0 <= i + by < count]
    return lax.ppermute(array, axis, pairs)


def padded_2(block, sides, width):
    for axis, dim in sides:
        count = lax.axis_size(axis)
        forward = [(i, i + 1) for i in range(count - 1)]
        backward = [(target, source) for source, target in forward]
        low = lax.ppermute(
            lax.slice_in_dim(block, block.shape[dim] - width, None, axis=dim), axis, forward
        )
        high = lax.ppermute(lax.slice_in_dim(block, 0, width, axis=dim), axis, backward)
        block = jnp.concatenate([low, block, high], axis=dim)
    return block


def from_partner(block, axis, bit):
    count = lax.axis_size(axis)
    route = []
    for low in range(count):
        high = low | 1 << bit
        if high != low and high < count:
            route += [(low, high), (high, low)]
    return lax.ppermute(block, axis, route)


def tables(length):
    counter = jnp.arange(length, dtype=jnp.int32)
    product = counter[:, None] * counter[None, :] % length
    angles = product.astype(jnp.float32) * (2.0 * math.pi / length)
    cosine = jnp.cos(angles)
    sine_part = jnp.sin(angles)
    forward = jnp.concatenate(
        [
            jnp.concatenate([cosine, -sine_part], axis=1),
            jnp.concatenate([sine_part, cosine], axis=1),
        ],
        axis=0,
    )
    inverse = jnp.concatenate(
        [
            jnp.concatenate([cosine, sine_part], axis=1),
            jnp.concatenate([-sine_part, cosine], axis=1),
        ],
        axis=0,
    )
    return (forward, inverse)


def compress(echoes, tail, matched, forward_exact, forward, inverse_kept):
    pulses, blocks, parts, hop_bins = echoes.shape
    length = 2 * hop_bins
    previous = jnp.concatenate([tail[:, None], echoes[:, :-1]], axis=1)
    windows = jnp.concatenate([previous, echoes], axis=3).reshape(pulses * blocks, parts * length)
    taps_padded = jnp.concatenate(
        [matched, jnp.zeros((2, length - hop_bins), jnp.float32)], axis=1
    ).reshape(1, 2 * length)
    response = jnp.dot(taps_padded, forward_exact, precision=lax.Precision.HIGHEST)[0]
    resp_real = response[:length]
    resp_imag = response[length:]
    spectrum = jnp.dot(windows, forward, preferred_element_type=jnp.float32)
    spec_real = spectrum[:, :length]
    spec_imag = spectrum[:, length:]
    filt_real = spec_real * resp_real - spec_imag * resp_imag
    filt_imag = spec_real * resp_imag + spec_imag * resp_real
    shaped = jnp.concatenate([filt_real, filt_imag], axis=1).astype(jnp.bfloat16)
    restored = jnp.dot(shaped, inverse_kept, preferred_element_type=jnp.float32) * (1.0 / length)
    return restored.astype(jnp.bfloat16).reshape(pulses, blocks, parts, hop_bins)


def kept_columns(inverse, length):
    half = length // 2
    return jnp.concatenate([inverse[:, half:length], inverse[:, length + half :]], axis=1)


def inside_mask(first_cell, out_cells, bins):
    global_cells = first_cell + jnp.arange(out_cells, dtype=jnp.int32)
    return ((global_cells >= 0) & (global_cells < bins)).astype(jnp.float32)


def row_slices(rows, starts, width):

    def per_pulse(row, start_row):
        return jax.vmap(lambda start: lax.dynamic_slice_in_dim(row, start, width, 1))(start_row)

    return jax.vmap(per_pulse)(rows, starts)


def project(padded, delay_rows, phase_rows, offset_base, out_cells, first_cell, bins):
    pulses = padded.shape[0]
    beam_count = delay_rows.shape[1]
    group_size = math.gcd(pulses, 4)
    block_count = pulses // group_size

    def accumulate(summed, block_index):
        first_row = block_index * group_size
        pulses_block = lax.dynamic_slice_in_dim(padded, first_row, group_size, 0)
        delay_block = lax.dynamic_slice_in_dim(delay_rows, first_row, group_size, 0)
        phase_block = lax.dynamic_slice_in_dim(phase_rows, first_row, group_size, 0)
        starts = delay_block + offset_base
        gathered = row_slices(pulses_block, starts, out_cells).astype(jnp.float32)
        cosine = jnp.cos(phase_block)[:, :, None]
        sine_part = jnp.sin(phase_block)[:, :, None]
        real_part = gathered[:, :, 0] * cosine - gathered[:, :, 1] * sine_part
        imag_part = gathered[:, :, 0] * sine_part + gathered[:, :, 1] * cosine
        return (summed + jnp.stack([jnp.sum(real_part, axis=0), jnp.sum(imag_part, axis=0)]), None)

    summed, unused = lax.scan(
        accumulate,
        jnp.zeros((2, beam_count, out_cells), jnp.float32),
        jnp.arange(block_count, dtype=jnp.int32),
    )
    return summed * inside_mask(first_cell, out_cells, bins) * (1.0 / math.sqrt(pulses))


def tap_weights(tap_values):
    weights = SPREAD + 1.0 - jnp.abs(tap_values).astype(jnp.float32)
    return weights / jnp.sum(weights)


def merge_side(
    source,
    beam_rows,
    offsets,
    phase_zero,
    phase_slope,
    weights,
    tap_values,
    offset_base,
    out_cells,
    first_cell,
    bins,
):
    span = out_cells + 2 * SPREAD
    starts = offsets + offset_base - SPREAD
    windows = jax.vmap(
        lambda beam, start: lax.dynamic_slice(source, (0, beam, start), (2, 1, span))[:, 0],
        out_axes=1,
    )(beam_rows, starts)
    summed = jnp.zeros((2, beam_rows.shape[0], out_cells), jnp.float32)
    for tap_index in range(tap_values.shape[0]):
        tap_start = tap_values[tap_index] + SPREAD
        summed = summed + weights[tap_index] * lax.dynamic_slice_in_dim(
            windows, tap_start, out_cells, 2
        )
    positions = jnp.arange(out_cells, dtype=jnp.int32)
    global_cells = (first_cell + positions).astype(jnp.float32)
    angle_grid = (
        phase_zero[:, None] + 2.0 * math.pi / bins * phase_slope[:, None] * global_cells[None, :]
    )
    cosine = jnp.cos(angle_grid)
    sine_part = jnp.sin(angle_grid)
    return jnp.stack(
        [summed[0] * cosine - summed[1] * sine_part, summed[0] * sine_part + summed[1] * cosine]
    )


def pick_sides(table, level_index, side_bit):
    half_rows = lax.dynamic_index_in_dim(table[level_index], side_bit, 0, keepdims=False)
    own_rows = lax.dynamic_index_in_dim(half_rows, side_bit, 0, keepdims=False)
    other_rows = lax.dynamic_index_in_dim(half_rows, 1 - side_bit, 0, keepdims=False)
    return (own_rows, other_rows)


def local_split(
    raw_echoes,
    matched,
    delays,
    pulse_phase,
    beam_map,
    range_shift,
    phase_base,
    phase_rate,
    tap_offsets,
):
    pulses = raw_echoes.shape[0]
    hop_bins = raw_echoes.shape[3]
    local_cells = raw_echoes.shape[1] * hop_bins
    bins = local_cells * lax.axis_size("rng")
    length = 2 * hop_bins
    levels = tap_offsets.shape[0]
    forward_exact, inverse_exact = tables(length)
    forward = forward_exact.astype(jnp.bfloat16)
    inverse_kept = kept_columns(inverse_exact.astype(jnp.bfloat16), length)
    tail = shifted(raw_echoes[:, -1], "rng", 1)
    compressed = compress(raw_echoes, tail, matched, forward_exact, forward, inverse_kept)
    compressed = jnp.transpose(compressed, (0, 2, 1, 3)).reshape(pulses, 2, local_cells)
    first_cell = lax.axis_index("rng") * local_cells
    rim_cells = SHIFT + SPREAD
    margin_cells = levels * rim_cells
    padded = padded_2(compressed, (("rng", 2),), SHIFT + margin_cells)
    polar_image = project(
        padded,
        delays,
        pulse_phase,
        SHIFT,
        local_cells + 2 * margin_cells,
        first_cell - margin_cells,
        bins,
    )
    pulse_index = lax.axis_index("pulse")
    for level_index in range(levels):
        side_bit = pulse_index // 2**level_index % 2
        own_beams, other_beams = pick_sides(beam_map, level_index, side_bit)
        own_offsets, other_offsets = pick_sides(range_shift, level_index, side_bit)
        own_zero, other_zero = pick_sides(phase_base, level_index, side_bit)
        own_slope, other_slope = pick_sides(phase_rate, level_index, side_bit)
        tap_values = tap_offsets[level_index]
        weights = tap_weights(tap_values)
        received = from_partner(polar_image, "pulse", level_index)
        own_source = polar_image
        out_margin = max(margin_cells - rim_cells * (level_index + 1), 0)
        out_cells = local_cells + 2 * out_margin
        start_cell = first_cell - out_margin
        own_side = merge_side(
            own_source,
            own_beams,
            own_offsets,
            own_zero,
            own_slope,
            weights,
            tap_values,
            rim_cells,
            out_cells,
            start_cell,
            bins,
        )
        other_side = merge_side(
            received,
            other_beams,
            other_offsets,
            other_zero,
            other_slope,
            weights,
            tap_values,
            rim_cells,
            out_cells,
            start_cell,
            bins,
        )
        polar_image = (own_side + other_side) * SQRT_HALF * inside_mask(start_cell, out_cells, bins)
    return polar_image


def solution(mesh):
    in_specs = (
        P(("grp", "pulse"), "rng", None, None),
        P(),
        P(("grp", "pulse"), None),
        P(("grp", "pulse"), None),
        P(),
        P(),
        P(),
        P(),
        P(),
    )
    out_specs = P(None, ("grp", "pulse"), "rng")
    whole_range = mesh.shape["rng"] == 1
    return jax.shard_map(local if whole_range else local_split, mesh=mesh, in_specs=in_specs, out_specs=out_specs, check_vma=False)
```

```python
import functools
import math

import jax
import jax.numpy as jnp
import numpy as np
from jax import lax
from jax.experimental import pallas as pl
from jax.experimental.pallas import tpu as pltpu
from jax.sharding import PartitionSpec as P

SPREAD = 4
SHIFT = 24
HALO = 32
LANES = 128
HALF = 64
FIRST = 5
ORDERED = (1, 2)
SQRT_HALF = 0.7071067811865476
VMEM_LIMIT = 24 * 2**20

COS_COEFFS = (
    1.0,
    -19.73920440673828,
    64.93911743164062,
    -85.45014190673828,
    60.16762924194336,
    -25.967599868774414,
    6.528658390045166,
)
SIN_COEFFS = (
    6.2831854820251465,
    -41.34170150756836,
    81.60513305664062,
    -76.70301818847656,
    42.02592849731445,
    -14.899847030639648,
    3.2381374835968018,
)

SMEM_SPEC = pl.BlockSpec(memory_space=pltpu.SMEM)
VMEM_SPEC = pl.BlockSpec(memory_space=pltpu.VMEM)
HBM_SPEC = pl.BlockSpec(memory_space=pltpu.HBM)


def cos_sin_turns(turns):
    f = turns - jnp.round(turns)
    u = f * f
    c = jnp.full_like(u, COS_COEFFS[-1])
    for a in COS_COEFFS[-2::-1]:
        c = c * u + a
    s = jnp.full_like(u, SIN_COEFFS[-1])
    for a in SIN_COEFFS[-2::-1]:
        s = s * u + a
    return c, s * f


def times(x, y):
    return x[0] * y[0] - x[1] * y[1], x[0] * y[1] + x[1] * y[0]


def lane_iota(rows):
    return lax.broadcasted_iota(jnp.int32, (rows, LANES), 1)


def store_extended(ext_ref, where, body):
    lane = lane_iota(HALO)
    high, low = body[:HALO], body[HALF - HALO :]
    ext_ref[(*where, pl.ds(HALO, HALF))] = body
    after = jnp.where(lane < HALF, pltpu.roll(high, HALF, 1), pltpu.roll(high, HALF - 1, 1))
    ext_ref[(*where, pl.ds(HALO + HALF, HALO))] = jnp.where(lane == LANES - 1, 0.0, after)
    before = jnp.where(lane < HALF, pltpu.roll(low, HALF + 1, 1), pltpu.roll(low, HALF, 1))
    ext_ref[(*where, pl.ds(0, HALO))] = jnp.where(lane == 0, 0.0, before)


def front_kernel(
    index_ref, raw_hbm, matched_hbm, delays_hbm, phase_hbm, *rest
):
    tables, rest = rest[:5], rest[5:]
    send_ref, rest_ref, rest = rest[0], rest[1], rest[2:]
    copied, rest = rest[:5], rest[5:]
    raw, matched, phase, delays, raw32, taps, windows, ext, trig, trig_smem, sems = rest
    pulses, beams = phase.shape
    rows = raw.shape[0] // 2
    blocks = rows // pulses
    pairs = rows // LANES
    size = raw.shape[0] // pairs
    side_bit = index_ref[0] % 2

    small = [
        pltpu.make_async_copy(matched_hbm, matched, sems.at[0]),
        pltpu.make_async_copy(phase_hbm, phase, sems.at[1]),
        pltpu.make_async_copy(delays_hbm, delays, sems.at[2]),
    ]
    small += [
        pltpu.make_async_copy(source, target, sems.at[4 + i]) for i, (source, target) in enumerate(zip(tables, copied))
    ]
    large = [
        pltpu.make_async_copy(
            raw_hbm.at[pl.ds(pair * size, size)], raw.at[pl.ds(pair * size, size)], sems.at[4 + len(tables) + pair]
        )
        for pair in range(pairs)
    ]
    small[1].start()
    small[0].start()
    for copy in large:
        copy.start()
    for copy in small[2:]:
        copy.start()
    small[1].wait()
    scale = 1.0 / math.sqrt(pulses)
    c, s = cos_sin_turns(phase[...] * (0.5 / math.pi))
    trig[0] = c * scale
    trig[1] = s * scale
    factors = pltpu.make_async_copy(trig, trig_smem, sems.at[3])
    factors.start()
    small[0].wait()
    row = lax.broadcasted_iota(jnp.int32, (LANES, LANES), 0)
    column = lax.broadcasted_iota(jnp.int32, (LANES, LANES), 1)
    for part in range(2):
        line = jnp.broadcast_to(matched[part : part + 1, :], (LANES, LANES))
        circulant = pltpu.roll(line, 0, 1, stride=1, stride_axis=0).T
        now = jnp.where(column <= row, circulant, 0.0).astype(jnp.bfloat16)
        before = jnp.where(column > row, circulant, 0.0).astype(jnp.bfloat16)
        if part == 0:
            taps[0:LANES, 0:LANES] = before
            taps[LANES:, LANES : 2 * LANES] = before
            taps[0:LANES, 2 * LANES : 3 * LANES] = now
            taps[LANES:, 3 * LANES :] = now
        else:
            taps[0:LANES, LANES : 2 * LANES] = -before
            taps[LANES:, 0:LANES] = before
            taps[0:LANES, 3 * LANES :] = -now
            taps[LANES:, 2 * LANES : 3 * LANES] = now
    raw32[0:16] = jnp.zeros((16, LANES), jnp.float32)
    first = lax.broadcasted_iota(jnp.int32, (LANES, LANES), 0) % blocks == 0
    lane = lane_iota(HALF)
    for pair in range(pairs):
        large[pair].wait()
        raw32[16 + pair * size : 16 + (pair + 1) * size] = raw[pair * size : (pair + 1) * size, :].astype(jnp.float32)
        mine = slice(pair * LANES, (pair + 1) * LANES)
        for part in range(2):
            previous = raw32[pl.ds(14 + pair * size + part, LANES, stride=2), :]
            windows[mine, part * LANES : (part + 1) * LANES] = jnp.where(first, 0.0, previous).astype(jnp.bfloat16)
            current = raw32[pl.ds(16 + pair * size + part, LANES, stride=2), :]
            windows[mine, (2 + part) * LANES : (3 + part) * LANES] = current.astype(jnp.bfloat16)
    for pair in range(pairs):
        made = lax.dot_general(
            taps[...],
            windows[pair * LANES : (pair + 1) * LANES, :],
            (((1,), (1,)), ((), ())),
            preferred_element_type=jnp.float32,
        )
        for part in range(2):
            a = made[part * LANES : part * LANES + HALF]
            b = made[part * LANES + HALF : (part + 1) * LANES]
            store_extended(ext, (2 * pair, part), jnp.where(lane < HALF, a, pltpu.roll(b, HALF, 1)))
            store_extended(ext, (2 * pair + 1, part), jnp.where(lane < HALF, pltpu.roll(a, HALF, 1), b))
    factors.wait()
    small[2].wait()
    urgent = (1 - side_bit) * 7
    count = send_ref.shape[0]
    piece = 32

    def beam(m, carry, sent):
        k = (urgent + m) % beams
        for first_row in range(0, HALF, piece):
            real = imag = None
            for p in range(pulses):
                start = delays[p, k] + (HALO + first_row)
                x = ext[p, 0, pl.ds(start, piece), :]
                y = ext[p, 1, pl.ds(start, piece), :]
                cosine = trig_smem[0, p, k]
                sine = trig_smem[1, p, k]
                re = x * cosine - y * sine
                im = x * sine + y * cosine
                real = re if real is None else real + re
                imag = im if imag is None else imag + im
            rows_here = pl.ds(first_row, piece)
            if sent:
                send_ref[m, 0, rows_here] = real.astype(jnp.bfloat16)
                send_ref[m, 1, rows_here] = imag.astype(jnp.bfloat16)
            else:
                rest_ref[m - count, 0, rows_here] = real
                rest_ref[m - count, 1, rows_here] = imag
        return carry

    lax.fori_loop(0, count, functools.partial(beam, sent=True), 0, unroll=3)
    lax.fori_loop(count, beams, functools.partial(beam, sent=False), 0, unroll=7)
    for copy in small[3:]:
        copy.wait()


def tap_factors(taps_ref, level):
    count = taps_ref.shape[1]
    offsets = [taps_ref[level, t] for t in range(count)]
    weights = [(SPREAD + 1.0) - jnp.abs(o).astype(jnp.float32) for o in offsets]
    total = weights[0]
    for w in weights[1:]:
        total = total + w
    scale = SQRT_HALF / total
    return offsets, [w * scale for w in weights]


def filtered(ext, slot, start, rows, offsets, weights):
    sums = []
    for part in range(2):
        total = None
        for offset, weight in zip(offsets, weights):
            term = ext[slot, part, pl.ds(start + offset, rows), :] * weight
            total = term if total is None else total + term
        sums.append(total)
    return tuple(sums)


def order_start(level, index):
    first, second, third = (index >> 1) & 1, (index >> 2) & 1, (index >> 3) & 1
    if level == 1:
        low = (1 - third) * first
        high = third * (2 + first) + (1 - third) * 4
        return second * low + (1 - second) * high
    if level == 2:
        return (1 - third) * (2 + second)
    return 0


def place_of(slot, start, count):
    place = slot - start
    return jnp.where(place < 0, place + count, place)


def slot_at(place, start, count):
    slot = start + place
    return jnp.where(slot >= count, slot - count, slot)


def merged(level, index, k, first_row, rows, tables, factors, count, ext, partial_ref, turn_ref):
    beam_ref, shift_ref = tables
    side_bit = (index >> level) % 2
    other = (level, side_bit, 1 - side_bit, k)
    slot = beam_ref[other] - side_bit * 7
    if level in ORDERED:
        slot = place_of(slot, order_start(level, index), count)
    start = shift_ref[other] + (HALO + first_row)
    here = pl.ds(first_row, rows)
    real, imag = times(filtered(ext, slot, start, rows, *factors), (turn_ref[k, 0, here], turn_ref[k, 1, here]))
    return real + partial_ref[k, 0, here], imag + partial_ref[k, 1, here]


def turns(base, rate, bins):
    t = lax.broadcasted_iota(jnp.int32, (8, LANES), 0)
    lane = lane_iota(8)
    position = (t + (lane % HALF) * LANES + (lane // HALF) * HALF).astype(jnp.float32) * (1.0 / bins)
    groups = [cos_sin_turns(position * rate + base * (0.5 / math.pi))]
    step = cos_sin_turns(jnp.full((8, LANES), rate * (8.0 / bins)))
    while len(groups) < HALF // 8:
        groups += [times(g, step) for g in groups]
        step = times(step, step)
    return tuple(jnp.concatenate([g[i] for g in groups], axis=0) for i in range(2))


def own_kernel(
    level, bins, count, index_ref, beam_ref, shift_ref, base_ref, rate_ref, taps_ref, *rest
):
    if level == 0:
        (send_ref, rest_ref, partial_ref, turn_ref, ext) = rest
    else:
        (first_ref, second_ref, received_ext, last_partial, last_turn, partial_ref, turn_ref, ext) = rest
    index = index_ref[0]
    side_bit = (index >> level) % 2
    beams = partial_ref.shape[0]
    shared = 2 * count - beams
    low_beam = side_bit * 7
    urgent = (1 - side_bit) * 7

    start = order_start(level, index ^ (1 << level))
    for i in range(shared):
        slot = 7 * side_bit + i
        for part in range(2):
            if level == 0:
                body = send_ref[slot, part].astype(jnp.float32)
            else:
                place = place_of(slot, start, count)
                in_first = place < FIRST
                body = jnp.where(
                    in_first,
                    first_ref[jnp.minimum(place, FIRST - 1), part].astype(jnp.float32),
                    second_ref[jnp.maximum(place - FIRST, 0), part].astype(jnp.float32),
                )
            store_extended(ext, (7 * (1 - side_bit) + i, part), body)
    if level > 0:
        last_factors = tap_factors(taps_ref, level - 1)

    def remaining(m, carry):
        k = (urgent + m) % beams
        if level == 0:
            pair = rest_ref[m - count, 0], rest_ref[m - count, 1]
        else:
            pair = merged(
                level - 1, index, k, 0, HALF, (beam_ref, shift_ref), last_factors, count, received_ext, last_partial, last_turn
            )
        for part in range(2):
            store_extended(ext, (k - low_beam, part), pair[part])
        return carry

    lax.fori_loop(count, beams, remaining, 0, unroll=7)
    factors = tap_factors(taps_ref, level)

    def beam(k, carry):
        own = (level, side_bit, side_bit, k)
        other = (level, side_bit, 1 - side_bit, k)
        slot = beam_ref[own] - low_beam
        start = shift_ref[own] + HALO
        turn = turns(base_ref[own], rate_ref[own], bins)
        for first_row in range(0, HALF, 32):
            here = slice(first_row, first_row + 32)
            real, imag = times(
                filtered(ext, slot, start + first_row, 32, *factors), (turn[0][here], turn[1][here])
            )
            partial_ref[k, 0, here] = real
            partial_ref[k, 1, here] = imag
        turn_ref[k, 0], turn_ref[k, 1] = turns(base_ref[other], rate_ref[other], bins)
        return carry

    lax.fori_loop(0, beams, beam, 0, unroll=2)


def extend_received(received_ref, ext, first, unroll):
    def extend(slot, carry):
        for part in range(2):
            store_extended(ext, (first + slot, part), received_ref[slot, part].astype(jnp.float32))
        return carry

    lax.fori_loop(0, received_ref.shape[0], extend, 0, unroll=unroll)


def copy_extended(source, target):
    for slot in range(source.shape[0]):
        target[slot] = source[slot]


def send_parents(level, index, places, sends, tables, factors, count, ext, partial_ref, turn_ref):
    next_bit = (index >> (level + 1)) % 2
    start = order_start(level + 1, index ^ (2 << level))
    for place in places:
        k = (1 - next_bit) * 7 + slot_at(place, start, count)
        target, at = (sends[0], place) if place < FIRST else (sends[-1], place - FIRST)
        for first_row in range(0, HALF, 32):
            pair = merged(level, index, k, first_row, 32, tables, factors, count, ext, partial_ref, turn_ref)
            for part in range(2):
                target[at, part, pl.ds(first_row, 32)] = pair[part].astype(jnp.bfloat16)


def bottom_kernel(
    count, index_ref, beam_ref, shift_ref, taps_ref, received_ref, partial_ref, turn_ref, first_ref, second_ref, ext,
):
    extend_received(received_ref, ext, 0, 3)
    send_parents(
        0, index_ref[0], range(count), (first_ref, second_ref), (beam_ref, shift_ref), tap_factors(taps_ref, 0), count,
        ext, partial_ref, turn_ref,
    )


def middle_first_kernel(
    level, count, index_ref, beam_ref, shift_ref, taps_ref, received_ref, partial_ref, turn_ref, send_ref, ext,
):
    extend_received(received_ref, ext, 0, 5)
    send_parents(
        level, index_ref[0], range(FIRST), (send_ref,), (beam_ref, shift_ref), tap_factors(taps_ref, level), count,
        ext, partial_ref, turn_ref,
    )


def middle_second_kernel(
    level, count, index_ref, beam_ref, shift_ref, taps_ref, received_ref, first_ext, partial_ref, turn_ref, send_ref, ext,
):
    extend_received(received_ref, ext, FIRST, 4)
    copy_extended(first_ext, ext)
    send_parents(
        level, index_ref[0], range(FIRST, count), (send_ref,), (beam_ref, shift_ref), tap_factors(taps_ref, level), count,
        ext, partial_ref, turn_ref,
    )


def place_pair(level, index, m, out_ref, high, low, tables, factors, count, ext, partial_ref, turn_ref):
    lane = lane_iota(HALF)
    even = merged(level, index, 2 * m, 0, HALF, tables, factors, count, ext, partial_ref, turn_ref)
    odd = merged(level, index, 2 * m + 1, 0, HALF, tables, factors, count, ext, partial_ref, turn_ref)
    for part in range(2):
        turned = jnp.concatenate([even[part], odd[part]], axis=0).T
        a = turned[:HALF]
        b = turned[HALF:]
        where = (part,) if high is None else (part, high)
        out_ref[(*where, pl.ds(low, HALF, stride=8))] = jnp.where(lane < HALF, a, pltpu.roll(b, HALF, 1))
        out_ref[(*where, pl.ds(low + 1, HALF, stride=8))] = jnp.where(lane < HALF, pltpu.roll(a, HALF, 1), b)


EARLY = 3


def last_first_kernel(
    level, count, index_ref, beam_ref, shift_ref, taps_ref, received_ref, partial_ref, turn_ref, tiles_ref, ext,
):
    extend_received(received_ref, ext, 0, 5)
    factors = tap_factors(taps_ref, level)
    for m in range(EARLY):
        place_pair(
            level, index_ref[0], m, tiles_ref, None, 2 * m, (beam_ref, shift_ref), factors, count, ext, partial_ref, turn_ref
        )


def last_second_kernel(
    level, count, index_ref, beam_ref, shift_ref, taps_ref, received_ref, first_ext, tiles_ref, partial_ref, turn_ref, out_hbm,
    ext, tiles, sems,
):
    tiles[:, 0] = tiles_ref[...]
    extend_received(received_ref, ext, FIRST, 4)
    copy_extended(first_ext, ext)
    factors = tap_factors(taps_ref, level)
    copies = []
    for m in range(EARLY, partial_ref.shape[0] // 2):
        high, low = m // 4, 2 * (m % 4)
        place_pair(
            level, index_ref[0], m, tiles, high, low, (beam_ref, shift_ref), factors, count, ext, partial_ref, turn_ref
        )
        if low == 6:
            copy = pltpu.make_async_copy(tiles.at[:, high], out_hbm.at[:, high], sems.at[high])
            copy.start()
            copies.append(copy)
    for copy in copies:
        copy.wait()


def params():
    return pltpu.CompilerParams(vmem_limit_bytes=VMEM_LIMIT)


def route(axis, bit):
    count = lax.axis_size(axis)
    return [(i, i ^ (1 << bit)) for i in range(count) if i ^ (1 << bit) < count]


def local(raw_echoes, matched, delays, pulse_phase, beam_map, range_shift, phase_base, phase_rate, tap_offsets):
    pulses, blocks, parts, hop = raw_echoes.shape
    beams = delays.shape[1]
    levels = tap_offsets.shape[0]
    bins = blocks * hop
    slots = beams // 2 + 1
    index = lax.axis_index("pulse").astype(jnp.int32).reshape(1)
    f32, bf16 = jnp.float32, jnp.bfloat16
    image_shape = jax.ShapeDtypeStruct((beams, 2, HALF, LANES), f32)
    rest_shape = jax.ShapeDtypeStruct((beams - slots, 2, HALF, LANES), f32)
    send_shape = jax.ShapeDtypeStruct((slots, 2, HALF, LANES), bf16)
    rows = pulses * blocks
    inputs = (beam_map, range_shift, phase_base, phase_rate, tap_offsets)
    sources = (raw_echoes.reshape(rows * parts, hop), matched, delays, pulse_phase, *inputs)
    send, rest, *tables = pl.pallas_call(
        front_kernel,
        out_shape=(send_shape, rest_shape, *(pltpu.SMEM(x.shape, x.dtype) for x in inputs)),
        in_specs=[SMEM_SPEC] + [HBM_SPEC] * (4 + len(inputs)),
        out_specs=(VMEM_SPEC, VMEM_SPEC, *(SMEM_SPEC for x in inputs)),
        scratch_shapes=[
            pltpu.VMEM((parts * rows, LANES), bf16),
            pltpu.VMEM(matched.shape, f32),
            pltpu.VMEM(pulse_phase.shape, f32),
            pltpu.SMEM(delays.shape, jnp.int32),
            pltpu.VMEM((16 + parts * rows, LANES), f32),
            pltpu.VMEM((2 * LANES, 4 * LANES), bf16),
            pltpu.VMEM((rows, 4 * LANES), bf16),
            pltpu.VMEM((pulses, 2, HALF + 2 * HALO, LANES), f32),
            pltpu.VMEM((2, pulses, beams), f32),
            pltpu.SMEM((2, pulses, beams), f32),
            pltpu.SemaphoreType.DMA((4 + len(inputs) + rows // LANES,)),
        ],
        compiler_params=params(),
        name="front",
    )(index, *(pltpu.with_memory_space_constraint(x, pltpu.HBM) for x in sources))
    beam_table, shift_table, base_table, rate_table, tap_table = tables
    scalars = (index, beam_table, shift_table, tap_table)

    def shape(number, dtype=bf16, rows=HALF):
        return jax.ShapeDtypeStruct((number, 2, rows, LANES), dtype)

    def kernel(function, out_shape, operands, name, scratch=(), out_specs=None, scalar_count=len(scalars)):
        return pl.pallas_call(
            function,
            out_shape=out_shape,
            in_specs=[SMEM_SPEC] * scalar_count + [VMEM_SPEC] * (len(operands) - scalar_count),
            out_specs=jax.tree.map(lambda x: VMEM_SPEC, out_shape) if out_specs is None else out_specs,
            scratch_shapes=list(scratch),
            compiler_params=params(),
            cost_estimate=pl.CostEstimate(flops=2 * 10**6, bytes_accessed=2**20, transcendentals=0),
            name=name,
        )(*operands)

    own_scalars = (index, *tables)
    second = slots - FIRST
    long = HALF + 2 * HALO
    images = (image_shape, image_shape)
    ext_scratch = [pltpu.VMEM((slots, 2, long, LANES), f32)]

    def own(level, *operands):
        return kernel(
            functools.partial(own_kernel, level, bins, slots), images, own_scalars + operands, f"own{level}", ext_scratch,
            scalar_count=len(own_scalars),
        )

    received = lax.ppermute(send, "pulse", route("pulse", 0))
    partial, turn = own(0, send, rest)
    *sends, ext = kernel(
        functools.partial(bottom_kernel, slots),
        (shape(FIRST), shape(second), shape(slots, f32, long)),
        (*scalars, received, partial, turn),
        "bottom",
    )
    for level in range(1, levels):
        received = [lax.ppermute(x, "pulse", route("pulse", level)) for x in sends]
        partial, turn = own(level, *sends, ext, partial, turn)
        if level < levels - 1:
            early, first_ext = kernel(
                functools.partial(middle_first_kernel, level, slots),
                (shape(FIRST), shape(FIRST, f32, long)),
                (*scalars, received[0], partial, turn),
                f"middle{level}first",
            )
            late, ext = kernel(
                functools.partial(middle_second_kernel, level, slots),
                (shape(second), shape(slots, f32, long)),
                (*scalars, received[1], first_ext, partial, turn),
                f"middle{level}second",
            )
            sends = (early, late)
        else:
            tiles = jax.ShapeDtypeStruct((2, HALF * 8, LANES), f32)
            tiles, first_ext = kernel(
                functools.partial(last_first_kernel, level, slots),
                (tiles, shape(FIRST, f32, long)),
                (*scalars, received[0], partial, turn),
                "lastfirst",
            )
            out = kernel(
                functools.partial(last_second_kernel, level, slots),
                jax.ShapeDtypeStruct((2, beams // 8, HALF * 8, LANES), f32),
                (*scalars, received[1], first_ext, tiles, partial, turn),
                "lastsecond",
                ext_scratch
                + [pltpu.VMEM((2, beams // 8, HALF * 8, LANES), f32), pltpu.SemaphoreType.DMA((beams // 8,))],
                HBM_SPEC,
            )
    out = out.reshape(2, beams // 8, HALF, 8, LANES)
    return jnp.transpose(out, (0, 1, 3, 2, 4)).reshape(2, beams, bins)


def shifted(array, axis, by):
    count = lax.axis_size(axis)
    pairs = [(i, i + by) for i in range(count) if 0 <= i + by < count]
    return lax.ppermute(array, axis, pairs)


def padded_2(block, sides, width):
    for axis, dim in sides:
        count = lax.axis_size(axis)
        forward = [(i, i + 1) for i in range(count - 1)]
        backward = [(target, source) for source, target in forward]
        low = lax.ppermute(
            lax.slice_in_dim(block, block.shape[dim] - width, None, axis=dim), axis, forward
        )
        high = lax.ppermute(lax.slice_in_dim(block, 0, width, axis=dim), axis, backward)
        block = jnp.concatenate([low, block, high], axis=dim)
    return block


def from_partner(block, axis, bit):
    count = lax.axis_size(axis)
    route = []
    for low in range(count):
        high = low | 1 << bit
        if high != low and high < count:
            route += [(low, high), (high, low)]
    return lax.ppermute(block, axis, route)


def tables(length):
    counter = jnp.arange(length, dtype=jnp.int32)
    product = counter[:, None] * counter[None, :] % length
    angles = product.astype(jnp.float32) * (2.0 * math.pi / length)
    cosine = jnp.cos(angles)
    sine_part = jnp.sin(angles)
    forward = jnp.concatenate(
        [
            jnp.concatenate([cosine, -sine_part], axis=1),
            jnp.concatenate([sine_part, cosine], axis=1),
        ],
        axis=0,
    )
    inverse = jnp.concatenate(
        [
            jnp.concatenate([cosine, sine_part], axis=1),
            jnp.concatenate([-sine_part, cosine], axis=1),
        ],
        axis=0,
    )
    return (forward, inverse)


def compress(echoes, tail, matched, forward_exact, forward, inverse_kept):
    pulses, blocks, parts, hop_bins = echoes.shape
    length = 2 * hop_bins
    previous = jnp.concatenate([tail[:, None], echoes[:, :-1]], axis=1)
    windows = jnp.concatenate([previous, echoes], axis=3).reshape(pulses * blocks, parts * length)
    taps_padded = jnp.concatenate(
        [matched, jnp.zeros((2, length - hop_bins), jnp.float32)], axis=1
    ).reshape(1, 2 * length)
    response = jnp.dot(taps_padded, forward_exact, precision=lax.Precision.HIGHEST)[0]
    resp_real = response[:length]
    resp_imag = response[length:]
    spectrum = jnp.dot(windows, forward, preferred_element_type=jnp.float32)
    spec_real = spectrum[:, :length]
    spec_imag = spectrum[:, length:]
    filt_real = spec_real * resp_real - spec_imag * resp_imag
    filt_imag = spec_real * resp_imag + spec_imag * resp_real
    shaped = jnp.concatenate([filt_real, filt_imag], axis=1).astype(jnp.bfloat16)
    restored = jnp.dot(shaped, inverse_kept, preferred_element_type=jnp.float32) * (1.0 / length)
    return restored.astype(jnp.bfloat16).reshape(pulses, blocks, parts, hop_bins)


def kept_columns(inverse, length):
    half = length // 2
    return jnp.concatenate([inverse[:, half:length], inverse[:, length + half :]], axis=1)


def inside_mask(first_cell, out_cells, bins):
    global_cells = first_cell + jnp.arange(out_cells, dtype=jnp.int32)
    return ((global_cells >= 0) & (global_cells < bins)).astype(jnp.float32)


def row_slices(rows, starts, width):

    def per_pulse(row, start_row):
        return jax.vmap(lambda start: lax.dynamic_slice_in_dim(row, start, width, 1))(start_row)

    return jax.vmap(per_pulse)(rows, starts)


def project(padded, delay_rows, phase_rows, offset_base, out_cells, first_cell, bins):
    pulses = padded.shape[0]
    beam_count = delay_rows.shape[1]
    group_size = math.gcd(pulses, 4)
    block_count = pulses // group_size

    def accumulate(summed, block_index):
        first_row = block_index * group_size
        pulses_block = lax.dynamic_slice_in_dim(padded, first_row, group_size, 0)
        delay_block = lax.dynamic_slice_in_dim(delay_rows, first_row, group_size, 0)
        phase_block = lax.dynamic_slice_in_dim(phase_rows, first_row, group_size, 0)
        starts = delay_block + offset_base
        gathered = row_slices(pulses_block, starts, out_cells).astype(jnp.float32)
        cosine = jnp.cos(phase_block)[:, :, None]
        sine_part = jnp.sin(phase_block)[:, :, None]
        real_part = gathered[:, :, 0] * cosine - gathered[:, :, 1] * sine_part
        imag_part = gathered[:, :, 0] * sine_part + gathered[:, :, 1] * cosine
        return (summed + jnp.stack([jnp.sum(real_part, axis=0), jnp.sum(imag_part, axis=0)]), None)

    summed, unused = lax.scan(
        accumulate,
        jnp.zeros((2, beam_count, out_cells), jnp.float32),
        jnp.arange(block_count, dtype=jnp.int32),
    )
    return summed * inside_mask(first_cell, out_cells, bins) * (1.0 / math.sqrt(pulses))


def tap_weights(tap_values):
    weights = SPREAD + 1.0 - jnp.abs(tap_values).astype(jnp.float32)
    return weights / jnp.sum(weights)


def merge_side(
    source,
    beam_rows,
    offsets,
    phase_zero,
    phase_slope,
    weights,
    tap_values,
    offset_base,
    out_cells,
    first_cell,
    bins,
):
    span = out_cells + 2 * SPREAD
    starts = offsets + offset_base - SPREAD
    windows = jax.vmap(
        lambda beam, start: lax.dynamic_slice(source, (0, beam, start), (2, 1, span))[:, 0],
        out_axes=1,
    )(beam_rows, starts)
    summed = jnp.zeros((2, beam_rows.shape[0], out_cells), jnp.float32)
    for tap_index in range(tap_values.shape[0]):
        tap_start = tap_values[tap_index] + SPREAD
        summed = summed + weights[tap_index] * lax.dynamic_slice_in_dim(
            windows, tap_start, out_cells, 2
        )
    positions = jnp.arange(out_cells, dtype=jnp.int32)
    global_cells = (first_cell + positions).astype(jnp.float32)
    angle_grid = (
        phase_zero[:, None] + 2.0 * math.pi / bins * phase_slope[:, None] * global_cells[None, :]
    )
    cosine = jnp.cos(angle_grid)
    sine_part = jnp.sin(angle_grid)
    return jnp.stack(
        [summed[0] * cosine - summed[1] * sine_part, summed[0] * sine_part + summed[1] * cosine]
    )


def pick_sides(table, level_index, side_bit):
    half_rows = lax.dynamic_index_in_dim(table[level_index], side_bit, 0, keepdims=False)
    own_rows = lax.dynamic_index_in_dim(half_rows, side_bit, 0, keepdims=False)
    other_rows = lax.dynamic_index_in_dim(half_rows, 1 - side_bit, 0, keepdims=False)
    return (own_rows, other_rows)


def local_split(
    raw_echoes,
    matched,
    delays,
    pulse_phase,
    beam_map,
    range_shift,
    phase_base,
    phase_rate,
    tap_offsets,
):
    pulses = raw_echoes.shape[0]
    hop_bins = raw_echoes.shape[3]
    local_cells = raw_echoes.shape[1] * hop_bins
    bins = local_cells * lax.axis_size("rng")
    length = 2 * hop_bins
    levels = tap_offsets.shape[0]
    forward_exact, inverse_exact = tables(length)
    forward = forward_exact.astype(jnp.bfloat16)
    inverse_kept = kept_columns(inverse_exact.astype(jnp.bfloat16), length)
    tail = shifted(raw_echoes[:, -1], "rng", 1)
    compressed = compress(raw_echoes, tail, matched, forward_exact, forward, inverse_kept)
    compressed = jnp.transpose(compressed, (0, 2, 1, 3)).reshape(pulses, 2, local_cells)
    first_cell = lax.axis_index("rng") * local_cells
    rim_cells = SHIFT + SPREAD
    margin_cells = levels * rim_cells
    padded = padded_2(compressed, (("rng", 2),), SHIFT + margin_cells)
    polar_image = project(
        padded,
        delays,
        pulse_phase,
        SHIFT,
        local_cells + 2 * margin_cells,
        first_cell - margin_cells,
        bins,
    )
    pulse_index = lax.axis_index("pulse")
    for level_index in range(levels):
        side_bit = pulse_index // 2**level_index % 2
        own_beams, other_beams = pick_sides(beam_map, level_index, side_bit)
        own_offsets, other_offsets = pick_sides(range_shift, level_index, side_bit)
        own_zero, other_zero = pick_sides(phase_base, level_index, side_bit)
        own_slope, other_slope = pick_sides(phase_rate, level_index, side_bit)
        tap_values = tap_offsets[level_index]
        weights = tap_weights(tap_values)
        received = from_partner(polar_image, "pulse", level_index)
        own_source = polar_image
        out_margin = max(margin_cells - rim_cells * (level_index + 1), 0)
        out_cells = local_cells + 2 * out_margin
        start_cell = first_cell - out_margin
        own_side = merge_side(
            own_source,
            own_beams,
            own_offsets,
            own_zero,
            own_slope,
            weights,
            tap_values,
            rim_cells,
            out_cells,
            start_cell,
            bins,
        )
        other_side = merge_side(
            received,
            other_beams,
            other_offsets,
            other_zero,
            other_slope,
            weights,
            tap_values,
            rim_cells,
            out_cells,
            start_cell,
            bins,
        )
        polar_image = (own_side + other_side) * SQRT_HALF * inside_mask(start_cell, out_cells, bins)
    return polar_image


def solution(mesh):
    in_specs = (
        P(("grp", "pulse"), "rng", None, None),
        P(),
        P(("grp", "pulse"), None),
        P(("grp", "pulse"), None),
        P(),
        P(),
        P(),
        P(),
        P(),
    )
    out_specs = P(None, ("grp", "pulse"), "rng")
    whole_range = mesh.shape["rng"] == 1
    return jax.shard_map(local if whole_range else local_split, mesh=mesh, in_specs=in_specs, out_specs=out_specs, check_vma=False)
```

```python
import functools
import math

import jax
import jax.numpy as jnp
import numpy as np
from jax import lax
from jax.experimental import pallas as pl
from jax.experimental.pallas import tpu as pltpu
from jax.sharding import PartitionSpec as P

SPREAD = 4
SHIFT = 24
HALO = 32
LANES = 128
HALF = 64
PARTS = {0: (9,), 1: (5, 4), 2: (5, 4), 3: (5, 4)}
SQRT_HALF = 0.7071067811865476
VMEM_LIMIT = 24 * 2**20

COS_COEFFS = (
    1.0,
    -19.73920440673828,
    64.93911743164062,
    -85.45014190673828,
    60.16762924194336,
    -25.967599868774414,
    6.528658390045166,
)
SIN_COEFFS = (
    6.2831854820251465,
    -41.34170150756836,
    81.60513305664062,
    -76.70301818847656,
    42.02592849731445,
    -14.899847030639648,
    3.2381374835968018,
)

SMEM_SPEC = pl.BlockSpec(memory_space=pltpu.SMEM)
VMEM_SPEC = pl.BlockSpec(memory_space=pltpu.VMEM)
HBM_SPEC = pl.BlockSpec(memory_space=pltpu.HBM)


def cos_sin_turns(turns):
    f = turns - jnp.round(turns)
    u = f * f
    c = jnp.full_like(u, COS_COEFFS[-1])
    for a in COS_COEFFS[-2::-1]:
        c = c * u + a
    s = jnp.full_like(u, SIN_COEFFS[-1])
    for a in SIN_COEFFS[-2::-1]:
        s = s * u + a
    return c, s * f


def times(x, y):
    return x[0] * y[0] - x[1] * y[1], x[0] * y[1] + x[1] * y[0]


def lane_iota(rows):
    return lax.broadcasted_iota(jnp.int32, (rows, LANES), 1)


def store_extended(ext_ref, where, body):
    lane = lane_iota(HALO)
    high, low = body[:HALO], body[HALF - HALO :]
    ext_ref[(*where, pl.ds(HALO, HALF))] = body
    after = jnp.where(lane < HALF, pltpu.roll(high, HALF, 1), pltpu.roll(high, HALF - 1, 1))
    ext_ref[(*where, pl.ds(HALO + HALF, HALO))] = jnp.where(lane == LANES - 1, 0.0, after)
    before = jnp.where(lane < HALF, pltpu.roll(low, HALF + 1, 1), pltpu.roll(low, HALF, 1))
    ext_ref[(*where, pl.ds(0, HALO))] = jnp.where(lane == 0, 0.0, before)


def front_kernel(
    index_ref, raw_hbm, matched_hbm, phase_hbm, *rest
):
    tables, rest = rest[:6], rest[6:]
    send_ref, ext, trig, rest = rest[0], rest[1], rest[2], rest[3:]
    copied, rest = rest[:6], rest[6:]
    delays = copied[0]
    raw, matched, phase, raw32, taps, windows, sems = rest
    pulses, beams = phase.shape
    rows = raw.shape[0] // 2
    blocks = rows // pulses
    pairs = rows // LANES
    size = raw.shape[0] // pairs
    side_bit = index_ref[0] % 2

    small = [
        pltpu.make_async_copy(matched_hbm, matched, sems.at[0]),
        pltpu.make_async_copy(phase_hbm, phase, sems.at[1]),
    ]
    small += [
        pltpu.make_async_copy(source, target, sems.at[2 + i]) for i, (source, target) in enumerate(zip(tables, copied))
    ]
    large = [
        pltpu.make_async_copy(
            raw_hbm.at[pl.ds(pair * size, size)], raw.at[pl.ds(pair * size, size)], sems.at[2 + len(tables) + pair]
        )
        for pair in range(pairs)
    ]
    small[1].start()
    small[0].start()
    for copy in large:
        copy.start()
    for copy in small[2:]:
        copy.start()
    small[1].wait()
    scale = 1.0 / math.sqrt(pulses)
    pair_of = cos_sin_turns(phase[...] * (0.5 / math.pi))
    for part in range(2):
        for k in range(beams):
            trig[part, k] = jnp.broadcast_to(pair_of[part][:, k : k + 1] * scale, (pulses, LANES))
    small[0].wait()
    row = lax.broadcasted_iota(jnp.int32, (LANES, LANES), 0)
    column = lax.broadcasted_iota(jnp.int32, (LANES, LANES), 1)
    for part in range(2):
        line = jnp.broadcast_to(matched[part : part + 1, :], (LANES, LANES))
        circulant = pltpu.roll(line, 0, 1, stride=1, stride_axis=0).T
        now = jnp.where(column <= row, circulant, 0.0).astype(jnp.bfloat16)
        before = jnp.where(column > row, circulant, 0.0).astype(jnp.bfloat16)
        if part == 0:
            taps[0:LANES, 0:LANES] = before
            taps[LANES:, LANES : 2 * LANES] = before
            taps[0:LANES, 2 * LANES : 3 * LANES] = now
            taps[LANES:, 3 * LANES :] = now
        else:
            taps[0:LANES, LANES : 2 * LANES] = -before
            taps[LANES:, 0:LANES] = before
            taps[0:LANES, 3 * LANES :] = -now
            taps[LANES:, 2 * LANES : 3 * LANES] = now
    raw32[0:16] = jnp.zeros((16, LANES), jnp.float32)
    first = lax.broadcasted_iota(jnp.int32, (LANES, LANES), 0) % blocks == 0
    lane = lane_iota(HALF)
    for pair in range(pairs):
        large[pair].wait()
        raw32[16 + pair * size : 16 + (pair + 1) * size] = raw[pair * size : (pair + 1) * size, :].astype(jnp.float32)
        mine = slice(pair * LANES, (pair + 1) * LANES)
        for part in range(2):
            previous = raw32[pl.ds(14 + pair * size + part, LANES, stride=2), :]
            windows[mine, part * LANES : (part + 1) * LANES] = jnp.where(first, 0.0, previous).astype(jnp.bfloat16)
            current = raw32[pl.ds(16 + pair * size + part, LANES, stride=2), :]
            windows[mine, (2 + part) * LANES : (3 + part) * LANES] = current.astype(jnp.bfloat16)
    for pair in range(pairs):
        made = lax.dot_general(
            taps[...],
            windows[pair * LANES : (pair + 1) * LANES, :],
            (((1,), (1,)), ((), ())),
            preferred_element_type=jnp.float32,
        )
        for part in range(2):
            a = made[part * LANES : part * LANES + HALF]
            b = made[part * LANES + HALF : (part + 1) * LANES]
            store_extended(ext, (2 * pair, part), jnp.where(lane < HALF, a, pltpu.roll(b, HALF, 1)))
            store_extended(ext, (2 * pair + 1, part), jnp.where(lane < HALF, pltpu.roll(a, HALF, 1), b))
    small[2].wait()
    count = send_ref.shape[0]
    start = order_start(0, index_ref[0] ^ 1)

    def beam(m, carry):
        k = (1 - side_bit) * 7 + slot_at(m, start, count)
        for first_row in range(0, HALF, 32):
            pair = projected(k, first_row, 32, delays, trig, ext)
            for part in range(2):
                send_ref[m, part, pl.ds(first_row, 32)] = pair[part].astype(jnp.bfloat16)
        return carry

    lax.fori_loop(0, count, beam, 0, unroll=3)
    for copy in small[3:]:
        copy.wait()


def projected(k, first_row, rows, delays, trig, ext):
    real = imag = None
    for p in range(ext.shape[0]):
        here = pl.ds(delays[p, k] + (HALO + first_row), rows)
        x = ext[p, 0, here, :]
        y = ext[p, 1, here, :]
        cosine = trig[0, k, pl.ds(p, 1), :]
        sine = trig[1, k, pl.ds(p, 1), :]
        re = x * cosine - y * sine
        im = x * sine + y * cosine
        real = re if real is None else real + re
        imag = im if imag is None else imag + im
    return real, imag


def tap_factors(taps_ref, level):
    count = taps_ref.shape[1]
    offsets = [taps_ref[level, t] for t in range(count)]
    weights = [(SPREAD + 1.0) - jnp.abs(o).astype(jnp.float32) for o in offsets]
    total = weights[0]
    for w in weights[1:]:
        total = total + w
    scale = SQRT_HALF / total
    return offsets, [w * scale for w in weights]


def filtered(ext, slot, start, rows, offsets, weights):
    sums = []
    for part in range(2):
        total = None
        for offset, weight in zip(offsets, weights):
            term = ext[slot, part, pl.ds(start + offset, rows), :] * weight
            total = term if total is None else total + term
        sums.append(total)
    return tuple(sums)


def order_start(level, index):
    if level == 0:
        first_beam = 7 * (1 - ((index >> 1) & 1)) + order_start(1, index ^ 2)
        return jnp.maximum(first_beam // 2 + (index & 1) - 1, 0)
    first, second, third = (index >> 1) & 1, (index >> 2) & 1, (index >> 3) & 1
    if level == 1:
        low = (1 - third) * first
        high = third * (2 + first) + (1 - third) * 4
        return second * low + (1 - second) * high
    if level == 2:
        return (1 - third) * (2 + second)
    return 0


def place_of(slot, start, count):
    place = slot - start
    return jnp.where(place < 0, place + count, place)


def slot_at(place, start, count):
    slot = start + place
    return jnp.where(slot >= count, slot - count, slot)


def merged(level, index, k, at, first_row, rows, tables, factors, count, ext, partial_ref, turn_ref):
    beam_ref, shift_ref = tables
    side_bit = (index >> level) % 2
    other = (level, side_bit, 1 - side_bit, k)
    slot = beam_ref[other] - side_bit * 7
    slot = place_of(slot, order_start(level, index), count)
    start = shift_ref[other] + (HALO + first_row)
    here = pl.ds(first_row, rows)
    real, imag = times(filtered(ext, slot, start, rows, *factors), (turn_ref[at, 0, here], turn_ref[at, 1, here]))
    return real + partial_ref[at, 0, here], imag + partial_ref[at, 1, here]


def turns(base, rate, bins):
    t = lax.broadcasted_iota(jnp.int32, (8, LANES), 0)
    lane = lane_iota(8)
    position = (t + (lane % HALF) * LANES + (lane // HALF) * HALF).astype(jnp.float32) * (1.0 / bins)
    groups = [cos_sin_turns(position * rate + base * (0.5 / math.pi))]
    step = cos_sin_turns(jnp.full((8, LANES), rate * (8.0 / bins)))
    while len(groups) < HALF // 8:
        groups += [times(g, step) for g in groups]
        step = times(step, step)
    return tuple(jnp.concatenate([g[i] for g in groups], axis=0) for i in range(2))


def read_sent(refs, place, part):
    value = None
    first = 0
    for ref in refs:
        size = ref.shape[0]
        here = ref[jnp.clip(place - first, 0, size - 1), part].astype(jnp.float32)
        value = here if value is None else jnp.where(place >= first, here, value)
        first += size
    return value


def bottom_beam(index, rank, count, beams):
    first = (1 - ((index >> 1) & 1)) * 7
    if rank < count:
        return first + slot_at(rank, order_start(1, index ^ 2), count)
    return (first + rank) % beams


def bottom_own_kernel(
    bins, count, first_place, first_rank, index_ref, beam_ref, shift_ref, base_ref, rate_ref, taps_ref, delays, pulse_ext,
    trig, *rest
):
    if first_place > 0:
        copy_extended(rest[0], rest[-1])
        rest = rest[1:]
    partial_ref, turn_ref, ext = rest
    index = index_ref[0]
    side_bit = index % 2
    start = order_start(0, index)
    for place in range(first_place, ext.shape[0]):
        k = side_bit * 7 + slot_at(place, start, count)
        pieces = [projected(k, first_row, 32, delays, trig, pulse_ext) for first_row in range(0, HALF, 32)]
        for part in range(2):
            store_extended(ext, (place, part), jnp.concatenate([x[part] for x in pieces], axis=0))
    factors = tap_factors(taps_ref, 0)
    for at in range(partial_ref.shape[0]):
        k = bottom_beam(index, first_rank + at, count, delays.shape[1])
        own = (0, side_bit, side_bit, k)
        other = (0, side_bit, 1 - side_bit, k)
        slot = place_of(beam_ref[own] - side_bit * 7, start, count)
        turn = turns(base_ref[own], rate_ref[own], bins)
        for first_row in range(0, HALF, 32):
            here = slice(first_row, first_row + 32)
            pair = times(
                filtered(ext, slot, shift_ref[own] + (HALO + first_row), 32, *factors), (turn[0][here], turn[1][here])
            )
            partial_ref[at, 0, here], partial_ref[at, 1, here] = pair
        turn_ref[at, 0], turn_ref[at, 1] = turns(base_ref[other], rate_ref[other], bins)


def own_kernel(level, bins, count, index_ref, beam_ref, shift_ref, base_ref, rate_ref, taps_ref, *rest):
    sent = len(PARTS[level])
    sent_refs, rest = rest[:sent], list(rest[sent:])
    received_ext, last_partial, last_turn = rest[:3]
    rest = rest[3:]
    own_turn = rest.pop(0) if level == 2 else None
    partial_ref = rest.pop(0)
    turn_ref = rest.pop(0) if level != 2 else None
    next_own, next_turn = (rest.pop(0), rest.pop(0)) if level == 1 else (None, None)
    ext = rest.pop(0)
    index = index_ref[0]
    side_bit = (index >> level) % 2
    next_bit = (index >> 2) % 2
    beams = partial_ref.shape[0]
    shared = 2 * count - beams
    low_beam = side_bit * 7
    urgent = (1 - side_bit) * 7

    for i in range(shared):
        place = place_of(7 * side_bit + i, order_start(level, index ^ (1 << level)), count)
        for part in range(2):
            store_extended(ext, (7 * (1 - side_bit) + i, part), read_sent(sent_refs, place, part))
    last_factors = tap_factors(taps_ref, level - 1)

    def remaining(m, carry):
        k = (urgent + m) % beams
        at = m - PARTS[1][0] if level == 1 else k
        pair = merged(
            level - 1, index, k, at, 0, HALF, (beam_ref, shift_ref), last_factors, count, received_ext, last_partial,
            last_turn,
        )
        for part in range(2):
            store_extended(ext, (k - low_beam, part), pair[part])
        return carry

    lax.fori_loop(count, beams, remaining, 0, unroll=7)
    factors = tap_factors(taps_ref, level)

    def beam(k, carry):
        own = (level, side_bit, side_bit, k)
        other = (level, side_bit, 1 - side_bit, k)
        slot = beam_ref[own] - low_beam
        start = shift_ref[own] + HALO
        if own_turn is None:
            turn = turns(base_ref[own], rate_ref[own], bins)
        else:
            turn = own_turn[k, 0], own_turn[k, 1]
        for first_row in range(0, HALF, 32):
            here = slice(first_row, first_row + 32)
            real, imag = times(
                filtered(ext, slot, start + first_row, 32, *factors), (turn[0][here], turn[1][here])
            )
            partial_ref[k, 0, here] = real
            partial_ref[k, 1, here] = imag
        if turn_ref is not None:
            turn_ref[k, 0], turn_ref[k, 1] = turns(base_ref[other], rate_ref[other], bins)
        if next_own is not None:
            for target, side in ((next_own, next_bit), (next_turn, 1 - next_bit)):
                entry = (level + 1, next_bit, side, k)
                target[k, 0], target[k, 1] = turns(base_ref[entry], rate_ref[entry], bins)
        return carry

    lax.fori_loop(0, beams, beam, 0, unroll=2)


def extend_received(received_ref, ext, first, number, source=0):
    for i in range(number):
        for part in range(2):
            store_extended(ext, (first + i, part), received_ref[source + i, part].astype(jnp.float32))


def copy_extended(source, target):
    for slot in range(source.shape[0]):
        target[slot] = source[slot]


def send_parents(level, index, first_place, sends, tables, factors, count, ext, partial_ref, turn_ref, offset=None):
    next_bit = (index >> (level + 1)) % 2
    start = order_start(level + 1, index ^ (2 << level))
    place = first_place
    for target in sends:
        for at in range(target.shape[0]):
            k = (1 - next_bit) * 7 + slot_at(place, start, count)
            row = k if offset is None else place - offset
            for first_row in range(0, HALF, 32):
                pair = merged(level, index, k, row, first_row, 32, tables, factors, count, ext, partial_ref, turn_ref)
                for part in range(2):
                    target[at, part, pl.ds(first_row, 32)] = pair[part].astype(jnp.bfloat16)
            place += 1


def bottom_first_kernel(
    count, index_ref, beam_ref, shift_ref, taps_ref, received_ref, partial_ref, turn_ref, send_ref, ext
):
    extend_received(received_ref, ext, 0, ext.shape[0])
    send_parents(
        0, index_ref[0], 0, (send_ref,), (beam_ref, shift_ref), tap_factors(taps_ref, 0), count, ext, partial_ref,
        turn_ref, 0,
    )


def bottom_second_kernel(
    count, index_ref, beam_ref, shift_ref, taps_ref, received_ref, first_ext, partial_ref, turn_ref, *outs
):
    sends, ext = outs[:-1], outs[-1]
    first = first_ext.shape[0]
    extend_received(received_ref, ext, first, count - first, first)
    copy_extended(first_ext, ext)
    send_parents(
        0, index_ref[0], first, sends, (beam_ref, shift_ref), tap_factors(taps_ref, 0), count, ext, partial_ref,
        turn_ref, first,
    )


def middle_first_kernel(
    level, count, index_ref, beam_ref, shift_ref, taps_ref, received_ref, partial_ref, turn_ref, send_ref, ext,
):
    extend_received(received_ref, ext, 0, received_ref.shape[0])
    send_parents(
        level, index_ref[0], 0, (send_ref,), (beam_ref, shift_ref), tap_factors(taps_ref, level), count,
        ext, partial_ref, turn_ref,
    )


def middle_second_kernel(
    level, count, index_ref, beam_ref, shift_ref, taps_ref, received_ref, first_ext, partial_ref, turn_ref, *outs
):
    sends, ext = outs[:-1], outs[-1]
    extend_received(received_ref, ext, first_ext.shape[0], received_ref.shape[0])
    copy_extended(first_ext, ext)
    send_parents(
        level, index_ref[0], PARTS[level + 1][0], sends, (beam_ref, shift_ref), tap_factors(taps_ref, level), count,
        ext, partial_ref, turn_ref,
    )


def make_pair(level, index, q, tables, factors, count, ext, partial_ref, turn_ref):
    even = merged(level, index, 2 * q, 2 * q, 0, HALF, tables, factors, count, ext, partial_ref, turn_ref)
    odd = merged(level, index, 2 * q + 1, 2 * q + 1, 0, HALF, tables, factors, count, ext, partial_ref, turn_ref)
    return even, odd


def place_pair(even, odd, out_ref, where, low):
    lane = lane_iota(HALF)
    turned = jnp.concatenate([even, odd], axis=0).T
    a = turned[:HALF]
    b = turned[HALF:]
    out_ref[(*where, pl.ds(low, HALF, stride=8))] = jnp.where(lane < HALF, a, pltpu.roll(b, HALF, 1))
    out_ref[(*where, pl.ds(low + 1, HALF, stride=8))] = jnp.where(lane < HALF, pltpu.roll(a, HALF, 1), b)


EARLY = 3


def last_first_kernel(
    level, count, index_ref, beam_ref, shift_ref, taps_ref, received_ref, partial_ref, turn_ref, tiles_ref, ext,
):
    extend_received(received_ref, ext, 0, received_ref.shape[0])
    factors = tap_factors(taps_ref, level)
    for q in range(EARLY):
        even, odd = make_pair(
            level, index_ref[0], q, (beam_ref, shift_ref), factors, count, ext, partial_ref, turn_ref
        )
        for part in range(2):
            place_pair(even[part], odd[part], tiles_ref, (part,), 2 * q)


def last_second_kernel(
    level, count, index_ref, beam_ref, shift_ref, taps_ref, received_ref, first_ext, tiles_ref, partial_ref, turn_ref, out_hbm,
    ext, tiles, sems,
):
    extend_received(received_ref, ext, first_ext.shape[0], received_ref.shape[0])
    copy_extended(first_ext, ext)
    tiles[:, 0] = tiles_ref[...]
    factors = tap_factors(taps_ref, level)
    copies = []
    for q in range(EARLY, partial_ref.shape[0] // 2):
        even, odd = make_pair(
            level, index_ref[0], q, (beam_ref, shift_ref), factors, count, ext, partial_ref, turn_ref
        )
        high, low = q // 4, 2 * (q % 4)
        for part in range(2):
            place_pair(even[part], odd[part], tiles, (part, high), low)
            if low == 6:
                copy = pltpu.make_async_copy(tiles.at[part, high], out_hbm.at[part, high], sems.at[part, high])
                copy.start()
                copies.append(copy)
    for copy in copies:
        copy.wait()


def params():
    return pltpu.CompilerParams(vmem_limit_bytes=VMEM_LIMIT)


def route(axis, bit):
    count = lax.axis_size(axis)
    return [(i, i ^ (1 << bit)) for i in range(count) if i ^ (1 << bit) < count]


def local(raw_echoes, matched, delays, pulse_phase, beam_map, range_shift, phase_base, phase_rate, tap_offsets):
    pulses, blocks, parts, hop = raw_echoes.shape
    beams = delays.shape[1]
    levels = tap_offsets.shape[0]
    bins = blocks * hop
    slots = beams // 2 + 1
    index = lax.axis_index("pulse").astype(jnp.int32).reshape(1)
    f32, bf16 = jnp.float32, jnp.bfloat16
    image_shape = jax.ShapeDtypeStruct((beams, 2, HALF, LANES), f32)
    send_shape = jax.ShapeDtypeStruct((slots, 2, HALF, LANES), bf16)
    rows = pulses * blocks
    inputs = (delays, beam_map, range_shift, phase_base, phase_rate, tap_offsets)
    sources = (raw_echoes.reshape(rows * parts, hop), matched, pulse_phase, *inputs)
    pulse_shape = jax.ShapeDtypeStruct((pulses, 2, HALF + 2 * HALO, LANES), f32)
    trig_shape = jax.ShapeDtypeStruct((2, beams, pulses, LANES), f32)
    send, pulse_ext, trig, delay_table, *tables = pl.pallas_call(
        front_kernel,
        out_shape=(send_shape, pulse_shape, trig_shape, *(pltpu.SMEM(x.shape, x.dtype) for x in inputs)),
        in_specs=[SMEM_SPEC] + [HBM_SPEC] * len(sources),
        out_specs=(VMEM_SPEC, VMEM_SPEC, VMEM_SPEC, *(SMEM_SPEC for x in inputs)),
        scratch_shapes=[
            pltpu.VMEM((parts * rows, LANES), bf16),
            pltpu.VMEM(matched.shape, f32),
            pltpu.VMEM(pulse_phase.shape, f32),
            pltpu.VMEM((16 + parts * rows, LANES), f32),
            pltpu.VMEM((2 * LANES, 4 * LANES), bf16),
            pltpu.VMEM((rows, 4 * LANES), bf16),
            pltpu.SemaphoreType.DMA((2 + len(inputs) + rows // LANES,)),
        ],
        compiler_params=params(),
        name="front",
    )(index, *(pltpu.with_memory_space_constraint(x, pltpu.HBM) for x in sources))
    beam_table, shift_table, base_table, rate_table, tap_table = tables
    scalars = (index, beam_table, shift_table, tap_table)

    def shape(number, dtype=bf16, rows=HALF):
        return jax.ShapeDtypeStruct((number, 2, rows, LANES), dtype)

    def kernel(function, out_shape, operands, name, scratch=(), out_specs=None, scalar_count=len(scalars)):
        return pl.pallas_call(
            function,
            out_shape=out_shape,
            in_specs=[SMEM_SPEC] * scalar_count + [VMEM_SPEC] * (len(operands) - scalar_count),
            out_specs=jax.tree.map(lambda x: VMEM_SPEC, out_shape) if out_specs is None else out_specs,
            scratch_shapes=list(scratch),
            compiler_params=params(),
            cost_estimate=pl.CostEstimate(flops=2 * 10**6, bytes_accessed=2**20, transcendentals=0),
            name=name,
        )(*operands)

    own_scalars = (index, *tables)
    long = HALF + 2 * HALO
    ext_scratch = [pltpu.VMEM((slots, 2, long, LANES), f32)]

    def own(level, outs, *operands):
        return kernel(
            functools.partial(own_kernel, level, bins, slots), (image_shape,) * outs, own_scalars + operands, f"own{level}",
            ext_scratch, scalar_count=len(own_scalars),
        )

    received = lax.ppermute(send, "pulse", route("pulse", 0))
    first, later = PARTS[1]
    bottom_scalars = (*own_scalars, delay_table)
    partial, turn, own_ext = kernel(
        functools.partial(bottom_own_kernel, bins, slots, 0, 0),
        (shape(first, f32), shape(first, f32), shape(first, f32, long)),
        (*bottom_scalars, pulse_ext, trig),
        "bottomownfirst",
        scalar_count=len(bottom_scalars),
    )
    early, first_ext = kernel(
        functools.partial(bottom_first_kernel, slots),
        (shape(first), shape(first, f32, long)),
        (*scalars, received, partial, turn),
        "bottomfirst",
    )
    partial, turn = kernel(
        functools.partial(bottom_own_kernel, bins, slots, first, first),
        (shape(beams - first, f32), shape(beams - first, f32)),
        (*bottom_scalars, pulse_ext, trig, own_ext),
        "bottomownsecond",
        ext_scratch,
        scalar_count=len(bottom_scalars),
    )
    late, ext = kernel(
        functools.partial(bottom_second_kernel, slots),
        (shape(later), shape(slots, f32, long)),
        (*scalars, received, first_ext, partial, turn),
        "bottomsecond",
    )
    sends = (early, late)
    for level in range(1, levels):
        received = [lax.ppermute(x, "pulse", route("pulse", level)) for x in sends]
        if level == 1:
            partial, turn, own_turn, next_turn = own(level, 4, *sends, ext, partial, turn)
        elif level == 2:
            (partial,) = own(level, 1, *sends, ext, partial, turn, own_turn)
            turn = next_turn
        else:
            partial, turn = own(level, 2, *sends, ext, partial, turn)
        if level < levels - 1:
            following = PARTS[level + 1]
            early, first_ext = kernel(
                functools.partial(middle_first_kernel, level, slots),
                (shape(following[0]), shape(PARTS[level][0], f32, long)),
                (*scalars, received[0], partial, turn),
                f"middle{level}first",
            )
            *late, ext = kernel(
                functools.partial(middle_second_kernel, level, slots),
                (*(shape(n) for n in following[1:]), shape(slots, f32, long)),
                (*scalars, received[1], first_ext, partial, turn),
                f"middle{level}second",
            )
            sends = (early, *late)
        else:
            tiles = jax.ShapeDtypeStruct((2, HALF * 8, LANES), f32)
            tiles, first_ext = kernel(
                functools.partial(last_first_kernel, level, slots),
                (tiles, shape(PARTS[level][0], f32, long)),
                (*scalars, received[0], partial, turn),
                "lastfirst",
            )
            out = kernel(
                functools.partial(last_second_kernel, level, slots),
                jax.ShapeDtypeStruct((2, beams // 8, HALF * 8, LANES), f32),
                (*scalars, received[1], first_ext, tiles, partial, turn),
                "lastsecond",
                ext_scratch
                + [pltpu.VMEM((2, beams // 8, HALF * 8, LANES), f32), pltpu.SemaphoreType.DMA((2, beams // 8))],
                HBM_SPEC,
            )
    out = out.reshape(2, beams // 8, HALF, 8, LANES)
    return jnp.transpose(out, (0, 1, 3, 2, 4)).reshape(2, beams, bins)


def shifted(array, axis, by):
    count = lax.axis_size(axis)
    pairs = [(i, i + by) for i in range(count) if 0 <= i + by < count]
    return lax.ppermute(array, axis, pairs)


def padded_2(block, sides, width):
    for axis, dim in sides:
        count = lax.axis_size(axis)
        forward = [(i, i + 1) for i in range(count - 1)]
        backward = [(target, source) for source, target in forward]
        low = lax.ppermute(
            lax.slice_in_dim(block, block.shape[dim] - width, None, axis=dim), axis, forward
        )
        high = lax.ppermute(lax.slice_in_dim(block, 0, width, axis=dim), axis, backward)
        block = jnp.concatenate([low, block, high], axis=dim)
    return block


def from_partner(block, axis, bit):
    count = lax.axis_size(axis)
    route = []
    for low in range(count):
        high = low | 1 << bit
        if high != low and high < count:
            route += [(low, high), (high, low)]
    return lax.ppermute(block, axis, route)


def tables(length):
    counter = jnp.arange(length, dtype=jnp.int32)
    product = counter[:, None] * counter[None, :] % length
    angles = product.astype(jnp.float32) * (2.0 * math.pi / length)
    cosine = jnp.cos(angles)
    sine_part = jnp.sin(angles)
    forward = jnp.concatenate(
        [
            jnp.concatenate([cosine, -sine_part], axis=1),
            jnp.concatenate([sine_part, cosine], axis=1),
        ],
        axis=0,
    )
    inverse = jnp.concatenate(
        [
            jnp.concatenate([cosine, sine_part], axis=1),
            jnp.concatenate([-sine_part, cosine], axis=1),
        ],
        axis=0,
    )
    return (forward, inverse)


def compress(echoes, tail, matched, forward_exact, forward, inverse_kept):
    pulses, blocks, parts, hop_bins = echoes.shape
    length = 2 * hop_bins
    previous = jnp.concatenate([tail[:, None], echoes[:, :-1]], axis=1)
    windows = jnp.concatenate([previous, echoes], axis=3).reshape(pulses * blocks, parts * length)
    taps_padded = jnp.concatenate(
        [matched, jnp.zeros((2, length - hop_bins), jnp.float32)], axis=1
    ).reshape(1, 2 * length)
    response = jnp.dot(taps_padded, forward_exact, precision=lax.Precision.HIGHEST)[0]
    resp_real = response[:length]
    resp_imag = response[length:]
    spectrum = jnp.dot(windows, forward, preferred_element_type=jnp.float32)
    spec_real = spectrum[:, :length]
    spec_imag = spectrum[:, length:]
    filt_real = spec_real * resp_real - spec_imag * resp_imag
    filt_imag = spec_real * resp_imag + spec_imag * resp_real
    shaped = jnp.concatenate([filt_real, filt_imag], axis=1).astype(jnp.bfloat16)
    restored = jnp.dot(shaped, inverse_kept, preferred_element_type=jnp.float32) * (1.0 / length)
    return restored.astype(jnp.bfloat16).reshape(pulses, blocks, parts, hop_bins)


def kept_columns(inverse, length):
    half = length // 2
    return jnp.concatenate([inverse[:, half:length], inverse[:, length + half :]], axis=1)


def inside_mask(first_cell, out_cells, bins):
    global_cells = first_cell + jnp.arange(out_cells, dtype=jnp.int32)
    return ((global_cells >= 0) & (global_cells < bins)).astype(jnp.float32)


def row_slices(rows, starts, width):

    def per_pulse(row, start_row):
        return jax.vmap(lambda start: lax.dynamic_slice_in_dim(row, start, width, 1))(start_row)

    return jax.vmap(per_pulse)(rows, starts)


def project(padded, delay_rows, phase_rows, offset_base, out_cells, first_cell, bins):
    pulses = padded.shape[0]
    beam_count = delay_rows.shape[1]
    group_size = math.gcd(pulses, 4)
    block_count = pulses // group_size

    def accumulate(summed, block_index):
        first_row = block_index * group_size
        pulses_block = lax.dynamic_slice_in_dim(padded, first_row, group_size, 0)
        delay_block = lax.dynamic_slice_in_dim(delay_rows, first_row, group_size, 0)
        phase_block = lax.dynamic_slice_in_dim(phase_rows, first_row, group_size, 0)
        starts = delay_block + offset_base
        gathered = row_slices(pulses_block, starts, out_cells).astype(jnp.float32)
        cosine = jnp.cos(phase_block)[:, :, None]
        sine_part = jnp.sin(phase_block)[:, :, None]
        real_part = gathered[:, :, 0] * cosine - gathered[:, :, 1] * sine_part
        imag_part = gathered[:, :, 0] * sine_part + gathered[:, :, 1] * cosine
        return (summed + jnp.stack([jnp.sum(real_part, axis=0), jnp.sum(imag_part, axis=0)]), None)

    summed, unused = lax.scan(
        accumulate,
        jnp.zeros((2, beam_count, out_cells), jnp.float32),
        jnp.arange(block_count, dtype=jnp.int32),
    )
    return summed * inside_mask(first_cell, out_cells, bins) * (1.0 / math.sqrt(pulses))


def tap_weights(tap_values):
    weights = SPREAD + 1.0 - jnp.abs(tap_values).astype(jnp.float32)
    return weights / jnp.sum(weights)


def merge_side(
    source,
    beam_rows,
    offsets,
    phase_zero,
    phase_slope,
    weights,
    tap_values,
    offset_base,
    out_cells,
    first_cell,
    bins,
):
    span = out_cells + 2 * SPREAD
    starts = offsets + offset_base - SPREAD
    windows = jax.vmap(
        lambda beam, start: lax.dynamic_slice(source, (0, beam, start), (2, 1, span))[:, 0],
        out_axes=1,
    )(beam_rows, starts)
    summed = jnp.zeros((2, beam_rows.shape[0], out_cells), jnp.float32)
    for tap_index in range(tap_values.shape[0]):
        tap_start = tap_values[tap_index] + SPREAD
        summed = summed + weights[tap_index] * lax.dynamic_slice_in_dim(
            windows, tap_start, out_cells, 2
        )
    positions = jnp.arange(out_cells, dtype=jnp.int32)
    global_cells = (first_cell + positions).astype(jnp.float32)
    angle_grid = (
        phase_zero[:, None] + 2.0 * math.pi / bins * phase_slope[:, None] * global_cells[None, :]
    )
    cosine = jnp.cos(angle_grid)
    sine_part = jnp.sin(angle_grid)
    return jnp.stack(
        [summed[0] * cosine - summed[1] * sine_part, summed[0] * sine_part + summed[1] * cosine]
    )


def pick_sides(table, level_index, side_bit):
    half_rows = lax.dynamic_index_in_dim(table[level_index], side_bit, 0, keepdims=False)
    own_rows = lax.dynamic_index_in_dim(half_rows, side_bit, 0, keepdims=False)
    other_rows = lax.dynamic_index_in_dim(half_rows, 1 - side_bit, 0, keepdims=False)
    return (own_rows, other_rows)


def local_split(
    raw_echoes,
    matched,
    delays,
    pulse_phase,
    beam_map,
    range_shift,
    phase_base,
    phase_rate,
    tap_offsets,
):
    pulses = raw_echoes.shape[0]
    hop_bins = raw_echoes.shape[3]
    local_cells = raw_echoes.shape[1] * hop_bins
    bins = local_cells * lax.axis_size("rng")
    length = 2 * hop_bins
    levels = tap_offsets.shape[0]
    forward_exact, inverse_exact = tables(length)
    forward = forward_exact.astype(jnp.bfloat16)
    inverse_kept = kept_columns(inverse_exact.astype(jnp.bfloat16), length)
    tail = shifted(raw_echoes[:, -1], "rng", 1)
    compressed = compress(raw_echoes, tail, matched, forward_exact, forward, inverse_kept)
    compressed = jnp.transpose(compressed, (0, 2, 1, 3)).reshape(pulses, 2, local_cells)
    first_cell = lax.axis_index("rng") * local_cells
    rim_cells = SHIFT + SPREAD
    margin_cells = levels * rim_cells
    padded = padded_2(compressed, (("rng", 2),), SHIFT + margin_cells)
    polar_image = project(
        padded,
        delays,
        pulse_phase,
        SHIFT,
        local_cells + 2 * margin_cells,
        first_cell - margin_cells,
        bins,
    )
    pulse_index = lax.axis_index("pulse")
    for level_index in range(levels):
        side_bit = pulse_index // 2**level_index % 2
        own_beams, other_beams = pick_sides(beam_map, level_index, side_bit)
        own_offsets, other_offsets = pick_sides(range_shift, level_index, side_bit)
        own_zero, other_zero = pick_sides(phase_base, level_index, side_bit)
        own_slope, other_slope = pick_sides(phase_rate, level_index, side_bit)
        tap_values = tap_offsets[level_index]
        weights = tap_weights(tap_values)
        received = from_partner(polar_image, "pulse", level_index)
        own_source = polar_image
        out_margin = max(margin_cells - rim_cells * (level_index + 1), 0)
        out_cells = local_cells + 2 * out_margin
        start_cell = first_cell - out_margin
        own_side = merge_side(
            own_source,
            own_beams,
            own_offsets,
            own_zero,
            own_slope,
            weights,
            tap_values,
            rim_cells,
            out_cells,
            start_cell,
            bins,
        )
        other_side = merge_side(
            received,
            other_beams,
            other_offsets,
            other_zero,
            other_slope,
            weights,
            tap_values,
            rim_cells,
            out_cells,
            start_cell,
            bins,
        )
        polar_image = (own_side + other_side) * SQRT_HALF * inside_mask(start_cell, out_cells, bins)
    return polar_image


def solution(mesh):
    in_specs = (
        P(("grp", "pulse"), "rng", None, None),
        P(),
        P(("grp", "pulse"), None),
        P(("grp", "pulse"), None),
        P(),
        P(),
        P(),
        P(),
        P(),
    )
    out_specs = P(None, ("grp", "pulse"), "rng")
    whole_range = mesh.shape["rng"] == 1
    return jax.shard_map(local if whole_range else local_split, mesh=mesh, in_specs=in_specs, out_specs=out_specs, check_vma=False)
```

```python
import functools
import math

import jax
import jax.numpy as jnp
import numpy as np
from jax import lax
from jax.experimental import pallas as pl
from jax.experimental.pallas import tpu as pltpu
from jax.sharding import PartitionSpec as P

SPREAD = 4
SHIFT = 24
HALO = 32
LANES = 128
HALF = 64
PARTS = {0: (5, 4), 1: (5, 4), 2: (5, 4), 3: (5, 4)}
SQRT_HALF = 0.7071067811865476
VMEM_LIMIT = 24 * 2**20

COS_COEFFS = (
    1.0,
    -19.73920440673828,
    64.93911743164062,
    -85.45014190673828,
    60.16762924194336,
    -25.967599868774414,
    6.528658390045166,
)
SIN_COEFFS = (
    6.2831854820251465,
    -41.34170150756836,
    81.60513305664062,
    -76.70301818847656,
    42.02592849731445,
    -14.899847030639648,
    3.2381374835968018,
)

SMEM_SPEC = pl.BlockSpec(memory_space=pltpu.SMEM)
VMEM_SPEC = pl.BlockSpec(memory_space=pltpu.VMEM)
COSTS = {
    "bottomownfirst": 800,
    "bottomfirst": 300,
    "bottomownsecond": 1050,
    "bottomsecond": 270,
    "own1": 1500,
    "frontsecond": 350,
    "turns2": 500,
    "middle1first": 310,
    "own2first": 600,
    "middle1second": 180,
    "middle2first": 320,
    "own2second": 640,
    "middle2second": 260,
    "own3": 1470,
    "lastfirst": 570,
    "lastsecond": 1550,
}
COSTS = {name: 1000 * cost for name, cost in COSTS.items()}

HBM_SPEC = pl.BlockSpec(memory_space=pltpu.HBM)


def cos_sin_turns(turns):
    f = turns - jnp.round(turns)
    u = f * f
    c = jnp.full_like(u, COS_COEFFS[-1])
    for a in COS_COEFFS[-2::-1]:
        c = c * u + a
    s = jnp.full_like(u, SIN_COEFFS[-1])
    for a in SIN_COEFFS[-2::-1]:
        s = s * u + a
    return c, s * f


def times(x, y):
    return x[0] * y[0] - x[1] * y[1], x[0] * y[1] + x[1] * y[0]


def lane_iota(rows):
    return lax.broadcasted_iota(jnp.int32, (rows, LANES), 1)


def store_extended(ext_ref, where, body):
    lane = lane_iota(HALO)
    high, low = body[:HALO], body[HALF - HALO :]
    ext_ref[(*where, pl.ds(HALO, HALF))] = body
    after = jnp.where(lane < HALF, pltpu.roll(high, HALF, 1), pltpu.roll(high, HALF - 1, 1))
    ext_ref[(*where, pl.ds(HALO + HALF, HALO))] = jnp.where(lane == LANES - 1, 0.0, after)
    before = jnp.where(lane < HALF, pltpu.roll(low, HALF + 1, 1), pltpu.roll(low, HALF, 1))
    ext_ref[(*where, pl.ds(0, HALO))] = jnp.where(lane == 0, 0.0, before)


def front_kernel(
    index_ref, raw_hbm, matched_hbm, phase_hbm, *rest
):
    tables, rest = rest[:6], rest[6:]
    send_ref, ext, trig, rest = rest[0], rest[1], rest[2], rest[3:]
    copied, rest = rest[:6], rest[6:]
    delays = copied[0]
    raw, matched, phase, raw32, taps, windows, sems = rest
    pulses, beams = phase.shape
    rows = raw.shape[0] // 2
    blocks = rows // pulses
    pairs = rows // LANES
    size = raw.shape[0] // pairs

    small = [
        pltpu.make_async_copy(matched_hbm, matched, sems.at[0]),
        pltpu.make_async_copy(phase_hbm, phase, sems.at[1]),
    ]
    small += [
        pltpu.make_async_copy(source, target, sems.at[2 + i]) for i, (source, target) in enumerate(zip(tables, copied))
    ]
    large = [
        pltpu.make_async_copy(
            raw_hbm.at[pl.ds(pair * size, size)], raw.at[pl.ds(pair * size, size)], sems.at[2 + len(tables) + pair]
        )
        for pair in range(pairs)
    ]
    for copy in large[:1] + small[:2] + large[1:] + small[2:]:
        copy.start()
    raw32[0:16] = jnp.zeros((16, LANES), jnp.float32)
    for copy in small[:2] + large:
        copy.wait()
    scale = 1.0 / math.sqrt(pulses)
    pair_of = cos_sin_turns(phase[...] * (0.5 / math.pi))
    for part in range(2):
        for k in range(beams):
            trig[part, k] = jnp.broadcast_to(pair_of[part][:, k : k + 1] * scale, (pulses, LANES))
    row = lax.broadcasted_iota(jnp.int32, (LANES, LANES), 0)
    column = lax.broadcasted_iota(jnp.int32, (LANES, LANES), 1)
    for part in range(2):
        line = jnp.broadcast_to(matched[part : part + 1, :], (LANES, LANES))
        circulant = pltpu.roll(line, 0, 1, stride=1, stride_axis=0).T
        now = jnp.where(column <= row, circulant, 0.0).astype(jnp.bfloat16)
        before = jnp.where(column > row, circulant, 0.0).astype(jnp.bfloat16)
        if part == 0:
            taps[0:LANES, 0:LANES] = before
            taps[LANES:, LANES : 2 * LANES] = before
            taps[0:LANES, 2 * LANES : 3 * LANES] = now
            taps[LANES:, 3 * LANES :] = now
        else:
            taps[0:LANES, LANES : 2 * LANES] = -before
            taps[LANES:, 0:LANES] = before
            taps[0:LANES, 3 * LANES :] = -now
            taps[LANES:, 2 * LANES : 3 * LANES] = now
    first = lax.broadcasted_iota(jnp.int32, (LANES, LANES), 0) % blocks == 0
    lane = lane_iota(HALF)
    for pair in range(pairs):
        raw32[16 + pair * size : 16 + (pair + 1) * size] = raw[pair * size : (pair + 1) * size, :].astype(jnp.float32)
        mine = slice(pair * LANES, (pair + 1) * LANES)
        for part in range(2):
            previous = raw32[pl.ds(14 + pair * size + part, LANES, stride=2), :]
            windows[mine, part * LANES : (part + 1) * LANES] = jnp.where(first, 0.0, previous).astype(jnp.bfloat16)
            current = raw32[pl.ds(16 + pair * size + part, LANES, stride=2), :]
            windows[mine, (2 + part) * LANES : (3 + part) * LANES] = current.astype(jnp.bfloat16)
    for pair in range(pairs):
        made = lax.dot_general(
            taps[...],
            windows[pair * LANES : (pair + 1) * LANES, :],
            (((1,), (1,)), ((), ())),
            preferred_element_type=jnp.float32,
        )
        for part in range(2):
            a = made[part * LANES : part * LANES + HALF]
            b = made[part * LANES + HALF : (part + 1) * LANES]
            store_extended(ext, (2 * pair, part), jnp.where(lane < HALF, a, pltpu.roll(b, HALF, 1)))
            store_extended(ext, (2 * pair + 1, part), jnp.where(lane < HALF, pltpu.roll(a, HALF, 1), b))
    small[2].wait()
    send_pulses(index_ref[0], 0, send_ref, delays, trig, ext)
    for copy in small[3:]:
        copy.wait()


def send_pulses(index, first_place, send_ref, delays, trig, ext):
    count = sum(PARTS[0])
    start = order_start(0, index ^ 1)
    for at in range(send_ref.shape[0]):
        k = (1 - index % 2) * 7 + slot_at(first_place + at, start, count)
        for first_row in range(0, HALF, 32):
            pair = projected(k, first_row, 32, delays, trig, ext)
            for part in range(2):
                send_ref[at, part, pl.ds(first_row, 32)] = pair[part].astype(jnp.bfloat16)


def front_second_kernel(index_ref, delays, pulse_ext, trig, after_ref, send_ref):
    send_pulses(index_ref[0], PARTS[0][0], send_ref, delays, trig, pulse_ext)


def projected(k, first_row, rows, delays, trig, ext):
    real = imag = None
    for p in range(ext.shape[0]):
        here = pl.ds(delays[p, k] + (HALO + first_row), rows)
        x = ext[p, 0, here, :]
        y = ext[p, 1, here, :]
        cosine = trig[0, k, pl.ds(p, 1), :]
        sine = trig[1, k, pl.ds(p, 1), :]
        re = x * cosine - y * sine
        im = x * sine + y * cosine
        real = re if real is None else real + re
        imag = im if imag is None else imag + im
    return real, imag


def tap_factors(taps_ref, level):
    count = taps_ref.shape[1]
    offsets = [taps_ref[level, t] for t in range(count)]
    weights = [(SPREAD + 1.0) - jnp.abs(o).astype(jnp.float32) for o in offsets]
    total = weights[0]
    for w in weights[1:]:
        total = total + w
    scale = SQRT_HALF / total
    return offsets, [w * scale for w in weights]


def filtered(ext, slot, start, rows, offsets, weights):
    sums = []
    for part in range(2):
        total = None
        for offset, weight in zip(offsets, weights):
            term = ext[slot, part, pl.ds(start + offset, rows), :] * weight
            total = term if total is None else total + term
        sums.append(total)
    return tuple(sums)


def order_start(level, index):
    if level == 0:
        first_beam = 7 * (1 - ((index >> 1) & 1)) + order_start(1, index ^ 2)
        return jnp.maximum(first_beam // 2 + (index & 1) - 1, 0)
    first, second, third = (index >> 1) & 1, (index >> 2) & 1, (index >> 3) & 1
    if level == 1:
        low = (1 - third) * first
        high = third * (2 + first) + (1 - third) * 4
        return second * low + (1 - second) * high
    if level == 2:
        return (1 - third) * (2 + second)
    return 0


def place_of(slot, start, count):
    place = slot - start
    return jnp.where(place < 0, place + count, place)


def slot_at(place, start, count):
    slot = start + place
    return jnp.where(slot >= count, slot - count, slot)


def merged(level, index, k, at, first_row, rows, tables, factors, count, ext, partial_ref, turn_ref):
    beam_ref, shift_ref = tables
    side_bit = (index >> level) % 2
    other = (level, side_bit, 1 - side_bit, k)
    slot = beam_ref[other] - side_bit * 7
    slot = place_of(slot, order_start(level, index), count)
    start = shift_ref[other] + (HALO + first_row)
    here = pl.ds(first_row, rows)
    real, imag = times(filtered(ext, slot, start, rows, *factors), (turn_ref[at, 0, here], turn_ref[at, 1, here]))
    return real + partial_ref[at, 0, here], imag + partial_ref[at, 1, here]


def turns(base, rate, bins):
    t = lax.broadcasted_iota(jnp.int32, (8, LANES), 0)
    lane = lane_iota(8)
    position = (t + (lane % HALF) * LANES + (lane // HALF) * HALF).astype(jnp.float32) * (1.0 / bins)
    groups = [cos_sin_turns(position * rate + base * (0.5 / math.pi))]
    step = cos_sin_turns(jnp.full((8, LANES), rate * (8.0 / bins)))
    while len(groups) < HALF // 8:
        groups += [times(g, step) for g in groups]
        step = times(step, step)
    return tuple(jnp.concatenate([g[i] for g in groups], axis=0) for i in range(2))


def read_sent(refs, place, part):
    value = None
    first = 0
    for ref in refs:
        size = ref.shape[0]
        here = ref[jnp.clip(place - first, 0, size - 1), part].astype(jnp.float32)
        value = here if value is None else jnp.where(place >= first, here, value)
        first += size
    return value


def rank_beam(level, index, rank, count, beams):
    first = (1 - ((index >> (level + 1)) & 1)) * 7
    if rank < count:
        return first + slot_at(rank, order_start(level + 1, index ^ (2 << level)), count)
    return (first + rank) % beams


def bottom_own_kernel(
    bins, count, first_place, first_rank, index_ref, beam_ref, shift_ref, base_ref, rate_ref, taps_ref, delays, pulse_ext,
    trig, *rest
):
    if first_place > 0:
        copy_extended(rest[0], rest[-1])
        rest = rest[1:]
    partial_ref, turn_ref, ext = rest
    index = index_ref[0]
    side_bit = index % 2
    start = order_start(0, index)
    for place in range(first_place, ext.shape[0]):
        k = side_bit * 7 + slot_at(place, start, count)
        pieces = [projected(k, first_row, 32, delays, trig, pulse_ext) for first_row in range(0, HALF, 32)]
        for part in range(2):
            store_extended(ext, (place, part), jnp.concatenate([x[part] for x in pieces], axis=0))
    factors = tap_factors(taps_ref, 0)
    for at in range(partial_ref.shape[0]):
        k = rank_beam(0, index, first_rank + at, count, delays.shape[1])
        own = (0, side_bit, side_bit, k)
        other = (0, side_bit, 1 - side_bit, k)
        slot = place_of(beam_ref[own] - side_bit * 7, start, count)
        turn = turns(base_ref[own], rate_ref[own], bins)
        for first_row in range(0, HALF, 32):
            here = slice(first_row, first_row + 32)
            pair = times(
                filtered(ext, slot, shift_ref[own] + (HALO + first_row), 32, *factors), (turn[0][here], turn[1][here])
            )
            partial_ref[at, 0, here], partial_ref[at, 1, here] = pair
        turn_ref[at, 0], turn_ref[at, 1] = turns(base_ref[other], rate_ref[other], bins)


def own_kernel(level, bins, count, index_ref, beam_ref, shift_ref, base_ref, rate_ref, taps_ref, *rest):
    sent = len(PARTS[level])
    sent_refs, rest = rest[:sent], list(rest[sent:])
    received_ext, last_partial, last_turn = rest[:3]
    rest = rest[3:]
    partial_ref = rest.pop(0)
    turn_ref = rest.pop(0)
    ext = rest.pop(0)
    index = index_ref[0]
    side_bit = (index >> level) % 2
    beams = partial_ref.shape[0]
    shared = 2 * count - beams
    low_beam = side_bit * 7
    urgent = (1 - side_bit) * 7

    for i in range(shared):
        place = place_of(7 * side_bit + i, order_start(level, index ^ (1 << level)), count)
        for part in range(2):
            store_extended(ext, (7 * (1 - side_bit) + i, part), read_sent(sent_refs, place, part))
    last_factors = tap_factors(taps_ref, level - 1)

    def remaining(m, carry):
        k = (urgent + m) % beams
        at = m - PARTS[1][0] if level == 1 else m
        pair = merged(
            level - 1, index, k, at, 0, HALF, (beam_ref, shift_ref), last_factors, count, received_ext, last_partial,
            last_turn,
        )
        for part in range(2):
            store_extended(ext, (k - low_beam, part), pair[part])
        return carry

    lax.fori_loop(count, beams, remaining, 0, unroll=7)
    factors = tap_factors(taps_ref, level)

    def beam(k, carry):
        own = (level, side_bit, side_bit, k)
        other = (level, side_bit, 1 - side_bit, k)
        slot = beam_ref[own] - low_beam
        start = shift_ref[own] + HALO
        turn = turns(base_ref[own], rate_ref[own], bins)
        for first_row in range(0, HALF, 32):
            here = slice(first_row, first_row + 32)
            real, imag = times(
                filtered(ext, slot, start + first_row, 32, *factors), (turn[0][here], turn[1][here])
            )
            partial_ref[k, 0, here] = real
            partial_ref[k, 1, here] = imag
        turn_ref[k, 0], turn_ref[k, 1] = turns(base_ref[other], rate_ref[other], bins)
        return carry

    lax.fori_loop(0, beams, beam, 0, unroll=2)


def turns_kernel(level, bins, index_ref, base_ref, rate_ref, after_ref, own_ref, other_ref):
    index = index_ref[0]
    side_bit = (index >> level) % 2
    beams = own_ref.shape[0]

    def beam(rank, carry):
        k = ((1 - ((index >> (level + 1)) & 1)) * 7 + rank) % beams
        for target, side in ((own_ref, side_bit), (other_ref, 1 - side_bit)):
            entry = (level, side_bit, side, k)
            target[rank, 0], target[rank, 1] = turns(base_ref[entry], rate_ref[entry], bins)
        return carry

    lax.fori_loop(0, beams, beam, 0, unroll=4)


def split_own_kernel(
    level, count, late, index_ref, beam_ref, shift_ref, taps_ref, *rest
):
    if late:
        received_ext, last_partial, last_turn, own_turn, own_ext, partial_ref, ext = rest
        first_place, first_rank = own_ext.shape[0], own_ext.shape[0]
        copy_extended(own_ext, ext)
    else:
        first_ext, received_ref, last_partial, last_turn, own_turn, received_ext, partial_ref, ext = rest
        first_place, first_rank = 0, 0
        extend_received(received_ref, received_ext, first_ext.shape[0], received_ref.shape[0])
        copy_extended(first_ext, received_ext)
    index = index_ref[0]
    side_bit = (index >> level) % 2
    start = order_start(level, index)
    last_factors = tap_factors(taps_ref, level - 1)
    for place in range(first_place, ext.shape[0]):
        k = side_bit * 7 + slot_at(place, start, count)
        pair = merged(
            level - 1, index, k, k, 0, HALF, (beam_ref, shift_ref), last_factors, count, received_ext, last_partial,
            last_turn,
        )
        for part in range(2):
            store_extended(ext, (place, part), pair[part])
    factors = tap_factors(taps_ref, level)
    for rank in range(first_rank, partial_ref.shape[0]):
        k = rank_beam(level, index, rank, count, own_turn.shape[0])
        own = (level, side_bit, side_bit, k)
        slot = place_of(beam_ref[own] - side_bit * 7, start, count)
        for first_row in range(0, HALF, 32):
            here = pl.ds(first_row, 32)
            pair = times(
                filtered(ext, slot, shift_ref[own] + (HALO + first_row), 32, *factors),
                (own_turn[rank, 0, here], own_turn[rank, 1, here]),
            )
            partial_ref[rank, 0, here], partial_ref[rank, 1, here] = pair


def extend_received(received_ref, ext, first, number):
    for i in range(number):
        for part in range(2):
            store_extended(ext, (first + i, part), received_ref[i, part].astype(jnp.float32))


def copy_extended(source, target):
    for slot in range(source.shape[0]):
        target[slot] = source[slot]


def send_parents(level, index, first_place, sends, tables, factors, count, ext, partial_ref, turn_ref, offset=None):
    next_bit = (index >> (level + 1)) % 2
    start = order_start(level + 1, index ^ (2 << level))
    place = first_place
    for target in sends:
        for at in range(target.shape[0]):
            k = (1 - next_bit) * 7 + slot_at(place, start, count)
            row = k if offset is None else place - offset
            for first_row in range(0, HALF, 32):
                pair = merged(level, index, k, row, first_row, 32, tables, factors, count, ext, partial_ref, turn_ref)
                for part in range(2):
                    target[at, part, pl.ds(first_row, 32)] = pair[part].astype(jnp.bfloat16)
            place += 1


def bottom_first_kernel(
    count, index_ref, beam_ref, shift_ref, taps_ref, received_ref, partial_ref, turn_ref, send_ref, ext
):
    extend_received(received_ref, ext, 0, ext.shape[0])
    send_parents(
        0, index_ref[0], 0, (send_ref,), (beam_ref, shift_ref), tap_factors(taps_ref, 0), count, ext, partial_ref,
        turn_ref, 0,
    )


def bottom_second_kernel(
    count, index_ref, beam_ref, shift_ref, taps_ref, received_ref, first_ext, partial_ref, turn_ref, *outs
):
    sends, ext = outs[:-1], outs[-1]
    first = first_ext.shape[0]
    extend_received(received_ref, ext, first, count - first)
    copy_extended(first_ext, ext)
    send_parents(
        0, index_ref[0], first, sends, (beam_ref, shift_ref), tap_factors(taps_ref, 0), count, ext, partial_ref,
        turn_ref, first,
    )


def middle_first_kernel(
    level, offset, count, index_ref, beam_ref, shift_ref, taps_ref, received_ref, partial_ref, turn_ref, send_ref, ext,
):
    extend_received(received_ref, ext, 0, received_ref.shape[0])
    send_parents(
        level, index_ref[0], 0, (send_ref,), (beam_ref, shift_ref), tap_factors(taps_ref, level), count,
        ext, partial_ref, turn_ref, offset,
    )


def late_send_kernel(
    level, count, index_ref, beam_ref, shift_ref, taps_ref, ext, partial_ref, turn_ref, send_ref,
):
    send_parents(
        level, index_ref[0], PARTS[level + 1][0], (send_ref,), (beam_ref, shift_ref), tap_factors(taps_ref, level), count,
        ext, partial_ref, turn_ref,
    )


def middle_second_kernel(
    level, count, index_ref, beam_ref, shift_ref, taps_ref, received_ref, first_ext, partial_ref, turn_ref, send_ref, ext
):
    extend_received(received_ref, ext, first_ext.shape[0], received_ref.shape[0])
    copy_extended(first_ext, ext)
    send_parents(
        level, index_ref[0], PARTS[level + 1][0], (send_ref,), (beam_ref, shift_ref), tap_factors(taps_ref, level), count,
        ext, partial_ref, turn_ref, 0,
    )


def make_pair(level, index, q, tables, factors, count, ext, partial_ref, turn_ref):
    even = merged(level, index, 2 * q, 2 * q, 0, HALF, tables, factors, count, ext, partial_ref, turn_ref)
    odd = merged(level, index, 2 * q + 1, 2 * q + 1, 0, HALF, tables, factors, count, ext, partial_ref, turn_ref)
    return even, odd


def place_pair(even, odd, out_ref, where, low):
    lane = lane_iota(HALF)
    turned = jnp.concatenate([even, odd], axis=0).T
    a = turned[:HALF]
    b = turned[HALF:]
    out_ref[(*where, pl.ds(low, HALF, stride=8))] = jnp.where(lane < HALF, a, pltpu.roll(b, HALF, 1))
    out_ref[(*where, pl.ds(low + 1, HALF, stride=8))] = jnp.where(lane < HALF, pltpu.roll(a, HALF, 1), b)


EARLY = 3


def last_first_kernel(
    level, count, index_ref, beam_ref, shift_ref, taps_ref, received_ref, partial_ref, turn_ref, tiles_ref, ext,
):
    extend_received(received_ref, ext, 0, received_ref.shape[0])
    factors = tap_factors(taps_ref, level)
    for q in range(EARLY):
        even, odd = make_pair(
            level, index_ref[0], q, (beam_ref, shift_ref), factors, count, ext, partial_ref, turn_ref
        )
        for part in range(2):
            place_pair(even[part], odd[part], tiles_ref, (part,), 2 * q)


def last_second_kernel(
    level, count, index_ref, beam_ref, shift_ref, taps_ref, received_ref, first_ext, tiles_ref, partial_ref, turn_ref, out_hbm,
    ext, tiles, sems,
):
    extend_received(received_ref, ext, first_ext.shape[0], received_ref.shape[0])
    copy_extended(first_ext, ext)
    tiles[:, 0] = tiles_ref[...]
    factors = tap_factors(taps_ref, level)
    copies = []
    for q in range(EARLY, partial_ref.shape[0] // 2):
        even, odd = make_pair(
            level, index_ref[0], q, (beam_ref, shift_ref), factors, count, ext, partial_ref, turn_ref
        )
        high, low = q // 4, 2 * (q % 4)
        for part in range(2):
            place_pair(even[part], odd[part], tiles, (part, high), low)
            if low == 6:
                copy = pltpu.make_async_copy(tiles.at[part, high], out_hbm.at[part, high], sems.at[part, high])
                copy.start()
                copies.append(copy)
    for copy in copies:
        copy.wait()


def params():
    return pltpu.CompilerParams(vmem_limit_bytes=VMEM_LIMIT)


def route(axis, bit):
    count = lax.axis_size(axis)
    return [(i, i ^ (1 << bit)) for i in range(count) if i ^ (1 << bit) < count]


def local(raw_echoes, matched, delays, pulse_phase, beam_map, range_shift, phase_base, phase_rate, tap_offsets):
    pulses, blocks, parts, hop = raw_echoes.shape
    beams = delays.shape[1]
    levels = tap_offsets.shape[0]
    bins = blocks * hop
    slots = beams // 2 + 1
    index = lax.axis_index("pulse").astype(jnp.int32).reshape(1)
    f32, bf16 = jnp.float32, jnp.bfloat16
    image_shape = jax.ShapeDtypeStruct((beams, 2, HALF, LANES), f32)
    send_shape = jax.ShapeDtypeStruct((PARTS[0][0], 2, HALF, LANES), bf16)
    rows = pulses * blocks
    inputs = (delays, beam_map, range_shift, phase_base, phase_rate, tap_offsets)
    sources = (raw_echoes.reshape(rows * parts, hop), matched, pulse_phase, *inputs)
    pulse_shape = jax.ShapeDtypeStruct((pulses, 2, HALF + 2 * HALO, LANES), f32)
    trig_shape = jax.ShapeDtypeStruct((2, beams, pulses, LANES), f32)
    send, pulse_ext, trig, delay_table, *tables = pl.pallas_call(
        front_kernel,
        out_shape=(send_shape, pulse_shape, trig_shape, *(pltpu.SMEM(x.shape, x.dtype) for x in inputs)),
        in_specs=[SMEM_SPEC] + [HBM_SPEC] * len(sources),
        out_specs=(VMEM_SPEC, VMEM_SPEC, VMEM_SPEC, *(SMEM_SPEC for x in inputs)),
        scratch_shapes=[
            pltpu.VMEM((parts * rows, LANES), bf16),
            pltpu.VMEM(matched.shape, f32),
            pltpu.VMEM(pulse_phase.shape, f32),
            pltpu.VMEM((16 + parts * rows, LANES), f32),
            pltpu.VMEM((2 * LANES, 4 * LANES), bf16),
            pltpu.VMEM((rows, 4 * LANES), bf16),
            pltpu.SemaphoreType.DMA((2 + len(inputs) + rows // LANES,)),
        ],
        compiler_params=params(),
        name="front",
    )(index, *(pltpu.with_memory_space_constraint(x, pltpu.HBM) for x in sources))
    beam_table, shift_table, base_table, rate_table, tap_table = tables
    scalars = (index, beam_table, shift_table, tap_table)

    def shape(number, dtype=bf16, rows=HALF):
        return jax.ShapeDtypeStruct((number, 2, rows, LANES), dtype)

    def kernel(function, out_shape, operands, name, scratch=(), out_specs=None, scalar_count=len(scalars)):
        return pl.pallas_call(
            function,
            out_shape=out_shape,
            in_specs=[SMEM_SPEC] * scalar_count + [VMEM_SPEC] * (len(operands) - scalar_count),
            out_specs=jax.tree.map(lambda x: VMEM_SPEC, out_shape) if out_specs is None else out_specs,
            scratch_shapes=list(scratch),
            compiler_params=params(),
            cost_estimate=pl.CostEstimate(flops=COSTS[name], bytes_accessed=2**20, transcendentals=0),
            name=name,
        )(*operands)

    own_scalars = (index, *tables)
    long = HALF + 2 * HALO
    images = (image_shape, image_shape)
    ext_scratch = [pltpu.VMEM((slots, 2, long, LANES), f32)]

    def own(level, outs, *operands):
        return kernel(
            functools.partial(own_kernel, level, bins, slots), (image_shape,) * outs, own_scalars + operands, f"own{level}",
            ext_scratch, scalar_count=len(own_scalars),
        )

    def exchange(x, level):
        return lax.ppermute(x, "pulse", route("pulse", level))

    received = exchange(send, 0)
    first, later = PARTS[1]
    bottom_scalars = (*own_scalars, delay_table)
    partial, turn, own_ext = kernel(
        functools.partial(bottom_own_kernel, bins, slots, 0, 0),
        (shape(first, f32), shape(first, f32), shape(first, f32, long)),
        (*bottom_scalars, pulse_ext, trig),
        "bottomownfirst",
        scalar_count=len(bottom_scalars),
    )
    early, first_ext = kernel(
        functools.partial(bottom_first_kernel, slots),
        (shape(first), shape(first, f32, long)),
        (*scalars, received, partial, turn),
        "bottomfirst",
    )
    send = kernel(
        front_second_kernel,
        shape(PARTS[0][1]),
        (index, delay_table, pulse_ext, trig, early),
        "frontsecond",
        scalar_count=2,
    )
    partial, turn = kernel(
        functools.partial(bottom_own_kernel, bins, slots, first, first),
        (shape(beams - first, f32), shape(beams - first, f32)),
        (*bottom_scalars, pulse_ext, trig, own_ext),
        "bottomownsecond",
        ext_scratch,
        scalar_count=len(bottom_scalars),
    )
    late, ext = kernel(
        functools.partial(bottom_second_kernel, slots),
        (shape(later), shape(slots, f32, long)),
        (*scalars, exchange(send, 0), first_ext, partial, turn),
        "bottomsecond",
    )
    received = exchange(early, 1), exchange(late, 1)
    partial, turn = own(1, 2, early, late, ext, partial, turn)
    early, first_ext = kernel(
        functools.partial(middle_first_kernel, 1, None, slots),
        (shape(PARTS[2][0]), shape(PARTS[1][0], f32, long)),
        (*scalars, received[0], partial, turn),
        "middle1first",
    )
    received_first = exchange(early, 2)
    own_turn, next_turn = kernel(
        functools.partial(turns_kernel, 2, bins),
        images,
        (index, base_table, rate_table, early),
        "turns2",
        scalar_count=3,
    )
    ext, next_partial, own_ext = kernel(
        functools.partial(split_own_kernel, 2, slots, False),
        (shape(slots, f32, long), shape(PARTS[3][0], f32), shape(PARTS[2][0], f32, long)),
        (*scalars, first_ext, received[1], partial, turn, own_turn),
        "own2first",
    )
    last_early, last_ext = kernel(
        functools.partial(middle_first_kernel, 2, 0, slots),
        (shape(PARTS[3][0]), shape(PARTS[2][0], f32, long)),
        (*scalars, received_first, next_partial, next_turn),
        "middle2first",
    )
    last_first = exchange(last_early, 3)
    late = kernel(
        functools.partial(late_send_kernel, 1, slots),
        shape(PARTS[2][1]),
        (*scalars, ext, partial, turn),
        "middle1second",
    )
    received_second = exchange(late, 2)
    next_partial = kernel(
        functools.partial(split_own_kernel, 2, slots, True),
        image_shape,
        (*scalars, ext, partial, turn, own_turn, own_ext),
        "own2second",
        ext_scratch,
    )
    last_late, ext = kernel(
        functools.partial(middle_second_kernel, 2, slots),
        (shape(PARTS[3][1]), shape(slots, f32, long)),
        (*scalars, received_second, last_ext, next_partial, next_turn),
        "middle2second",
    )
    last_second = exchange(last_late, 3)
    partial, turn = own(3, 2, last_early, last_late, ext, next_partial, next_turn)
    tiles, first_ext = kernel(
        functools.partial(last_first_kernel, 3, slots),
        (jax.ShapeDtypeStruct((2, HALF * 8, LANES), f32), shape(PARTS[3][0], f32, long)),
        (*scalars, last_first, partial, turn),
        "lastfirst",
    )
    out = kernel(
        functools.partial(last_second_kernel, 3, slots),
        jax.ShapeDtypeStruct((2, beams // 8, HALF * 8, LANES), f32),
        (*scalars, last_second, first_ext, tiles, partial, turn),
        "lastsecond",
        ext_scratch + [pltpu.VMEM((2, beams // 8, HALF * 8, LANES), f32), pltpu.SemaphoreType.DMA((2, beams // 8))],
        HBM_SPEC,
    )
    out = out.reshape(2, beams // 8, HALF, 8, LANES)
    return jnp.transpose(out, (0, 1, 3, 2, 4)).reshape(2, beams, bins)


def shifted(array, axis, by):
    count = lax.axis_size(axis)
    pairs = [(i, i + by) for i in range(count) if 0 <= i + by < count]
    return lax.ppermute(array, axis, pairs)


def padded_2(block, sides, width):
    for axis, dim in sides:
        count = lax.axis_size(axis)
        forward = [(i, i + 1) for i in range(count - 1)]
        backward = [(target, source) for source, target in forward]
        low = lax.ppermute(
            lax.slice_in_dim(block, block.shape[dim] - width, None, axis=dim), axis, forward
        )
        high = lax.ppermute(lax.slice_in_dim(block, 0, width, axis=dim), axis, backward)
        block = jnp.concatenate([low, block, high], axis=dim)
    return block


def from_partner(block, axis, bit):
    count = lax.axis_size(axis)
    route = []
    for low in range(count):
        high = low | 1 << bit
        if high != low and high < count:
            route += [(low, high), (high, low)]
    return lax.ppermute(block, axis, route)


def tables(length):
    counter = jnp.arange(length, dtype=jnp.int32)
    product = counter[:, None] * counter[None, :] % length
    angles = product.astype(jnp.float32) * (2.0 * math.pi / length)
    cosine = jnp.cos(angles)
    sine_part = jnp.sin(angles)
    forward = jnp.concatenate(
        [
            jnp.concatenate([cosine, -sine_part], axis=1),
            jnp.concatenate([sine_part, cosine], axis=1),
        ],
        axis=0,
    )
    inverse = jnp.concatenate(
        [
            jnp.concatenate([cosine, sine_part], axis=1),
            jnp.concatenate([-sine_part, cosine], axis=1),
        ],
        axis=0,
    )
    return (forward, inverse)


def compress(echoes, tail, matched, forward_exact, forward, inverse_kept):
    pulses, blocks, parts, hop_bins = echoes.shape
    length = 2 * hop_bins
    previous = jnp.concatenate([tail[:, None], echoes[:, :-1]], axis=1)
    windows = jnp.concatenate([previous, echoes], axis=3).reshape(pulses * blocks, parts * length)
    taps_padded = jnp.concatenate(
        [matched, jnp.zeros((2, length - hop_bins), jnp.float32)], axis=1
    ).reshape(1, 2 * length)
    response = jnp.dot(taps_padded, forward_exact, precision=lax.Precision.HIGHEST)[0]
    resp_real = response[:length]
    resp_imag = response[length:]
    spectrum = jnp.dot(windows, forward, preferred_element_type=jnp.float32)
    spec_real = spectrum[:, :length]
    spec_imag = spectrum[:, length:]
    filt_real = spec_real * resp_real - spec_imag * resp_imag
    filt_imag = spec_real * resp_imag + spec_imag * resp_real
    shaped = jnp.concatenate([filt_real, filt_imag], axis=1).astype(jnp.bfloat16)
    restored = jnp.dot(shaped, inverse_kept, preferred_element_type=jnp.float32) * (1.0 / length)
    return restored.astype(jnp.bfloat16).reshape(pulses, blocks, parts, hop_bins)


def kept_columns(inverse, length):
    half = length // 2
    return jnp.concatenate([inverse[:, half:length], inverse[:, length + half :]], axis=1)


def inside_mask(first_cell, out_cells, bins):
    global_cells = first_cell + jnp.arange(out_cells, dtype=jnp.int32)
    return ((global_cells >= 0) & (global_cells < bins)).astype(jnp.float32)


def row_slices(rows, starts, width):

    def per_pulse(row, start_row):
        return jax.vmap(lambda start: lax.dynamic_slice_in_dim(row, start, width, 1))(start_row)

    return jax.vmap(per_pulse)(rows, starts)


def project(padded, delay_rows, phase_rows, offset_base, out_cells, first_cell, bins):
    pulses = padded.shape[0]
    beam_count = delay_rows.shape[1]
    group_size = math.gcd(pulses, 4)
    block_count = pulses // group_size

    def accumulate(summed, block_index):
        first_row = block_index * group_size
        pulses_block = lax.dynamic_slice_in_dim(padded, first_row, group_size, 0)
        delay_block = lax.dynamic_slice_in_dim(delay_rows, first_row, group_size, 0)
        phase_block = lax.dynamic_slice_in_dim(phase_rows, first_row, group_size, 0)
        starts = delay_block + offset_base
        gathered = row_slices(pulses_block, starts, out_cells).astype(jnp.float32)
        cosine = jnp.cos(phase_block)[:, :, None]
        sine_part = jnp.sin(phase_block)[:, :, None]
        real_part = gathered[:, :, 0] * cosine - gathered[:, :, 1] * sine_part
        imag_part = gathered[:, :, 0] * sine_part + gathered[:, :, 1] * cosine
        return (summed + jnp.stack([jnp.sum(real_part, axis=0), jnp.sum(imag_part, axis=0)]), None)

    summed, unused = lax.scan(
        accumulate,
        jnp.zeros((2, beam_count, out_cells), jnp.float32),
        jnp.arange(block_count, dtype=jnp.int32),
    )
    return summed * inside_mask(first_cell, out_cells, bins) * (1.0 / math.sqrt(pulses))


def tap_weights(tap_values):
    weights = SPREAD + 1.0 - jnp.abs(tap_values).astype(jnp.float32)
    return weights / jnp.sum(weights)


def merge_side(
    source,
    beam_rows,
    offsets,
    phase_zero,
    phase_slope,
    weights,
    tap_values,
    offset_base,
    out_cells,
    first_cell,
    bins,
):
    span = out_cells + 2 * SPREAD
    starts = offsets + offset_base - SPREAD
    windows = jax.vmap(
        lambda beam, start: lax.dynamic_slice(source, (0, beam, start), (2, 1, span))[:, 0],
        out_axes=1,
    )(beam_rows, starts)
    summed = jnp.zeros((2, beam_rows.shape[0], out_cells), jnp.float32)
    for tap_index in range(tap_values.shape[0]):
        tap_start = tap_values[tap_index] + SPREAD
        summed = summed + weights[tap_index] * lax.dynamic_slice_in_dim(
            windows, tap_start, out_cells, 2
        )
    positions = jnp.arange(out_cells, dtype=jnp.int32)
    global_cells = (first_cell + positions).astype(jnp.float32)
    angle_grid = (
        phase_zero[:, None] + 2.0 * math.pi / bins * phase_slope[:, None] * global_cells[None, :]
    )
    cosine = jnp.cos(angle_grid)
    sine_part = jnp.sin(angle_grid)
    return jnp.stack(
        [summed[0] * cosine - summed[1] * sine_part, summed[0] * sine_part + summed[1] * cosine]
    )


def pick_sides(table, level_index, side_bit):
    half_rows = lax.dynamic_index_in_dim(table[level_index], side_bit, 0, keepdims=False)
    own_rows = lax.dynamic_index_in_dim(half_rows, side_bit, 0, keepdims=False)
    other_rows = lax.dynamic_index_in_dim(half_rows, 1 - side_bit, 0, keepdims=False)
    return (own_rows, other_rows)


def local_split(
    raw_echoes,
    matched,
    delays,
    pulse_phase,
    beam_map,
    range_shift,
    phase_base,
    phase_rate,
    tap_offsets,
):
    pulses = raw_echoes.shape[0]
    hop_bins = raw_echoes.shape[3]
    local_cells = raw_echoes.shape[1] * hop_bins
    bins = local_cells * lax.axis_size("rng")
    length = 2 * hop_bins
    levels = tap_offsets.shape[0]
    forward_exact, inverse_exact = tables(length)
    forward = forward_exact.astype(jnp.bfloat16)
    inverse_kept = kept_columns(inverse_exact.astype(jnp.bfloat16), length)
    tail = shifted(raw_echoes[:, -1], "rng", 1)
    compressed = compress(raw_echoes, tail, matched, forward_exact, forward, inverse_kept)
    compressed = jnp.transpose(compressed, (0, 2, 1, 3)).reshape(pulses, 2, local_cells)
    first_cell = lax.axis_index("rng") * local_cells
    rim_cells = SHIFT + SPREAD
    margin_cells = levels * rim_cells
    padded = padded_2(compressed, (("rng", 2),), SHIFT + margin_cells)
    polar_image = project(
        padded,
        delays,
        pulse_phase,
        SHIFT,
        local_cells + 2 * margin_cells,
        first_cell - margin_cells,
        bins,
    )
    pulse_index = lax.axis_index("pulse")
    for level_index in range(levels):
        side_bit = pulse_index // 2**level_index % 2
        own_beams, other_beams = pick_sides(beam_map, level_index, side_bit)
        own_offsets, other_offsets = pick_sides(range_shift, level_index, side_bit)
        own_zero, other_zero = pick_sides(phase_base, level_index, side_bit)
        own_slope, other_slope = pick_sides(phase_rate, level_index, side_bit)
        tap_values = tap_offsets[level_index]
        weights = tap_weights(tap_values)
        received = from_partner(polar_image, "pulse", level_index)
        own_source = polar_image
        out_margin = max(margin_cells - rim_cells * (level_index + 1), 0)
        out_cells = local_cells + 2 * out_margin
        start_cell = first_cell - out_margin
        own_side = merge_side(
            own_source,
            own_beams,
            own_offsets,
            own_zero,
            own_slope,
            weights,
            tap_values,
            rim_cells,
            out_cells,
            start_cell,
            bins,
        )
        other_side = merge_side(
            received,
            other_beams,
            other_offsets,
            other_zero,
            other_slope,
            weights,
            tap_values,
            rim_cells,
            out_cells,
            start_cell,
            bins,
        )
        polar_image = (own_side + other_side) * SQRT_HALF * inside_mask(start_cell, out_cells, bins)
    return polar_image


def solution(mesh):
    in_specs = (
        P(("grp", "pulse"), "rng", None, None),
        P(),
        P(("grp", "pulse"), None),
        P(("grp", "pulse"), None),
        P(),
        P(),
        P(),
        P(),
        P(),
    )
    out_specs = P(None, ("grp", "pulse"), "rng")
    whole_range = mesh.shape["rng"] == 1
    return jax.shard_map(local if whole_range else local_split, mesh=mesh, in_specs=in_specs, out_specs=out_specs, check_vma=False)
```

```python
import functools
import math

import jax
import jax.numpy as jnp
import numpy as np
from jax import lax
from jax.experimental import pallas as pl
from jax.experimental.pallas import tpu as pltpu
from jax.sharding import PartitionSpec as P

SPREAD = 4
SHIFT = 24
HALO = 32
LANES = 128
HALF = 64
PARTS = {0: (9,), 1: (5, 4), 2: (5, 4), 3: (5, 4)}
SQRT_HALF = 0.7071067811865476
VMEM_LIMIT = 24 * 2**20

COS_COEFFS = (
    1.0,
    -19.73920440673828,
    64.93911743164062,
    -85.45014190673828,
    60.16762924194336,
    -25.967599868774414,
    6.528658390045166,
)
SIN_COEFFS = (
    6.2831854820251465,
    -41.34170150756836,
    81.60513305664062,
    -76.70301818847656,
    42.02592849731445,
    -14.899847030639648,
    3.2381374835968018,
)

SMEM_SPEC = pl.BlockSpec(memory_space=pltpu.SMEM)
VMEM_SPEC = pl.BlockSpec(memory_space=pltpu.VMEM)
COSTS = {
    "bottomownfirst": 800,
    "bottomfirst": 300,
    "bottomownsecond": 1050,
    "bottomsecond": 270,
    "own1": 1500,
    "turns2": 500,
    "middle1first": 310,
    "own2first": 600,
    "middle1second": 180,
    "middle2first": 320,
    "own2second": 640,
    "middle2second": 260,
    "own3": 1470,
    "lastfirst": 570,
    "lastsecond": 1550,
}
COSTS = {name: 1000 * cost for name, cost in COSTS.items()}

HBM_SPEC = pl.BlockSpec(memory_space=pltpu.HBM)


def cos_sin_turns(turns):
    f = turns - jnp.round(turns)
    u = f * f
    c = jnp.full_like(u, COS_COEFFS[-1])
    for a in COS_COEFFS[-2::-1]:
        c = c * u + a
    s = jnp.full_like(u, SIN_COEFFS[-1])
    for a in SIN_COEFFS[-2::-1]:
        s = s * u + a
    return c, s * f


def times(x, y):
    return x[0] * y[0] - x[1] * y[1], x[0] * y[1] + x[1] * y[0]


def lane_iota(rows):
    return lax.broadcasted_iota(jnp.int32, (rows, LANES), 1)


def store_extended(ext_ref, where, body):
    lane = lane_iota(HALO)
    high, low = body[:HALO], body[HALF - HALO :]
    ext_ref[(*where, pl.ds(HALO, HALF))] = body
    after = jnp.where(lane < HALF, pltpu.roll(high, HALF, 1), pltpu.roll(high, HALF - 1, 1))
    ext_ref[(*where, pl.ds(HALO + HALF, HALO))] = jnp.where(lane == LANES - 1, 0.0, after)
    before = jnp.where(lane < HALF, pltpu.roll(low, HALF + 1, 1), pltpu.roll(low, HALF, 1))
    ext_ref[(*where, pl.ds(0, HALO))] = jnp.where(lane == 0, 0.0, before)


def front_kernel(
    index_ref, raw_hbm, matched_hbm, phase_hbm, *rest
):
    tables, rest = rest[:6], rest[6:]
    send_ref, ext, trig, rest = rest[0], rest[1], rest[2], rest[3:]
    copied, rest = rest[:6], rest[6:]
    delays = copied[0]
    raw, matched, phase, raw32, taps, windows, sems = rest
    pulses, beams = phase.shape
    rows = raw.shape[0] // 2
    blocks = rows // pulses
    pairs = rows // LANES
    size = raw.shape[0] // pairs

    small = [
        pltpu.make_async_copy(matched_hbm, matched, sems.at[0]),
        pltpu.make_async_copy(phase_hbm, phase, sems.at[1]),
    ]
    small += [
        pltpu.make_async_copy(source, target, sems.at[2 + i]) for i, (source, target) in enumerate(zip(tables, copied))
    ]
    large = [
        pltpu.make_async_copy(
            raw_hbm.at[pl.ds(pair * size, size)], raw.at[pl.ds(pair * size, size)], sems.at[2 + len(tables) + pair]
        )
        for pair in range(pairs)
    ]
    for copy in large[:1] + small[:2] + large[1:] + small[2:]:
        copy.start()
    raw32[0:16] = jnp.zeros((16, LANES), jnp.float32)
    for copy in small[:2] + large:
        copy.wait()
    scale = 1.0 / math.sqrt(pulses)
    pair_of = cos_sin_turns(phase[...] * (0.5 / math.pi))
    for part in range(2):
        for k in range(beams):
            trig[part, k] = jnp.broadcast_to(pair_of[part][:, k : k + 1] * scale, (pulses, LANES))
    row = lax.broadcasted_iota(jnp.int32, (LANES, LANES), 0)
    column = lax.broadcasted_iota(jnp.int32, (LANES, LANES), 1)
    for part in range(2):
        line = jnp.broadcast_to(matched[part : part + 1, :], (LANES, LANES))
        circulant = pltpu.roll(line, 0, 1, stride=1, stride_axis=0).T
        now = jnp.where(column <= row, circulant, 0.0).astype(jnp.bfloat16)
        before = jnp.where(column > row, circulant, 0.0).astype(jnp.bfloat16)
        if part == 0:
            taps[0:LANES, 0:LANES] = before
            taps[LANES:, LANES : 2 * LANES] = before
            taps[0:LANES, 2 * LANES : 3 * LANES] = now
            taps[LANES:, 3 * LANES :] = now
        else:
            taps[0:LANES, LANES : 2 * LANES] = -before
            taps[LANES:, 0:LANES] = before
            taps[0:LANES, 3 * LANES :] = -now
            taps[LANES:, 2 * LANES : 3 * LANES] = now
    first = lax.broadcasted_iota(jnp.int32, (LANES, LANES), 0) % blocks == 0
    lane = lane_iota(HALF)
    for pair in range(pairs):
        raw32[16 + pair * size : 16 + (pair + 1) * size] = raw[pair * size : (pair + 1) * size, :].astype(jnp.float32)
        mine = slice(pair * LANES, (pair + 1) * LANES)
        for part in range(2):
            previous = raw32[pl.ds(14 + pair * size + part, LANES, stride=2), :]
            windows[mine, part * LANES : (part + 1) * LANES] = jnp.where(first, 0.0, previous).astype(jnp.bfloat16)
            current = raw32[pl.ds(16 + pair * size + part, LANES, stride=2), :]
            windows[mine, (2 + part) * LANES : (3 + part) * LANES] = current.astype(jnp.bfloat16)
    for pair in range(pairs):
        made = lax.dot_general(
            taps[...],
            windows[pair * LANES : (pair + 1) * LANES, :],
            (((1,), (1,)), ((), ())),
            preferred_element_type=jnp.float32,
        )
        for part in range(2):
            a = made[part * LANES : part * LANES + HALF]
            b = made[part * LANES + HALF : (part + 1) * LANES]
            store_extended(ext, (2 * pair, part), jnp.where(lane < HALF, a, pltpu.roll(b, HALF, 1)))
            store_extended(ext, (2 * pair + 1, part), jnp.where(lane < HALF, pltpu.roll(a, HALF, 1), b))
    small[2].wait()
    send_pulses(index_ref[0], 0, send_ref, delays, trig, ext)
    for copy in small[3:]:
        copy.wait()


def send_pulses(index, first_place, send_ref, delays, trig, ext):
    count = sum(PARTS[0])
    start = order_start(0, index ^ 1)
    for at in range(send_ref.shape[0]):
        k = (1 - index % 2) * 7 + slot_at(first_place + at, start, count)
        for first_row in range(0, HALF, 32):
            pair = projected(k, first_row, 32, delays, trig, ext)
            for part in range(2):
                send_ref[at, part, pl.ds(first_row, 32)] = pair[part].astype(jnp.bfloat16)


def projected(k, first_row, rows, delays, trig, ext):
    real = imag = None
    for p in range(ext.shape[0]):
        here = pl.ds(delays[p, k] + (HALO + first_row), rows)
        x = ext[p, 0, here, :]
        y = ext[p, 1, here, :]
        cosine = trig[0, k, pl.ds(p, 1), :]
        sine = trig[1, k, pl.ds(p, 1), :]
        re = x * cosine - y * sine
        im = x * sine + y * cosine
        real = re if real is None else real + re
        imag = im if imag is None else imag + im
    return real, imag


def tap_factors(taps_ref, level):
    count = taps_ref.shape[1]
    offsets = [taps_ref[level, t] for t in range(count)]
    weights = [(SPREAD + 1.0) - jnp.abs(o).astype(jnp.float32) for o in offsets]
    total = weights[0]
    for w in weights[1:]:
        total = total + w
    scale = SQRT_HALF / total
    return offsets, [w * scale for w in weights]


def filtered(ext, slot, start, rows, offsets, weights):
    sums = []
    for part in range(2):
        total = None
        for offset, weight in zip(offsets, weights):
            term = ext[slot, part, pl.ds(start + offset, rows), :] * weight
            total = term if total is None else total + term
        sums.append(total)
    return tuple(sums)


def order_start(level, index):
    if level == 0:
        first_beam = 7 * (1 - ((index >> 1) & 1)) + order_start(1, index ^ 2)
        return jnp.maximum(first_beam // 2 + (index & 1) - 1, 0)
    first, second, third = (index >> 1) & 1, (index >> 2) & 1, (index >> 3) & 1
    if level == 1:
        low = (1 - third) * first
        high = third * (2 + first) + (1 - third) * 4
        return second * low + (1 - second) * high
    if level == 2:
        return (1 - third) * (2 + second)
    return 0


def place_of(slot, start, count):
    place = slot - start
    return jnp.where(place < 0, place + count, place)


def slot_at(place, start, count):
    slot = start + place
    return jnp.where(slot >= count, slot - count, slot)


def merged(level, index, k, at, first_row, rows, tables, factors, count, ext, partial_ref, turn_ref):
    beam_ref, shift_ref = tables
    side_bit = (index >> level) % 2
    other = (level, side_bit, 1 - side_bit, k)
    slot = beam_ref[other] - side_bit * 7
    slot = place_of(slot, order_start(level, index), count)
    start = shift_ref[other] + (HALO + first_row)
    here = pl.ds(first_row, rows)
    real, imag = times(filtered(ext, slot, start, rows, *factors), (turn_ref[at, 0, here], turn_ref[at, 1, here]))
    return real + partial_ref[at, 0, here], imag + partial_ref[at, 1, here]


def turns(base, rate, bins):
    t = lax.broadcasted_iota(jnp.int32, (8, LANES), 0)
    lane = lane_iota(8)
    position = (t + (lane % HALF) * LANES + (lane // HALF) * HALF).astype(jnp.float32) * (1.0 / bins)
    groups = [cos_sin_turns(position * rate + base * (0.5 / math.pi))]
    step = cos_sin_turns(jnp.full((8, LANES), rate * (8.0 / bins)))
    while len(groups) < HALF // 8:
        groups += [times(g, step) for g in groups]
        step = times(step, step)
    return tuple(jnp.concatenate([g[i] for g in groups], axis=0) for i in range(2))


def read_sent(refs, place, part):
    value = None
    first = 0
    for ref in refs:
        size = ref.shape[0]
        here = ref[jnp.clip(place - first, 0, size - 1), part].astype(jnp.float32)
        value = here if value is None else jnp.where(place >= first, here, value)
        first += size
    return value


def rank_beam(level, index, rank, count, beams):
    first = (1 - ((index >> (level + 1)) & 1)) * 7
    if rank < count:
        return first + slot_at(rank, order_start(level + 1, index ^ (2 << level)), count)
    return (first + rank) % beams


def bottom_own_kernel(
    bins, count, first_place, first_rank, index_ref, beam_ref, shift_ref, base_ref, rate_ref, taps_ref, delays, pulse_ext,
    trig, *rest
):
    if first_place > 0:
        copy_extended(rest[0], rest[-1])
        rest = rest[1:]
    partial_ref, turn_ref, ext = rest
    index = index_ref[0]
    side_bit = index % 2
    start = order_start(0, index)
    for place in range(first_place, ext.shape[0]):
        k = side_bit * 7 + slot_at(place, start, count)
        pieces = [projected(k, first_row, 32, delays, trig, pulse_ext) for first_row in range(0, HALF, 32)]
        for part in range(2):
            store_extended(ext, (place, part), jnp.concatenate([x[part] for x in pieces], axis=0))
    factors = tap_factors(taps_ref, 0)
    for at in range(partial_ref.shape[0]):
        k = rank_beam(0, index, first_rank + at, count, delays.shape[1])
        own = (0, side_bit, side_bit, k)
        other = (0, side_bit, 1 - side_bit, k)
        slot = place_of(beam_ref[own] - side_bit * 7, start, count)
        turn = turns(base_ref[own], rate_ref[own], bins)
        for first_row in range(0, HALF, 32):
            here = slice(first_row, first_row + 32)
            pair = times(
                filtered(ext, slot, shift_ref[own] + (HALO + first_row), 32, *factors), (turn[0][here], turn[1][here])
            )
            partial_ref[at, 0, here], partial_ref[at, 1, here] = pair
        turn_ref[at, 0], turn_ref[at, 1] = turns(base_ref[other], rate_ref[other], bins)


def own_kernel(level, bins, count, index_ref, beam_ref, shift_ref, base_ref, rate_ref, taps_ref, *rest):
    sent = len(PARTS[level])
    sent_refs, rest = rest[:sent], list(rest[sent:])
    received_ext, last_partial, last_turn = rest[:3]
    rest = rest[3:]
    partial_ref = rest.pop(0)
    turn_ref = rest.pop(0)
    ext = rest.pop(0)
    index = index_ref[0]
    side_bit = (index >> level) % 2
    beams = partial_ref.shape[0]
    shared = 2 * count - beams
    low_beam = side_bit * 7
    urgent = (1 - side_bit) * 7

    for i in range(shared):
        place = place_of(7 * side_bit + i, order_start(level, index ^ (1 << level)), count)
        for part in range(2):
            store_extended(ext, (7 * (1 - side_bit) + i, part), read_sent(sent_refs, place, part))
    last_factors = tap_factors(taps_ref, level - 1)

    def remaining(m, carry):
        k = (urgent + m) % beams
        at = m - PARTS[1][0] if level == 1 else m
        pair = merged(
            level - 1, index, k, at, 0, HALF, (beam_ref, shift_ref), last_factors, count, received_ext, last_partial,
            last_turn,
        )
        for part in range(2):
            store_extended(ext, (k - low_beam, part), pair[part])
        return carry

    lax.fori_loop(count, beams, remaining, 0, unroll=7)
    factors = tap_factors(taps_ref, level)

    def beam(k, carry):
        own = (level, side_bit, side_bit, k)
        other = (level, side_bit, 1 - side_bit, k)
        slot = beam_ref[own] - low_beam
        start = shift_ref[own] + HALO
        turn = turns(base_ref[own], rate_ref[own], bins)
        for first_row in range(0, HALF, 32):
            here = slice(first_row, first_row + 32)
            real, imag = times(
                filtered(ext, slot, start + first_row, 32, *factors), (turn[0][here], turn[1][here])
            )
            partial_ref[k, 0, here] = real
            partial_ref[k, 1, here] = imag
        turn_ref[k, 0], turn_ref[k, 1] = turns(base_ref[other], rate_ref[other], bins)
        return carry

    lax.fori_loop(0, beams, beam, 0, unroll=2)


def turns_kernel(level, bins, index_ref, base_ref, rate_ref, after_ref, own_ref, other_ref):
    index = index_ref[0]
    side_bit = (index >> level) % 2
    beams = own_ref.shape[0]

    def beam(rank, carry):
        k = ((1 - ((index >> (level + 1)) & 1)) * 7 + rank) % beams
        for target, side in ((own_ref, side_bit), (other_ref, 1 - side_bit)):
            entry = (level, side_bit, side, k)
            target[rank, 0], target[rank, 1] = turns(base_ref[entry], rate_ref[entry], bins)
        return carry

    lax.fori_loop(0, beams, beam, 0, unroll=4)


def split_own_kernel(
    level, count, late, index_ref, beam_ref, shift_ref, taps_ref, *rest
):
    if late:
        received_ext, last_partial, last_turn, own_turn, own_ext, partial_ref, ext = rest
        first_place, first_rank = own_ext.shape[0], own_ext.shape[0]
        copy_extended(own_ext, ext)
    else:
        first_ext, received_ref, last_partial, last_turn, own_turn, received_ext, partial_ref, ext = rest
        first_place, first_rank = 0, 0
        extend_received(received_ref, received_ext, first_ext.shape[0], received_ref.shape[0])
        copy_extended(first_ext, received_ext)
    index = index_ref[0]
    side_bit = (index >> level) % 2
    start = order_start(level, index)
    last_factors = tap_factors(taps_ref, level - 1)
    for place in range(first_place, ext.shape[0]):
        k = side_bit * 7 + slot_at(place, start, count)
        pair = merged(
            level - 1, index, k, k, 0, HALF, (beam_ref, shift_ref), last_factors, count, received_ext, last_partial,
            last_turn,
        )
        for part in range(2):
            store_extended(ext, (place, part), pair[part])
    factors = tap_factors(taps_ref, level)
    for rank in range(first_rank, partial_ref.shape[0]):
        k = rank_beam(level, index, rank, count, own_turn.shape[0])
        own = (level, side_bit, side_bit, k)
        slot = place_of(beam_ref[own] - side_bit * 7, start, count)
        for first_row in range(0, HALF, 32):
            here = pl.ds(first_row, 32)
            pair = times(
                filtered(ext, slot, shift_ref[own] + (HALO + first_row), 32, *factors),
                (own_turn[rank, 0, here], own_turn[rank, 1, here]),
            )
            partial_ref[rank, 0, here], partial_ref[rank, 1, here] = pair


def extend_received(received_ref, ext, first, number, source=0):
    for i in range(number):
        for part in range(2):
            store_extended(ext, (first + i, part), received_ref[source + i, part].astype(jnp.float32))


def copy_extended(source, target):
    for slot in range(source.shape[0]):
        target[slot] = source[slot]


def send_parents(level, index, first_place, sends, tables, factors, count, ext, partial_ref, turn_ref, offset=None):
    next_bit = (index >> (level + 1)) % 2
    start = order_start(level + 1, index ^ (2 << level))
    place = first_place
    for target in sends:
        for at in range(target.shape[0]):
            k = (1 - next_bit) * 7 + slot_at(place, start, count)
            row = k if offset is None else place - offset
            for first_row in range(0, HALF, 32):
                pair = merged(level, index, k, row, first_row, 32, tables, factors, count, ext, partial_ref, turn_ref)
                for part in range(2):
                    target[at, part, pl.ds(first_row, 32)] = pair[part].astype(jnp.bfloat16)
            place += 1


def bottom_first_kernel(
    count, index_ref, beam_ref, shift_ref, taps_ref, received_ref, partial_ref, turn_ref, send_ref, ext
):
    extend_received(received_ref, ext, 0, ext.shape[0])
    send_parents(
        0, index_ref[0], 0, (send_ref,), (beam_ref, shift_ref), tap_factors(taps_ref, 0), count, ext, partial_ref,
        turn_ref, 0,
    )


def bottom_second_kernel(
    count, index_ref, beam_ref, shift_ref, taps_ref, received_ref, first_ext, partial_ref, turn_ref, *outs
):
    sends, ext = outs[:-1], outs[-1]
    first = first_ext.shape[0]
    extend_received(received_ref, ext, first, count - first, first)
    copy_extended(first_ext, ext)
    send_parents(
        0, index_ref[0], first, sends, (beam_ref, shift_ref), tap_factors(taps_ref, 0), count, ext, partial_ref,
        turn_ref, first,
    )


def middle_first_kernel(
    level, offset, count, index_ref, beam_ref, shift_ref, taps_ref, received_ref, partial_ref, turn_ref, send_ref, ext,
):
    extend_received(received_ref, ext, 0, received_ref.shape[0])
    send_parents(
        level, index_ref[0], 0, (send_ref,), (beam_ref, shift_ref), tap_factors(taps_ref, level), count,
        ext, partial_ref, turn_ref, offset,
    )


def late_send_kernel(
    level, count, index_ref, beam_ref, shift_ref, taps_ref, ext, partial_ref, turn_ref, send_ref,
):
    send_parents(
        level, index_ref[0], PARTS[level + 1][0], (send_ref,), (beam_ref, shift_ref), tap_factors(taps_ref, level), count,
        ext, partial_ref, turn_ref,
    )


def middle_second_kernel(
    level, count, index_ref, beam_ref, shift_ref, taps_ref, received_ref, first_ext, partial_ref, turn_ref, send_ref, ext
):
    extend_received(received_ref, ext, first_ext.shape[0], received_ref.shape[0])
    copy_extended(first_ext, ext)
    send_parents(
        level, index_ref[0], PARTS[level + 1][0], (send_ref,), (beam_ref, shift_ref), tap_factors(taps_ref, level), count,
        ext, partial_ref, turn_ref, 0,
    )


def make_pair(level, index, q, tables, factors, count, ext, partial_ref, turn_ref):
    even = merged(level, index, 2 * q, 2 * q, 0, HALF, tables, factors, count, ext, partial_ref, turn_ref)
    odd = merged(level, index, 2 * q + 1, 2 * q + 1, 0, HALF, tables, factors, count, ext, partial_ref, turn_ref)
    return even, odd


def place_pair(even, odd, out_ref, where, low):
    lane = lane_iota(HALF)
    turned = jnp.concatenate([even, odd], axis=0).T
    a = turned[:HALF]
    b = turned[HALF:]
    out_ref[(*where, pl.ds(low, HALF, stride=8))] = jnp.where(lane < HALF, a, pltpu.roll(b, HALF, 1))
    out_ref[(*where, pl.ds(low + 1, HALF, stride=8))] = jnp.where(lane < HALF, pltpu.roll(a, HALF, 1), b)


EARLY = 3


def last_first_kernel(
    level, count, index_ref, beam_ref, shift_ref, taps_ref, received_ref, partial_ref, turn_ref, tiles_ref, ext,
):
    extend_received(received_ref, ext, 0, received_ref.shape[0])
    factors = tap_factors(taps_ref, level)
    for q in range(EARLY):
        even, odd = make_pair(
            level, index_ref[0], q, (beam_ref, shift_ref), factors, count, ext, partial_ref, turn_ref
        )
        for part in range(2):
            place_pair(even[part], odd[part], tiles_ref, (part,), 2 * q)


def last_second_kernel(
    level, count, index_ref, beam_ref, shift_ref, taps_ref, received_ref, first_ext, tiles_ref, partial_ref, turn_ref, out_hbm,
    ext, tiles, sems,
):
    extend_received(received_ref, ext, first_ext.shape[0], received_ref.shape[0])
    for slot in range(EARLY - 1, first_ext.shape[0]):
        ext[slot] = first_ext[slot]
    tiles[:, 0] = tiles_ref[...]
    factors = tap_factors(taps_ref, level)
    copies = []
    for q in range(EARLY, partial_ref.shape[0] // 2):
        even, odd = make_pair(
            level, index_ref[0], q, (beam_ref, shift_ref), factors, count, ext, partial_ref, turn_ref
        )
        high, low = q // 4, 2 * (q % 4)
        for part in range(2):
            place_pair(even[part], odd[part], tiles, (part, high), low)
            if low == 6:
                copy = pltpu.make_async_copy(tiles.at[part, high], out_hbm.at[part, high], sems.at[part, high])
                copy.start()
                copies.append(copy)
    for copy in copies:
        copy.wait()


def params():
    return pltpu.CompilerParams(vmem_limit_bytes=VMEM_LIMIT)


def route(axis, bit):
    count = lax.axis_size(axis)
    return [(i, i ^ (1 << bit)) for i in range(count) if i ^ (1 << bit) < count]


def local(raw_echoes, matched, delays, pulse_phase, beam_map, range_shift, phase_base, phase_rate, tap_offsets):
    pulses, blocks, parts, hop = raw_echoes.shape
    beams = delays.shape[1]
    levels = tap_offsets.shape[0]
    bins = blocks * hop
    slots = beams // 2 + 1
    index = lax.axis_index("pulse").astype(jnp.int32).reshape(1)
    f32, bf16 = jnp.float32, jnp.bfloat16
    image_shape = jax.ShapeDtypeStruct((beams, 2, HALF, LANES), f32)
    send_shape = jax.ShapeDtypeStruct((PARTS[0][0], 2, HALF, LANES), bf16)
    rows = pulses * blocks
    inputs = (delays, beam_map, range_shift, phase_base, phase_rate, tap_offsets)
    sources = (raw_echoes.reshape(rows * parts, hop), matched, pulse_phase, *inputs)
    pulse_shape = jax.ShapeDtypeStruct((pulses, 2, HALF + 2 * HALO, LANES), f32)
    trig_shape = jax.ShapeDtypeStruct((2, beams, pulses, LANES), f32)
    send, pulse_ext, trig, delay_table, *tables = pl.pallas_call(
        front_kernel,
        out_shape=(send_shape, pulse_shape, trig_shape, *(pltpu.SMEM(x.shape, x.dtype) for x in inputs)),
        in_specs=[SMEM_SPEC] + [HBM_SPEC] * len(sources),
        out_specs=(VMEM_SPEC, VMEM_SPEC, VMEM_SPEC, *(SMEM_SPEC for x in inputs)),
        scratch_shapes=[
            pltpu.VMEM((parts * rows, LANES), bf16),
            pltpu.VMEM(matched.shape, f32),
            pltpu.VMEM(pulse_phase.shape, f32),
            pltpu.VMEM((16 + parts * rows, LANES), f32),
            pltpu.VMEM((2 * LANES, 4 * LANES), bf16),
            pltpu.VMEM((rows, 4 * LANES), bf16),
            pltpu.SemaphoreType.DMA((2 + len(inputs) + rows // LANES,)),
        ],
        compiler_params=params(),
        name="front",
    )(index, *(pltpu.with_memory_space_constraint(x, pltpu.HBM) for x in sources))
    beam_table, shift_table, base_table, rate_table, tap_table = tables
    scalars = (index, beam_table, shift_table, tap_table)

    def shape(number, dtype=bf16, rows=HALF):
        return jax.ShapeDtypeStruct((number, 2, rows, LANES), dtype)

    def kernel(function, out_shape, operands, name, scratch=(), out_specs=None, scalar_count=len(scalars)):
        return pl.pallas_call(
            function,
            out_shape=out_shape,
            in_specs=[SMEM_SPEC] * scalar_count + [VMEM_SPEC] * (len(operands) - scalar_count),
            out_specs=jax.tree.map(lambda x: VMEM_SPEC, out_shape) if out_specs is None else out_specs,
            scratch_shapes=list(scratch),
            compiler_params=params(),
            cost_estimate=pl.CostEstimate(flops=COSTS[name], bytes_accessed=2**20, transcendentals=0),
            name=name,
        )(*operands)

    own_scalars = (index, *tables)
    long = HALF + 2 * HALO
    images = (image_shape, image_shape)
    ext_scratch = [pltpu.VMEM((slots, 2, long, LANES), f32)]

    def own(level, outs, *operands):
        return kernel(
            functools.partial(own_kernel, level, bins, slots), (image_shape,) * outs, own_scalars + operands, f"own{level}",
            ext_scratch, scalar_count=len(own_scalars),
        )

    def exchange(x, level):
        return lax.ppermute(x, "pulse", route("pulse", level))

    received = exchange(send, 0)
    first, later = PARTS[1]
    bottom_scalars = (*own_scalars, delay_table)
    partial, turn, own_ext = kernel(
        functools.partial(bottom_own_kernel, bins, slots, 0, 0),
        (shape(first, f32), shape(first, f32), shape(first, f32, long)),
        (*bottom_scalars, pulse_ext, trig),
        "bottomownfirst",
        scalar_count=len(bottom_scalars),
    )
    early, first_ext = kernel(
        functools.partial(bottom_first_kernel, slots),
        (shape(first), shape(first, f32, long)),
        (*scalars, received, partial, turn),
        "bottomfirst",
    )
    partial, turn = kernel(
        functools.partial(bottom_own_kernel, bins, slots, first, first),
        (shape(beams - first, f32), shape(beams - first, f32)),
        (*bottom_scalars, pulse_ext, trig, own_ext),
        "bottomownsecond",
        ext_scratch,
        scalar_count=len(bottom_scalars),
    )
    late, ext = kernel(
        functools.partial(bottom_second_kernel, slots),
        (shape(later), shape(slots, f32, long)),
        (*scalars, received, first_ext, partial, turn),
        "bottomsecond",
    )
    received = exchange(early, 1), exchange(late, 1)
    partial, turn = own(1, 2, early, late, ext, partial, turn)
    early, first_ext = kernel(
        functools.partial(middle_first_kernel, 1, None, slots),
        (shape(PARTS[2][0]), shape(PARTS[1][0], f32, long)),
        (*scalars, received[0], partial, turn),
        "middle1first",
    )
    received_first = exchange(early, 2)
    own_turn, next_turn = kernel(
        functools.partial(turns_kernel, 2, bins),
        images,
        (index, base_table, rate_table, early),
        "turns2",
        scalar_count=3,
    )
    ext, next_partial, own_ext = kernel(
        functools.partial(split_own_kernel, 2, slots, False),
        (shape(slots, f32, long), shape(PARTS[3][0], f32), shape(PARTS[2][0], f32, long)),
        (*scalars, first_ext, received[1], partial, turn, own_turn),
        "own2first",
    )
    last_early, last_ext = kernel(
        functools.partial(middle_first_kernel, 2, 0, slots),
        (shape(PARTS[3][0]), shape(PARTS[2][0], f32, long)),
        (*scalars, received_first, next_partial, next_turn),
        "middle2first",
    )
    last_first = exchange(last_early, 3)
    late = kernel(
        functools.partial(late_send_kernel, 1, slots),
        shape(PARTS[2][1]),
        (*scalars, ext, partial, turn),
        "middle1second",
    )
    received_second = exchange(late, 2)
    next_partial = kernel(
        functools.partial(split_own_kernel, 2, slots, True),
        image_shape,
        (*scalars, ext, partial, turn, own_turn, own_ext),
        "own2second",
        ext_scratch,
    )
    last_late, ext = kernel(
        functools.partial(middle_second_kernel, 2, slots),
        (shape(PARTS[3][1]), shape(slots, f32, long)),
        (*scalars, received_second, last_ext, next_partial, next_turn),
        "middle2second",
    )
    last_second = exchange(last_late, 3)
    partial, turn = own(3, 2, last_early, last_late, ext, next_partial, next_turn)
    tiles, first_ext = kernel(
        functools.partial(last_first_kernel, 3, slots),
        (jax.ShapeDtypeStruct((2, HALF * 8, LANES), f32), shape(PARTS[3][0], f32, long)),
        (*scalars, last_first, partial, turn),
        "lastfirst",
    )
    out = kernel(
        functools.partial(last_second_kernel, 3, slots),
        jax.ShapeDtypeStruct((2, beams // 8, HALF * 8, LANES), f32),
        (*scalars, last_second, first_ext, tiles, partial, turn),
        "lastsecond",
        ext_scratch + [pltpu.VMEM((2, beams // 8, HALF * 8, LANES), f32), pltpu.SemaphoreType.DMA((2, beams // 8))],
        HBM_SPEC,
    )
    out = out.reshape(2, beams // 8, HALF, 8, LANES)
    return jnp.transpose(out, (0, 1, 3, 2, 4)).reshape(2, beams, bins)


def shifted(array, axis, by):
    count = lax.axis_size(axis)
    pairs = [(i, i + by) for i in range(count) if 0 <= i + by < count]
    return lax.ppermute(array, axis, pairs)


def padded_2(block, sides, width):
    for axis, dim in sides:
        count = lax.axis_size(axis)
        forward = [(i, i + 1) for i in range(count - 1)]
        backward = [(target, source) for source, target in forward]
        low = lax.ppermute(
            lax.slice_in_dim(block, block.shape[dim] - width, None, axis=dim), axis, forward
        )
        high = lax.ppermute(lax.slice_in_dim(block, 0, width, axis=dim), axis, backward)
        block = jnp.concatenate([low, block, high], axis=dim)
    return block


def from_partner(block, axis, bit):
    count = lax.axis_size(axis)
    route = []
    for low in range(count):
        high = low | 1 << bit
        if high != low and high < count:
            route += [(low, high), (high, low)]
    return lax.ppermute(block, axis, route)


def tables(length):
    counter = jnp.arange(length, dtype=jnp.int32)
    product = counter[:, None] * counter[None, :] % length
    angles = product.astype(jnp.float32) * (2.0 * math.pi / length)
    cosine = jnp.cos(angles)
    sine_part = jnp.sin(angles)
    forward = jnp.concatenate(
        [
            jnp.concatenate([cosine, -sine_part], axis=1),
            jnp.concatenate([sine_part, cosine], axis=1),
        ],
        axis=0,
    )
    inverse = jnp.concatenate(
        [
            jnp.concatenate([cosine, sine_part], axis=1),
            jnp.concatenate([-sine_part, cosine], axis=1),
        ],
        axis=0,
    )
    return (forward, inverse)


def compress(echoes, tail, matched, forward_exact, forward, inverse_kept):
    pulses, blocks, parts, hop_bins = echoes.shape
    length = 2 * hop_bins
    previous = jnp.concatenate([tail[:, None], echoes[:, :-1]], axis=1)
    windows = jnp.concatenate([previous, echoes], axis=3).reshape(pulses * blocks, parts * length)
    taps_padded = jnp.concatenate(
        [matched, jnp.zeros((2, length - hop_bins), jnp.float32)], axis=1
    ).reshape(1, 2 * length)
    response = jnp.dot(taps_padded, forward_exact, precision=lax.Precision.HIGHEST)[0]
    resp_real = response[:length]
    resp_imag = response[length:]
    spectrum = jnp.dot(windows, forward, preferred_element_type=jnp.float32)
    spec_real = spectrum[:, :length]
    spec_imag = spectrum[:, length:]
    filt_real = spec_real * resp_real - spec_imag * resp_imag
    filt_imag = spec_real * resp_imag + spec_imag * resp_real
    shaped = jnp.concatenate([filt_real, filt_imag], axis=1).astype(jnp.bfloat16)
    restored = jnp.dot(shaped, inverse_kept, preferred_element_type=jnp.float32) * (1.0 / length)
    return restored.astype(jnp.bfloat16).reshape(pulses, blocks, parts, hop_bins)


def kept_columns(inverse, length):
    half = length // 2
    return jnp.concatenate([inverse[:, half:length], inverse[:, length + half :]], axis=1)


def inside_mask(first_cell, out_cells, bins):
    global_cells = first_cell + jnp.arange(out_cells, dtype=jnp.int32)
    return ((global_cells >= 0) & (global_cells < bins)).astype(jnp.float32)


def row_slices(rows, starts, width):

    def per_pulse(row, start_row):
        return jax.vmap(lambda start: lax.dynamic_slice_in_dim(row, start, width, 1))(start_row)

    return jax.vmap(per_pulse)(rows, starts)


def project(padded, delay_rows, phase_rows, offset_base, out_cells, first_cell, bins):
    pulses = padded.shape[0]
    beam_count = delay_rows.shape[1]
    group_size = math.gcd(pulses, 4)
    block_count = pulses // group_size

    def accumulate(summed, block_index):
        first_row = block_index * group_size
        pulses_block = lax.dynamic_slice_in_dim(padded, first_row, group_size, 0)
        delay_block = lax.dynamic_slice_in_dim(delay_rows, first_row, group_size, 0)
        phase_block = lax.dynamic_slice_in_dim(phase_rows, first_row, group_size, 0)
        starts = delay_block + offset_base
        gathered = row_slices(pulses_block, starts, out_cells).astype(jnp.float32)
        cosine = jnp.cos(phase_block)[:, :, None]
        sine_part = jnp.sin(phase_block)[:, :, None]
        real_part = gathered[:, :, 0] * cosine - gathered[:, :, 1] * sine_part
        imag_part = gathered[:, :, 0] * sine_part + gathered[:, :, 1] * cosine
        return (summed + jnp.stack([jnp.sum(real_part, axis=0), jnp.sum(imag_part, axis=0)]), None)

    summed, unused = lax.scan(
        accumulate,
        jnp.zeros((2, beam_count, out_cells), jnp.float32),
        jnp.arange(block_count, dtype=jnp.int32),
    )
    return summed * inside_mask(first_cell, out_cells, bins) * (1.0 / math.sqrt(pulses))


def tap_weights(tap_values):
    weights = SPREAD + 1.0 - jnp.abs(tap_values).astype(jnp.float32)
    return weights / jnp.sum(weights)


def merge_side(
    source,
    beam_rows,
    offsets,
    phase_zero,
    phase_slope,
    weights,
    tap_values,
    offset_base,
    out_cells,
    first_cell,
    bins,
):
    span = out_cells + 2 * SPREAD
    starts = offsets + offset_base - SPREAD
    windows = jax.vmap(
        lambda beam, start: lax.dynamic_slice(source, (0, beam, start), (2, 1, span))[:, 0],
        out_axes=1,
    )(beam_rows, starts)
    summed = jnp.zeros((2, beam_rows.shape[0], out_cells), jnp.float32)
    for tap_index in range(tap_values.shape[0]):
        tap_start = tap_values[tap_index] + SPREAD
        summed = summed + weights[tap_index] * lax.dynamic_slice_in_dim(
            windows, tap_start, out_cells, 2
        )
    positions = jnp.arange(out_cells, dtype=jnp.int32)
    global_cells = (first_cell + positions).astype(jnp.float32)
    angle_grid = (
        phase_zero[:, None] + 2.0 * math.pi / bins * phase_slope[:, None] * global_cells[None, :]
    )
    cosine = jnp.cos(angle_grid)
    sine_part = jnp.sin(angle_grid)
    return jnp.stack(
        [summed[0] * cosine - summed[1] * sine_part, summed[0] * sine_part + summed[1] * cosine]
    )


def pick_sides(table, level_index, side_bit):
    half_rows = lax.dynamic_index_in_dim(table[level_index], side_bit, 0, keepdims=False)
    own_rows = lax.dynamic_index_in_dim(half_rows, side_bit, 0, keepdims=False)
    other_rows = lax.dynamic_index_in_dim(half_rows, 1 - side_bit, 0, keepdims=False)
    return (own_rows, other_rows)


def local_split(
    raw_echoes,
    matched,
    delays,
    pulse_phase,
    beam_map,
    range_shift,
    phase_base,
    phase_rate,
    tap_offsets,
):
    pulses = raw_echoes.shape[0]
    hop_bins = raw_echoes.shape[3]
    local_cells = raw_echoes.shape[1] * hop_bins
    bins = local_cells * lax.axis_size("rng")
    length = 2 * hop_bins
    levels = tap_offsets.shape[0]
    forward_exact, inverse_exact = tables(length)
    forward = forward_exact.astype(jnp.bfloat16)
    inverse_kept = kept_columns(inverse_exact.astype(jnp.bfloat16), length)
    tail = shifted(raw_echoes[:, -1], "rng", 1)
    compressed = compress(raw_echoes, tail, matched, forward_exact, forward, inverse_kept)
    compressed = jnp.transpose(compressed, (0, 2, 1, 3)).reshape(pulses, 2, local_cells)
    first_cell = lax.axis_index("rng") * local_cells
    rim_cells = SHIFT + SPREAD
    margin_cells = levels * rim_cells
    padded = padded_2(compressed, (("rng", 2),), SHIFT + margin_cells)
    polar_image = project(
        padded,
        delays,
        pulse_phase,
        SHIFT,
        local_cells + 2 * margin_cells,
        first_cell - margin_cells,
        bins,
    )
    pulse_index = lax.axis_index("pulse")
    for level_index in range(levels):
        side_bit = pulse_index // 2**level_index % 2
        own_beams, other_beams = pick_sides(beam_map, level_index, side_bit)
        own_offsets, other_offsets = pick_sides(range_shift, level_index, side_bit)
        own_zero, other_zero = pick_sides(phase_base, level_index, side_bit)
        own_slope, other_slope = pick_sides(phase_rate, level_index, side_bit)
        tap_values = tap_offsets[level_index]
        weights = tap_weights(tap_values)
        received = from_partner(polar_image, "pulse", level_index)
        own_source = polar_image
        out_margin = max(margin_cells - rim_cells * (level_index + 1), 0)
        out_cells = local_cells + 2 * out_margin
        start_cell = first_cell - out_margin
        own_side = merge_side(
            own_source,
            own_beams,
            own_offsets,
            own_zero,
            own_slope,
            weights,
            tap_values,
            rim_cells,
            out_cells,
            start_cell,
            bins,
        )
        other_side = merge_side(
            received,
            other_beams,
            other_offsets,
            other_zero,
            other_slope,
            weights,
            tap_values,
            rim_cells,
            out_cells,
            start_cell,
            bins,
        )
        polar_image = (own_side + other_side) * SQRT_HALF * inside_mask(start_cell, out_cells, bins)
    return polar_image


def solution(mesh):
    in_specs = (
        P(("grp", "pulse"), "rng", None, None),
        P(),
        P(("grp", "pulse"), None),
        P(("grp", "pulse"), None),
        P(),
        P(),
        P(),
        P(),
        P(),
    )
    out_specs = P(None, ("grp", "pulse"), "rng")
    whole_range = mesh.shape["rng"] == 1
    return jax.shard_map(local if whole_range else local_split, mesh=mesh, in_specs=in_specs, out_specs=out_specs, check_vma=False)
```
